256 devices in a mesh: fsdp: 32 (over z, y), tensor: 8 (over x, core).
Axes of the slice: x: 4, y: 4, z: 8, core: 2. Of those that a mesh axis runs over, the one named last changes fastest.
Arguments:
- momentum: float32 [2, 4096, 1536], P(None, 'fsdp', 'tensor'), may hold values from -90 to 90
- grad: bfloat16 [2, 4096, 1536], P(None, 'fsdp', 'tensor'), may hold values from -3 to 3
- basis: float32 [2, 1536, 512], P(None, 'tensor'), may hold values from -6 to 6
Outputs:
- new_momentum: float32 [2, 4096, 1536], P(None, 'fsdp', 'tensor')
- new_basis: float32 [2, 1536, 512], P(None, 'tensor')
- update: bfloat16 [2, 4096, 1536], P(None, 'fsdp', 'tensor')
The draws below stay inside these ranges and needn't reach their ends.
All inputs are finite; a program needn't handle non-finite values.
Results may differ from the reference program's by a relative error of at most 0.0011.
Values sent between devices are 32-bit elements; how exact they have to be, the bound alone decides.
A program may use at most 64 MiB of HBM per device.

```python
import math
import jax
import jax.numpy as jnp
from jax import lax

D = 4096
FF = 1536
RANK = 512
MATS = 2


def draw_momentum(key, part):
    key = jax.random.fold_in(key, 11)
    keys = jax.random.split(key, 3)
    rows = jnp.arange(D, dtype=jnp.float32) / D
    cols = jnp.arange(FF, dtype=jnp.float32) / FF
    row_scale = (1.0 + 2.0 * rows)[None, :, None] * jnp.exp(jax.random.uniform(keys[1], (MATS, D, 1), jnp.float32, -0.4, 0.4))
    col_scale = jnp.sqrt(1.0 + 2.0 * cols)[None, None, :] * jnp.exp(jax.random.uniform(keys[2], (MATS, 1, FF), jnp.float32, -0.4, 0.4))
    base = jnp.clip(jax.random.normal(keys[0], (MATS, D, FF), jnp.float32), -4.0, 4.0)
    return (base * row_scale * col_scale).astype(jnp.float32)


def shard_levels(key, dims, shards, low, largest):
    level, own = 1.0, jax.random.fold_in(key, 6)
    for position, shards_of in shards:
        steps = jnp.exp(jax.random.uniform(jax.random.fold_in(own, position), (shards_of,), jnp.float32, low / len(shards), largest / len(shards)))
        level = level * jnp.repeat(steps, dims[position] // shards_of).reshape([-1 if axis == position else 1 for axis in range(len(dims))])
    return level


def scatter_about(stream_key, dims, width, most, shards=(), kind=jnp.bfloat16):
    values = jax.random.normal(stream_key, dims, jnp.float32) * width
    if len(shards) > 0:
        values = shard_levels(stream_key, dims, shards, -0.22, 0.18) * values
    return jnp.clip(values, min=-most, max=most).astype(kind)


def setup_inputs(seed: int = 0) -> dict:
    splits = jax.random.split(jax.random.key(seed), 4)
    momentum = draw_momentum(jax.random.fold_in(splits[3], 71), 0)
    grad = scatter_about(splits[1], (MATS, D, FF), 0.5, 3.0, ((1, 32), (2, 8)))
    basis = scatter_about(splits[2], (MATS, FF, RANK), 1.0, 6.0, ((1, 8),), jnp.float32)
    return dict(momentum=momentum, grad=grad, basis=basis)


def reference(momentum, grad, basis):
    highest = lax.Precision.HIGHEST
    blended = momentum + grad.astype(jnp.float32)
    projected = jnp.einsum('mdf,mfr->mdr', blended, basis, precision=highest)
    gram = jnp.einsum('mdr,mds->mrs', projected, projected, precision=highest)
    factor = jnp.linalg.cholesky(gram)
    ortho = lax.linalg.triangular_solve(factor, projected, left_side=False, lower=True, transpose_a=True)
    coeffs = jnp.einsum('mdf,mdr->mfr', blended, ortho, precision=highest)
    new_momentum = blended - 0.05 * jnp.einsum('mdr,mfr->mdf', ortho, coeffs, precision=highest)
    squares = lax.optimization_barrier(jnp.sum(coeffs * coeffs, axis=1))
    new_basis = coeffs * lax.rsqrt(squares + 1e-06)[:, None, :]
    factor_scale = math.sqrt(D * FF / RANK)
    update = (factor_scale * jnp.einsum('mdr,mfr->mdf', ortho, new_basis, precision=highest)).astype(jnp.bfloat16)
    return (new_momentum, new_basis, update)
```

```python
import functools
import math

import jax
import jax.numpy as jnp
from jax import lax
from jax.experimental import pallas as pl
from jax.experimental.pallas import tpu as pltpu
from jax.sharding import PartitionSpec as P

D = 4096
FF = 1536
RANK = 512
NX, NY, NZ = 4, 4, 8
ROWS = 128
COLS = 192
BLK = 128
NB = 16
F32 = jnp.float32
BF16 = jnp.bfloat16
HIGHEST = lax.Precision.HIGHEST
MESH = pl.DeviceIdType.MESH

PIECES = [
    [(s, c) for s in (x, 7 - x) for c in range(s // 2 + 1)] for x in range(NX)
]
PLACE = {piece: (x, n) for x in range(NX) for n, piece in enumerate(PIECES[x])}


def dot6(a, b, ca, cb):
    return lax.dot_general(
        a, b, (((ca,), (cb,)), ((), ())), precision=HIGHEST, preferred_element_type=F32
    )


def split(a):
    hi = a.astype(BF16)
    return hi, (a - hi.astype(F32)).astype(BF16)


def dot3(a, b, ca, cb):
    dims = (((ca,), (cb,)), ((), ()))
    ah, al = split(a)
    bh, bl = split(b)
    one = functools.partial(lax.dot_general, dimension_numbers=dims, preferred_element_type=F32)
    return one(ah, bh) + (one(ah, bl) + one(al, bh))


def invert_factor(m_ref, out_ref, vfull, pan, between):
    lane = lax.broadcasted_iota(jnp.int32, (NB, BLK), 1)
    sub = lax.broadcasted_iota(jnp.int32, (NB, BLK), 0)
    lane_all = lax.broadcasted_iota(jnp.int32, (BLK, BLK), 1)
    eye = lax.broadcasted_iota(jnp.int32, (BLK, BLK), 0) == lane_all
    diagonal = jnp.where(eye, m_ref[...], 0.0)
    scale_row = lax.rsqrt(jnp.sum(diagonal, axis=0, keepdims=True))
    scale_col = lax.rsqrt(jnp.sum(diagonal, axis=1, keepdims=True))
    scaled = m_ref[...] * scale_col * scale_row
    m_ref[...] = scaled
    pan[...] = scaled[:NB]
    vfull[...] = jnp.zeros_like(vfull)

    def columns(rows, rel):
        return [
            jnp.broadcast_to(
                jnp.sum(jnp.where(rel == j, rows, 0.0), axis=1, keepdims=True), (NB, BLK)
            )
            for j in range(NB)
        ]

    def step(b, carry):
        r0 = pl.multiple_of(b * NB, NB)
        before = pl.multiple_of(jnp.maximum(r0 - NB, 0), NB)
        after = pl.multiple_of(jnp.minimum(r0 + NB, BLK - NB), NB)
        rel = lane - r0
        inside = jnp.logical_and(rel >= 0, rel < NB)
        rel_all = lane_all - r0
        inside_before = jnp.logical_and(rel_all >= -NB, rel_all < 0)

        old = m_ref[...]
        m_ref[...] = jnp.where(inside_before, 0.0, old) - dot6(old, vfull[...], 1, 0)

        rows = pan[...]
        cols = jnp.stack(columns(rows, rel))
        full = jnp.where(inside, jnp.where(rel == sub, 1.0, 0.0), rows)
        lower = full
        scale = jnp.zeros((NB, BLK), F32)
        for p in range(0, NB, 2):
            u1, u2 = cols[0], cols[1]
            a, e, d = u1[p : p + 1], u2[p : p + 1], u2[p + 1 : p + 2]
            det = a * d - e * e
            inv = pl.reciprocal(det, approx=True)
            inv = inv * (2.0 - det * inv)
            v1, v2 = d * u1 - e * u2, a * u2 - e * u1
            ia = 1.0 / a
            under = sub > p + 1
            l1 = jnp.where(under, v1 * inv, jnp.where(sub == p + 1, e * ia, 0.0))
            l2 = jnp.where(under, v2 * inv, 0.0)
            lower = lower - (l1 * lower[p : p + 1] + l2 * lower[p + 1 : p + 2])
            scale = jnp.where(sub == p, lax.rsqrt(a), scale)
            scale = jnp.where(sub == p + 1, lax.rsqrt(det * ia), scale)
            v1 = jnp.where(sub == p, det - d, jnp.where(sub == p + 1, e, v1))
            v2 = jnp.where(sub == p, e, jnp.where(sub == p + 1, det - a, v2))
            full = full - (v1 * full[p : p + 1] + v2 * full[p + 1 : p + 2]) * inv
            if p + 2 < NB:
                rest = cols[2:]
                cols = rest - (v1[None] * rest[:, p : p + 1] + v2[None] * rest[:, p + 1 : p + 2]) * inv
        out_ref[pl.ds(r0, NB), :] = lower * scale * scale_row

        rows = m_ref[pl.ds(after, NB), :]
        terms = [m * full[j : j + 1] for j, m in enumerate(columns(rows, rel))]
        while len(terms) > 1:
            terms = [terms[i] + terms[i + 1] for i in range(0, len(terms), 2)]
        pan[...] = jnp.where(inside, 0.0, rows) - terms[0]
        vfull[pl.ds(before, NB), :] = jnp.zeros((NB, BLK), F32)
        vfull[pl.ds(r0, NB), :] = full
        return carry

    half = BLK // NB // 2
    lax.fori_loop(0, half, step, 0)
    between()
    lax.fori_loop(half, 2 * half, step, 0)


def kernel(
    mom_hbm, grad_hbm, basis_hbm, nm_hbm, nb_hbm, up_hbm,
    mom_ref, grad_ref, basis_ref, in_sem, b2, bsend, pown, poth, prcv, psum, pcomb, xrcv, pfull, gp, zrcv, gz, yrcv, gown, gfull,
    wp, wcomb, wyrcv, wy, wzrcv, wfull, afac, mblk, iblk, vfull, pan, qs, cs, sq, sqrcv, nms, nbs, ups, uprcv, nmo, nbo, upo, out_sem,
    s_pair, r_pair, s_xr, r_xr, s_xa, r_xa, s_zr, r_zr, s_y, r_y, s_gx, r_gx, s_gz, r_gz,
    s_wy, r_wy, s_wz, r_wz, s_wza, r_wza, s_wya, r_wya, s_n, r_n,
):
    f = lax.axis_index("fsdp")
    t = lax.axis_index("tensor")
    z, y = f // NY, f % NY
    x, c = t // 2, t % 2
    o = 1 - c

    pair = (f, x * 2 + o)

    def on_x(k):
        return (f, ((x + k + NX) % NX) * 2 + c)

    def on_y(k):
        return (z * NY + (y + k + NY) % NY, t)

    def on_z(k):
        return (((z + k) % NZ) * NY + y, t)

    s = 1 - 2 * c

    pending = []

    def send(src, dst, ssem, rsem, to):
        copy = pltpu.make_async_remote_copy(
            src_ref=src, dst_ref=dst, send_sem=ssem, recv_sem=rsem,
            device_id=to, device_id_type=MESH,
        )
        copy.start()
        pending.append(copy)
        return copy

    loads = [
        pltpu.make_async_copy(src, dst, in_sem.at[i])
        for i, (src, dst) in enumerate(
            (
                (mom_hbm, mom_ref),
                (grad_hbm, grad_ref),
                (basis_hbm.at[o], basis_ref.at[o]),
                (basis_hbm.at[c], basis_ref.at[c]),
            )
        )
    ]
    for load in loads:
        load.start()
    barrier = pltpu.get_barrier_semaphore()
    peers = [pair] + [on_x(k) for k in range(1, NX)]
    peers += [on_y(k) for k in range(1, NY)] + [on_z(k) for k in range(1, NZ)]
    for peer in peers:
        pl.semaphore_signal(barrier, inc=1, device_id=peer, device_id_type=MESH)

    for load in loads[:3]:
        load.wait()
    bsend[...] = mom_ref[o] + grad_ref[o].astype(F32)
    p = dot6(bsend[...], basis_ref[o], 0, 0)
    for b in range(4):
        poth[b] = p[:, b * BLK : (b + 1) * BLK]
    pl.semaphore_wait(barrier, len(peers))
    cp = send(poth, prcv, s_pair.at[0], r_pair.at[0], pair)
    cb = send(bsend, b2.at[c], s_pair.at[1], r_pair.at[1], pair)
    own = mom_ref[c] + grad_ref[c].astype(F32)
    b2[c] = own
    loads[3].wait()
    p = dot6(own, basis_ref[c], 0, 0)
    for b in range(4):
        pown[b] = p[:, b * BLK : (b + 1) * BLK]
    cp.wait_recv()
    for b in range(4):
        psum[b] = pown[b] + prcv[b]

    def sum_start(parts, me, own, own_sem, rcv, rcv_sem, to):
        far = send(parts.at[(me + 2) % 4], rcv.at[0], own_sem.at[0], rcv_sem.at[0], to(s))
        near = send(parts.at[(me - s + 4) % 4], rcv.at[1], own_sem.at[1], rcv_sem.at[1], to(-s))
        return far, near

    def sum_relay(started, parts, me, own, own_sem, rcv, rcv_sem, to):
        started[0].wait_recv()
        own[...] = parts[(me + s + 4) % 4] + rcv[0]
        return started[1], send(own, rcv.at[2], own_sem.at[2], rcv_sem.at[2], to(s))

    def sum_end(started, parts, me, own, own_sem, rcv, rcv_sem, to):
        for copy in started:
            copy.wait_recv()
        return parts[me] + rcv[1] + rcv[2]

    def gather_start(slot, me, ssem, rsem, to):
        return [send(slot(me), slot(me), ssem.at[i], rsem.at[i], to(k)) for i, k in enumerate((s, -s))]

    def gather_relay(started, slot, me, ssem, rsem, to):
        started[0].wait_recv()
        here = slot((me - s + 4) % 4)
        return [started[1], send(here, here, ssem.at[2], rsem.at[2], to(s))]

    args = (psum, x, pcomb, s_xr, xrcv, r_xr, on_x)
    pfull[x] = sum_end(sum_relay(sum_start(*args), *args), *args)
    args = (lambda i: pfull.at[i], x, s_xa, r_xa, on_x)
    for copy in gather_relay(gather_start(*args), *args):
        copy.wait_recv()

    for i in range(4):
        for j in range(i + 1):
            g = dot6(pfull[i], pfull[j], 0, 0)
            for h in range(2):
                at, n = PLACE[(2 * i + h, j)]
                gp[at, n] = g[h * 64 : (h + 1) * 64]

    def rows8(k):
        return pl.ds(pl.multiple_of(((z + k) % NZ) * 8, 8), 8)

    first, rest = pl.ds(0, 1), pl.ds(1, 4)
    around = (4, 3, 5, 2, 6, 1, 7)

    def gram_z(part, n):
        return [
            send(
                gp.at[x, n, rows8(k), :], zrcv.at[k - 1, n],
                s_zr.at[part, k - 1], r_zr.at[part, k - 1], on_z(k),
            )
            for k in around
        ]

    def gram_y(part, n, before):
        for copy in before:
            copy.wait_recv()
        total = gp[x, n, rows8(0), :]
        for k in range(NZ - 1):
            total = total + zrcv[k, n]
        gz[n] = total
        return [
            send(gz.at[n], yrcv.at[k - 1, n], s_y.at[part, k - 1], r_y.at[part, k - 1], on_y(k))
            for k in (2, 1, 3)
        ]

    def gram_gather_z(part, n, before):
        for copy in before:
            copy.wait_recv()
        total = gz[n]
        for k in range(NY - 1):
            total = total + yrcv[k, n]
        gown[n] = total
        gfull[x, n, rows8(0), :] = total
        return [
            send(
                gown.at[n], gfull.at[x, n, rows8(0), :],
                s_gz.at[part, k - 1], r_gz.at[part, k - 1], on_z(k),
            )
            for k in around
        ]

    w_rows = COLS * 2 // NZ

    def wrows(k):
        return pl.ds(pl.multiple_of(((z + k) % NZ) * w_rows, 8), w_rows)

    def w_sum_z(before):
        wy[...] = sum_end(before, *w_args)
        return [
            send(wy.at[wrows(k), :], wzrcv.at[k - 1], s_wz.at[k - 1], r_wz.at[k - 1], on_z(k))
            for k in around
        ]

    def w_gather_z(before):
        for copy in before:
            copy.wait_recv()
        total = wy[wrows(0), :]
        for k in range(NZ - 1):
            total = total + wzrcv[k]
        wfull[y, wrows(0), :] = total
        here = wfull.at[y, wrows(0), :]
        return [send(here, here, s_wza.at[k - 1], r_wza.at[k - 1], on_z(k)) for k in around]

    g0 = gram_z(0, first)
    g1 = gram_z(1, rest)
    cb.wait_recv()
    for i in range(2):
        for b in range(4):
            wp[b, i * COLS : (i + 1) * COLS, :] = dot6(b2[i], pfull[b], 1, 0)
    g0 = gram_y(0, first, g0)
    w_args = (wp, y, wcomb, s_wy, wyrcv, r_wy, on_y)
    w = sum_start(*w_args)
    g1 = gram_y(1, rest, g1)
    g0 = gram_gather_z(0, first, g0)
    g1 = gram_gather_z(1, rest, g1)
    w = sum_relay(w, *w_args)
    for copy in g0:
        copy.wait_recv()
    here = gfull.at[x, first]
    g0 = [send(here, here, s_gx.at[k + 2], r_gx.at[k + 2], on_x(k)) for k in (1, 3, 2)]
    for copy in g1:
        copy.wait_recv()
    g_args = (lambda i: gfull.at[i, rest], x, s_gx, r_gx, on_x)
    g1 = gather_start(*g_args)
    w = w_sum_z(w)
    for copy in g0:
        copy.wait_recv()

    wg_args = (lambda i: wfull.at[i], y, s_wya, r_wya, on_y)

    def w_gather_y(before):
        for copy in before:
            copy.wait_recv()
        return gather_start(*wg_args)

    def w_relay_y(before):
        return gather_relay(before, *wg_args)

    flights = {"w": w, "g": g1}

    def between(kb):
        if kb == 0:
            flights["g"] = gather_relay(flights["g"], *g_args)

    def after(kb):
        sent = list(pending)
        pending.clear()
        if kb == 0:
            flights["w"] = w_gather_z(flights["w"])
        if kb == 1:
            flights["w"] = w_gather_y(flights["w"])
        if kb == 2:
            flights["w"] = w_relay_y(flights["w"])
        for copy in sent:
            copy.wait_send()

    def load(i, j):
        return jnp.concatenate([gfull[PLACE[(2 * i + h, j)]] for h in range(2)], axis=0)

    def lanes(b):
        return slice(b * BLK, (b + 1) * BLK)

    tril = lax.broadcasted_iota(jnp.int32, (BLK, BLK), 0) >= lax.broadcasted_iota(
        jnp.int32, (BLK, BLK), 1
    )
    afac[0, 0] = load(0, 0)
    inverses = []
    for kb in range(4):
        mblk[...] = afac[kb, kb]
        invert_factor(mblk, iblk, vfull, pan, functools.partial(between, kb))
        inv = jnp.where(tril, iblk[...], 0.0)
        after(kb)
        if kb == 0:
            for copy in flights["g"]:
                copy.wait_recv()
            for i in range(1, 4):
                for j in range(i + 1):
                    afac[i, j] = load(i, j)
        for i in range(kb + 1, 4):
            afac[i, kb] = dot6(afac[i, kb], inv, 1, 1)
        for i in range(kb + 1, 4):
            for j in range(kb + 1, i + 1):
                afac[i, j] = afac[i, j] - dot6(afac[i, kb], afac[j, kb], 1, 1)
        q = pfull[kb]
        for j in range(kb):
            q = q - dot3(qs[:, lanes(j)], afac[kb, j], 1, 1)
        qs[:, lanes(kb)] = dot3(q, inv, 1, 1)
        inverses.append(inv)
    for copy in flights["w"]:
        copy.wait_recv()
    for kb in range(4):
        w = wfull[kb]
        for j in range(kb):
            w = w - dot3(cs[:, lanes(j)], afac[kb, j], 1, 1)
        cs[:, lanes(kb)] = dot3(w, inverses[kb], 1, 1)

    sq[...] = jnp.sum(cs[...] * cs[...], axis=0, keepdims=True)
    copies = [send(sq, sqrcv.at[k - 1], s_n.at[k - 1], r_n.at[k - 1], on_x(k)) for k in (2, 1, 3)]

    def half(i):
        return pl.ds(pl.multiple_of(i * COLS, 8), COLS)

    q16 = qs[...].astype(BF16)

    def error(i):
        return lax.dot_general(
            cs[half(i), :].astype(BF16), q16, (((1,), (1,)), ((), ())), preferred_element_type=F32
        )

    nms[...] = b2[o] - 0.05 * error(o)
    out_m = send(nms, nm_hbm.at[c], s_pair.at[2], r_pair.at[2], pair)
    nmo[...] = b2[c] - 0.05 * error(c)
    stores = [pltpu.make_async_copy(nmo, nm_hbm.at[c], out_sem.at[0])]
    stores[0].start()
    for copy in copies:
        copy.wait_recv()
    norm = lax.rsqrt(sq[...] + sqrcv[0] + sqrcv[1] + sqrcv[2] + 1e-06)
    nbs[...] = cs[half(o), :] * norm
    out_b = send(nbs, nb_hbm.at[c], s_pair.at[3], r_pair.at[3], pair)
    factor_scale = math.sqrt(D * FF / RANK)
    ups[...] = factor_scale * dot3(nbs[...], qs[...], 1, 1)
    out_u = send(ups, uprcv, s_pair.at[4], r_pair.at[4], pair)
    nbo[...] = cs[half(c), :] * norm
    stores.append(pltpu.make_async_copy(nbo, nb_hbm.at[c], out_sem.at[1]))
    stores[1].start()
    upo[c] = (factor_scale * dot3(nbo[...], qs[...], 1, 1)).astype(BF16)
    out_u.wait_recv()
    upo[o] = uprcv[...].astype(BF16)
    stores.append(pltpu.make_async_copy(upo, up_hbm, out_sem.at[2]))
    stores[2].start()
    out_m.wait_recv()
    out_b.wait_recv()
    for store in stores:
        store.wait()
    for copy in pending:
        copy.wait_send()


def finish(nm_from, nb_from, up_from, nm_to, nb_to, up_to, nm, nb, up, sem_in, sem_out):
    ins, outs = [], []
    refs = ((nb_from, nb, nb_to), (nm_from, nm, nm_to), (up_from, up, up_to))
    for i, (src, mid, dst) in enumerate(refs):
        for h in range(2):
            ins.append(pltpu.make_async_copy(src.at[h], mid.at[h], sem_in.at[i, h]))
            outs.append(pltpu.make_async_copy(mid.at[h], dst.at[h], sem_out.at[i, h]))
    for copy in ins:
        copy.start()
    for first, second in zip(ins, outs, strict=True):
        first.wait()
        second.start()
    for copy in outs:
        copy.wait()


def on_device(momentum, grad, basis):
    vm = pltpu.VMEM
    chunk = (4, BLK, BLK)
    w_rows = COLS * 2 // NZ
    scratch = [
        vm((2, COLS, ROWS), F32), vm((2, COLS, ROWS), BF16), vm((2, COLS, RANK), F32),
        pltpu.SemaphoreType.DMA((4,)),
        vm((2, COLS, ROWS), F32), vm((COLS, ROWS), F32),
        vm(chunk, F32), vm(chunk, F32), vm(chunk, F32), vm(chunk, F32),
        vm((BLK, BLK), F32), vm((3, BLK, BLK), F32), vm(chunk, F32),
        vm((4, 5, 64, BLK), F32), vm((7, 5, 8, BLK), F32), vm((5, 8, BLK), F32),
        vm((3, 5, 8, BLK), F32), vm((5, 8, BLK), F32), vm((4, 5, 64, BLK), F32),
        vm((4, 2 * COLS, BLK), F32), vm((2 * COLS, BLK), F32),
        vm((3, 2 * COLS, BLK), F32), vm((2 * COLS, BLK), F32),
        vm((7, w_rows, BLK), F32), vm((4, 2 * COLS, BLK), F32),
        vm((4, 4, BLK, BLK), F32), *[vm((BLK, BLK), F32)] * 3, vm((NB, BLK), F32),
        vm((ROWS, RANK), F32), vm((2 * COLS, RANK), F32),
        vm((1, RANK), F32), vm((3, 1, RANK), F32),
        vm((COLS, ROWS), F32), vm((COLS, RANK), F32), vm((COLS, ROWS), F32), vm((COLS, ROWS), F32),
        vm((COLS, ROWS), F32), vm((COLS, RANK), F32), vm((2, COLS, ROWS), BF16),
        pltpu.SemaphoreType.DMA((3,)),
    ]
    for n in (5, 3, 3, (2, 7), (2, 3), 6, (2, 7), 3, 7, 7, 3, 3):
        shape = n if isinstance(n, tuple) else (n,)
        scratch += [pltpu.SemaphoreType.DMA(shape), pltpu.SemaphoreType.DMA(shape)]
    hbm = pl.BlockSpec(memory_space=pl.ANY)
    shapes = (
        jax.ShapeDtypeStruct((2, COLS, ROWS), F32),
        jax.ShapeDtypeStruct((2, COLS, RANK), F32),
        jax.ShapeDtypeStruct((2, COLS, ROWS), BF16),
    )
    results = pl.pallas_call(
        kernel,
        out_shape=shapes,
        in_specs=[hbm] * 3,
        out_specs=(hbm,) * 3,
        scratch_shapes=scratch,
        compiler_params=pltpu.CompilerParams(
            collective_id=0, has_side_effects=True, vmem_limit_bytes=58 * 2**20
        ),
    )(jnp.swapaxes(momentum, 1, 2), jnp.swapaxes(grad, 1, 2), basis)
    nm, nb, up = pl.pallas_call(
        finish,
        out_shape=shapes,
        in_specs=[hbm] * 3,
        out_specs=(hbm,) * 3,
        scratch_shapes=[vm(shape.shape, shape.dtype) for shape in shapes]
        + [pltpu.SemaphoreType.DMA((3, 2))] * 2,
        compiler_params=pltpu.CompilerParams(vmem_limit_bytes=58 * 2**20),
    )(*results)
    return jnp.swapaxes(nm, 1, 2), nb, jnp.swapaxes(up, 1, 2)


def solution(mesh):
    in_specs = (P(None, "fsdp", "tensor"), P(None, "fsdp", "tensor"), P(None, "tensor", None))
    out_specs = (P(None, "fsdp", "tensor"), P(None, "tensor", None), P(None, "fsdp", "tensor"))
    return jax.shard_map(
        on_device, mesh=mesh, in_specs=in_specs, out_specs=out_specs, check_vma=False
    )
```

```python
import functools
import math

import jax
import jax.numpy as jnp
from jax import lax
from jax.experimental import pallas as pl
from jax.experimental.pallas import tpu as pltpu
from jax.sharding import PartitionSpec as P

D = 4096
FF = 1536
RANK = 512
NX, NY, NZ = 4, 4, 8
ROWS = 128
COLS = 192
BLK = 128
NB = 16
F32 = jnp.float32
BF16 = jnp.bfloat16
HIGHEST = lax.Precision.HIGHEST
MESH = pl.DeviceIdType.MESH

PLACE = {(2 * x + h, x): (x, h) for x in range(NX) for h in range(2)}
PLACE.update({(2 * (x + 1 - x // 3) + h, x % 3): (x, 2 + h) for x in range(NX) for h in range(2)})
PLACE.update({(2 * (2 + (x + 1) % 2) + x // 2, (x + 1) % 2): (x, 4) for x in range(NX)})


def dot6(a, b, ca, cb):
    return lax.dot_general(
        a, b, (((ca,), (cb,)), ((), ())), precision=HIGHEST, preferred_element_type=F32
    )


def split(a):
    hi = a.astype(BF16)
    return hi, (a - hi.astype(F32)).astype(BF16)


def dot3(a, b, ca, cb):
    dims = (((ca,), (cb,)), ((), ()))
    ah, al = split(a)
    bh, bl = split(b)
    one = functools.partial(lax.dot_general, dimension_numbers=dims, preferred_element_type=F32)
    return one(ah, bh) + (one(ah, bl) + one(al, bh))


def gram_long(a):
    hi = a.astype(BF16).astype(F32)
    rest = a - hi
    mid = rest.astype(BF16).astype(F32)
    low = rest - mid
    lhs = jnp.concatenate([hi, hi, hi, mid, mid, low], axis=0).astype(BF16)
    rhs = jnp.concatenate([hi, mid, low, hi, mid, hi], axis=0).astype(BF16)
    return lax.dot_general(lhs, rhs, (((0,), (0,)), ((), ())), preferred_element_type=F32)


def invert_factor(m_ref, out_ref, prev, pan, between):
    lane = lax.broadcasted_iota(jnp.int32, (NB, BLK), 1)
    sub = lax.broadcasted_iota(jnp.int32, (NB, BLK), 0)
    lane_all = lax.broadcasted_iota(jnp.int32, (BLK, BLK), 1)
    eye = lax.broadcasted_iota(jnp.int32, (BLK, BLK), 0) == lane_all
    diagonal = jnp.where(eye, m_ref[...], 0.0)
    scale_row = lax.rsqrt(jnp.sum(diagonal, axis=0, keepdims=True))
    scale_col = lax.rsqrt(jnp.sum(diagonal, axis=1, keepdims=True))
    scaled = m_ref[...] * scale_col * scale_row
    m_ref[...] = scaled
    pan[...] = scaled[:NB]
    prev[...] = jnp.zeros_like(prev)

    def columns(rows, rel):
        return [
            jnp.broadcast_to(
                jnp.sum(jnp.where(rel == j, rows, 0.0), axis=1, keepdims=True), (NB, BLK)
            )
            for j in range(NB)
        ]

    def step(b, carry):
        r0 = pl.multiple_of(b * NB, NB)
        after = pl.multiple_of(jnp.minimum(r0 + NB, BLK - NB), NB)
        rel = lane - r0
        inside = jnp.logical_and(rel >= 0, rel < NB)
        rel_all = lane_all - r0
        inside_before = jnp.logical_and(rel_all >= -NB, rel_all < 0)

        m_ref[...] = jnp.where(inside_before, 0.0, m_ref[...]) - gram_long(prev[...])

        rows = pan[...]
        cols = jnp.stack(columns(rows, rel))
        full = jnp.where(inside, jnp.where(rel == sub, 1.0, 0.0), rows)
        lower = full
        scale = jnp.zeros((NB, BLK), F32)
        for p in range(0, NB, 2):
            u1, u2 = cols[0], cols[1]
            a, e, d = u1[p : p + 1], u2[p : p + 1], u2[p + 1 : p + 2]
            det = a * d - e * e
            inv = pl.reciprocal(det, approx=True)
            inv = inv * (2.0 - det * inv)
            v1, v2 = d * u1 - e * u2, a * u2 - e * u1
            ia = 1.0 / a
            under = sub > p + 1
            l1 = jnp.where(under, v1 * inv, jnp.where(sub == p + 1, e * ia, 0.0))
            l2 = jnp.where(under, v2 * inv, 0.0)
            lower = lower - (l1 * lower[p : p + 1] + l2 * lower[p + 1 : p + 2])
            scale = jnp.where(sub == p, lax.rsqrt(a), scale)
            scale = jnp.where(sub == p + 1, lax.rsqrt(det * ia), scale)
            v1 = jnp.where(sub == p, det - d, jnp.where(sub == p + 1, e, v1))
            v2 = jnp.where(sub == p, e, jnp.where(sub == p + 1, det - a, v2))
            full = full - (v1 * full[p : p + 1] + v2 * full[p + 1 : p + 2]) * inv
            if p + 2 < NB:
                rest = cols[2:]
                cols = rest - (v1[None] * rest[:, p : p + 1] + v2[None] * rest[:, p + 1 : p + 2]) * inv
        lower = lower * scale
        prev[...] = lower
        out_ref[pl.ds(r0, NB), :] = lower * scale_row

        rows = m_ref[pl.ds(after, NB), :]
        terms = [m * full[j : j + 1] for j, m in enumerate(columns(rows, rel))]
        while len(terms) > 1:
            terms = [terms[i] + terms[i + 1] for i in range(0, len(terms), 2)]
        pan[...] = jnp.where(inside, 0.0, rows) - terms[0]
        return carry

    last = 0
    for b, call in between + [(BLK // NB, None)]:
        lax.fori_loop(last, b, step, 0)
        last = b
        if call is not None:
            call()


def kernel(
    mom_hbm, grad_hbm, basis_hbm, q_hbm, c_hbm, n_hbm,
    mom_ref, grad_ref, basis_ref, in_sem, b2, bsend, pown, poth, prcv, psum, pcomb, xrcv, pfull, halves, gp, zrcv, gz, yrcv, gown, gfull,
    wp, wcomb, wyrcv, wy, wzrcv, wfull, afac, mblk, iblk, prev, pan, qs, cs, sq, out_sem,
    s_pair, r_pair, s_xr, r_xr, s_xa, r_xa, s_zr, r_zr, s_y, r_y, s_gx, r_gx, s_gz, r_gz,
    s_wy, r_wy, s_wz, r_wz, s_wza, r_wza, s_wya, r_wya, s_end, r_end, s_n, r_n,
):
    f = lax.axis_index("fsdp")
    t = lax.axis_index("tensor")
    z, y = f // NY, f % NY
    x, c = t // 2, t % 2
    o = 1 - c

    pair = (f, x * 2 + o)

    def on_x(k):
        return (f, ((x + k + NX) % NX) * 2 + c)

    def on_y(k):
        return (z * NY + (y + k + NY) % NY, t)

    def on_z(k):
        return (((z + k) % NZ) * NY + y, t)

    s = 1 - 2 * c

    pending = []

    def make(src, dst, ssem, rsem, to):
        return pltpu.make_async_remote_copy(
            src_ref=src, dst_ref=dst, send_sem=ssem, recv_sem=rsem,
            device_id=to, device_id_type=MESH,
        )

    def send(*args):
        copy = make(*args)
        copy.start()
        pending.append(copy)
        return copy

    loads = [
        pltpu.make_async_copy(src, dst, in_sem.at[i])
        for i, (src, dst) in enumerate(
            (
                (mom_hbm, mom_ref),
                (grad_hbm, grad_ref),
                (basis_hbm.at[o], basis_ref.at[o]),
                (basis_hbm.at[c], basis_ref.at[c]),
            )
        )
    ]
    for load in loads:
        load.start()
    barrier = pltpu.get_barrier_semaphore()
    peers = [pair] + [on_x(k) for k in range(1, NX)]
    peers += [(f, ((x + k) % NX) * 2 + o) for k in range(1, NX)]
    peers += [on_y(k) for k in range(1, NY)] + [on_z(k) for k in range(1, NZ)]
    for peer in peers:
        pl.semaphore_signal(barrier, inc=1, device_id=peer, device_id_type=MESH)

    for load in loads[:3]:
        load.wait()
    bsend[...] = mom_ref[o] + grad_ref[o].astype(F32)
    p = dot3(bsend[...], basis_ref[o], 0, 0)
    for b in range(4):
        poth[b] = p[:, b * BLK : (b + 1) * BLK]
    pl.semaphore_wait(barrier, len(peers))
    cp = send(poth, prcv, s_pair.at[0], r_pair.at[0], pair)
    cb = send(bsend, b2.at[c], s_pair.at[1], r_pair.at[1], pair)
    own = mom_ref[c] + grad_ref[c].astype(F32)
    b2[c] = own
    loads[3].wait()
    p = dot3(own, basis_ref[c], 0, 0)
    for b in range(4):
        pown[b] = p[:, b * BLK : (b + 1) * BLK]
    cp.wait_recv()
    for b in range(4):
        psum[b] = pown[b] + prcv[b]

    def sum_start(parts, me, own, own_sem, rcv, rcv_sem, to):
        far = send(parts.at[(me + 2) % 4], rcv.at[0], own_sem.at[0], rcv_sem.at[0], to(s))
        near = send(parts.at[(me - s + 4) % 4], rcv.at[1], own_sem.at[1], rcv_sem.at[1], to(-s))
        return far, near

    def sum_relay(started, parts, me, own, own_sem, rcv, rcv_sem, to):
        started[0].wait_recv()
        own[...] = parts[(me + s + 4) % 4] + rcv[0]
        return started[1], send(own, rcv.at[2], own_sem.at[2], rcv_sem.at[2], to(s))

    def sum_end(started, parts, me, own, own_sem, rcv, rcv_sem, to):
        for copy in started:
            copy.wait_recv()
        return parts[me] + rcv[1] + rcv[2]

    def gather_start(slot, me, ssem, rsem, to):
        return [send(slot(me), slot(me), ssem.at[i], rsem.at[i], to(k)) for i, k in enumerate((s, -s))]

    def gather_relay(started, slot, me, ssem, rsem, to):
        here = slot((me - s + 4) % 4)
        return [started[1], send(here, here, ssem.at[2], rsem.at[2], to(s))]

    args = (psum, x, pcomb, s_xr, xrcv, r_xr, on_x)
    pfull[x] = sum_end(sum_relay(sum_start(*args), *args), *args)
    a_args = (lambda i: pfull.at[i], x, s_xa, r_xa, on_x)
    across = gather_start(*a_args)

    def rows8(k):
        return pl.ds(pl.multiple_of(((z + k) % NZ) * 8, 8), 8)

    first, rest = pl.ds(0, 2), pl.ds(2, 3)
    around = (4, 3, 5, 2, 6, 1, 7)

    def gram_z(part, n):
        return [
            send(
                gp.at[x, n, rows8(k), :], zrcv.at[k - 1, n],
                s_zr.at[part, k - 1], r_zr.at[part, k - 1], on_z(k),
            )
            for k in around
        ]

    def gram_y(part, n, before):
        for copy in before:
            copy.wait_recv()
        total = gp[x, n, rows8(0), :]
        for k in range(NZ - 1):
            total = total + zrcv[k, n]
        gz[n] = total
        return [
            send(gz.at[n], yrcv.at[k - 1, n], s_y.at[part, k - 1], r_y.at[part, k - 1], on_y(k))
            for k in (2, 1, 3)
        ]

    def gram_gather_z(part, n, before):
        for copy in before:
            copy.wait_recv()
        total = gz[n]
        for k in range(NY - 1):
            total = total + yrcv[k, n]
        gown[n] = total
        gfull[x, n, rows8(0), :] = total
        return [
            send(
                gown.at[n], gfull.at[x, n, rows8(0), :],
                s_gz.at[part, k - 1], r_gz.at[part, k - 1], on_z(k),
            )
            for k in around
        ]

    w_rows = COLS * 2 // NZ

    def wrows(k):
        return pl.ds(pl.multiple_of(((z + k) % NZ) * w_rows, 8), w_rows)

    def w_sum_z(before):
        wy[...] = sum_end(before, *w_args)
        return [
            send(wy.at[wrows(k), :], wzrcv.at[k - 1], s_wz.at[k - 1], r_wz.at[k - 1], on_z(k))
            for k in around
        ]

    def w_gather_z(before):
        for copy in before:
            copy.wait_recv()
        total = wy[wrows(0), :]
        for k in range(NZ - 1):
            total = total + wzrcv[k]
        wfull[y, wrows(0), :] = total
        here = wfull.at[y, wrows(0), :]
        return [send(here, here, s_wza.at[k - 1], r_wza.at[k - 1], on_z(k)) for k in around]

    g = dot6(pfull[x], pfull[x], 0, 0)
    for h in range(2):
        gp[x, h] = g[h * 64 : (h + 1) * 64]
    g0 = gram_z(0, first)
    across[0].wait_recv()
    far = gather_relay(across, *a_args)[1]
    across[1].wait_recv()
    g = dot6(pfull[x + 1 - x // 3], pfull[x % 3], 0, 0)
    for h in range(2):
        gp[x, 2 + h] = g[h * 64 : (h + 1) * 64]
    between_two = (x + 1) % 2
    g = dot6(pfull[between_two + 2], pfull[between_two], 0, 0)
    for h in range(2):
        halves[h] = g[h * 64 : (h + 1) * 64]
    gp[x, 4] = halves[x // 2]
    g1 = gram_z(1, rest)
    g0 = gram_y(0, first, g0)
    far.wait_recv()
    cb.wait_recv()
    for i in range(2):
        for b in range(4):
            wp[b, i * COLS : (i + 1) * COLS, :] = dot3(b2[i], pfull[b], 1, 0)
    g0 = gram_gather_z(0, first, g0)
    g1 = gram_y(1, rest, g1)
    w_args = (wp, y, wcomb, s_wy, wyrcv, r_wy, on_y)
    flights = {"w": sum_start(*w_args)}
    for copy in g0:
        copy.wait_recv()

    def diagonals():
        here = gfull.at[x, first]
        return [make(here, here, s_gx.at[k + 2], r_gx.at[k + 2], on_x(k)) for k in (1, 3, 2)]

    def diagonal_from(chip):
        k = (x - chip + NX) % NX
        here = gfull.at[chip, first]
        return make(here, here, s_gx.at[k + 2], r_gx.at[k + 2], on_x(k))

    @pl.when(x == 0)
    def _():
        for copy in diagonals():
            copy.start()

    flights["g"] = gram_gather_z(1, rest, g1)

    @pl.when(x != 0)
    def _():
        for copy in diagonals():
            copy.start()
        diagonal_from(0).wait_recv()

    g_args = (lambda i: gfull.at[i, rest], x, s_gx, r_gx, on_x)
    wg_args = (lambda i: wfull.at[i], y, s_wya, r_wya, on_y)

    def w_gather_y(before):
        for copy in before:
            copy.wait_recv()
        return gather_start(*wg_args)

    def w_relay():
        flights["w"] = sum_relay(flights["w"], *w_args)

    def w_to_z():
        flights["w"] = w_sum_z(flights["w"])

    def w_back_z():
        flights["w"] = w_gather_z(flights["w"])

    def w_back_y():
        flights["w"] = w_gather_y(flights["w"])

    def w_back_y_far():
        flights["w"][0].wait_recv()
        flights["w"] = gather_relay(flights["w"], *wg_args)

    def rest_near():
        for copy in flights["g"]:
            copy.wait_recv()
        flights["g"] = gather_start(*g_args)

    def rest_far():
        flights["g"][0].wait_recv()
        flights["g"] = gather_relay(flights["g"], *g_args)

    def rest_end():
        for chip in range(1, NX):

            @pl.when(x != chip)
            def _(chip=chip):
                diagonal_from(chip).wait_recv()

        for copy in flights["g"]:
            copy.wait_recv()

    def let_go():
        for copy in pending:
            copy.wait_send()
        pending.clear()

    between = [
        [(2, rest_near), (4, w_relay), (5, rest_far), (7, w_to_z)],
        [(4, w_back_z)],
        [(4, w_back_y)],
        [(4, w_back_y_far)],
    ]

    def load(i, j):
        return jnp.concatenate([gfull[PLACE[(2 * i + h, j)]] for h in range(2)], axis=0)

    def lanes(b):
        return slice(b * BLK, (b + 1) * BLK)

    def half(i):
        return pl.ds(pl.multiple_of(i * COLS, 8), COLS)

    tril = lax.broadcasted_iota(jnp.int32, (BLK, BLK), 0) >= lax.broadcasted_iota(
        jnp.int32, (BLK, BLK), 1
    )
    afac[0, 0] = load(0, 0)
    inverses = []
    for kb in range(4):
        mblk[...] = afac[kb, kb]
        invert_factor(mblk, iblk, prev, pan, between[kb])
        inv = jnp.where(tril, iblk[...], 0.0)
        if kb == 0:
            rest_end()
            for i in range(1, 4):
                for j in range(i + 1):
                    afac[i, j] = load(i, j)
        for i in range(kb + 1, 4):
            afac[i, kb] = dot6(afac[i, kb], inv, 1, 1)
        for i in range(kb + 1, 4):
            for j in range(kb + 1, i + 1):
                afac[i, j] = afac[i, j] - dot6(afac[i, kb], afac[j, kb], 1, 1)
        q = pfull[kb]
        for j in range(kb):
            q = q - dot3(qs[:, lanes(j)], afac[kb, j], 1, 1)
        qs[:, lanes(kb)] = dot3(q, inv, 1, 1)
        inverses.append(inv)
        if kb == 1:
            let_go()
    ends = [
        send(qs, q_hbm.at[c], s_end.at[0], r_end.at[0], pair),
        make(cs.at[half(o), :], c_hbm.at[c], s_end.at[1], r_end.at[1], pair),
    ]
    stores = [
        pltpu.make_async_copy(qs, q_hbm.at[c], out_sem.at[0]),
        pltpu.make_async_copy(cs.at[half(c), :], c_hbm.at[c], out_sem.at[1]),
        pltpu.make_async_copy(sq, n_hbm.at[c, x], out_sem.at[2]),
    ]
    stores[0].start()
    for copy in flights["w"]:
        copy.wait_recv()
    for kb in range(4):
        w = wfull[kb]
        for j in range(kb):
            w = w - dot3(cs[:, lanes(j)], afac[kb, j], 1, 1)
        cs[:, lanes(kb)] = dot3(w, inverses[kb], 1, 1)

    ends[1].start()
    stores[1].start()
    sq[...] = jnp.sum(cs[...] * cs[...], axis=0, keepdims=True)
    stores[2].start()
    sums = [
        send(sq, n_hbm.at[c, x], s_n.at[i], r_n.at[i], to)
        for i, to in enumerate(
            [on_x(2), on_x(1), on_x(3)]
            + [(f, ((x + k) % NX) * 2 + o) for k in (2, 1, 3, 0)]
        )
    ]
    for copy in pending[:-len(sums)]:
        copy.wait_send()
    for copy in diagonals():
        copy.wait_send()
    for copy in ends + sums:
        copy.wait_recv()
    ends[1].wait_send()
    for copy in sums:
        copy.wait_send()
    for store in stores:
        store.wait()


def finish(mom_ref, grad_ref, q_ref, c_ref, n_ref, nm_ref, nb_ref, up_ref):
    q, coeffs = q_ref[0], c_ref[0]
    error = lax.dot_general(
        coeffs.astype(BF16), q.astype(BF16), (((1,), (1,)), ((), ())), preferred_element_type=F32
    )
    nm_ref[0] = mom_ref[0] + grad_ref[0].astype(F32) - 0.05 * error
    basis = coeffs * lax.rsqrt(n_ref[0, 0] + n_ref[0, 1] + n_ref[0, 2] + n_ref[0, 3] + 1e-06)
    nb_ref[0] = basis
    up_ref[0] = (math.sqrt(D * FF / RANK) * dot3(basis, q, 1, 1)).astype(BF16)


def on_device(momentum, grad, basis):
    vm = pltpu.VMEM
    chunk = (4, BLK, BLK)
    w_rows = COLS * 2 // NZ
    scratch = [
        vm((2, COLS, ROWS), F32), vm((2, COLS, ROWS), BF16), vm((2, COLS, RANK), F32),
        pltpu.SemaphoreType.DMA((4,)),
        vm((2, COLS, ROWS), F32), vm((COLS, ROWS), F32),
        vm(chunk, F32), vm(chunk, F32), vm(chunk, F32), vm(chunk, F32),
        vm((BLK, BLK), F32), vm((3, BLK, BLK), F32), vm(chunk, F32),
        vm((2, 64, BLK), F32),
        vm((4, 5, 64, BLK), F32), vm((7, 5, 8, BLK), F32), vm((5, 8, BLK), F32),
        vm((3, 5, 8, BLK), F32), vm((5, 8, BLK), F32), vm((4, 5, 64, BLK), F32),
        vm((4, 2 * COLS, BLK), F32), vm((2 * COLS, BLK), F32),
        vm((3, 2 * COLS, BLK), F32), vm((2 * COLS, BLK), F32),
        vm((7, w_rows, BLK), F32), vm((4, 2 * COLS, BLK), F32),
        vm((4, 4, BLK, BLK), F32), *[vm((BLK, BLK), F32)] * 2, *[vm((NB, BLK), F32)] * 2,
        vm((ROWS, RANK), F32), vm((2 * COLS, RANK), F32),
        vm((1, RANK), F32),
        pltpu.SemaphoreType.DMA((3,)),
    ]
    for n in (2, 3, 3, (2, 7), (2, 3), 6, (2, 7), 3, 7, 7, 3, 2, 7):
        shape = n if isinstance(n, tuple) else (n,)
        scratch += [pltpu.SemaphoreType.DMA(shape), pltpu.SemaphoreType.DMA(shape)]
    hbm = pl.BlockSpec(memory_space=pl.ANY)
    momentum, grad = jnp.swapaxes(momentum, 1, 2), jnp.swapaxes(grad, 1, 2)
    q, coeffs, sums = pl.pallas_call(
        kernel,
        out_shape=(
            jax.ShapeDtypeStruct((2, ROWS, RANK), F32),
            jax.ShapeDtypeStruct((2, COLS, RANK), F32),
            jax.ShapeDtypeStruct((2, NX, 1, RANK), F32),
        ),
        in_specs=[hbm] * 3,
        out_specs=(hbm,) * 3,
        scratch_shapes=scratch,
        compiler_params=pltpu.CompilerParams(
            collective_id=0, has_side_effects=True, vmem_limit_bytes=58 * 2**20
        ),
    )(momentum, grad, basis)

    def one(*shape):
        return pl.BlockSpec((1, *shape), lambda i: (i,) + (0,) * len(shape))

    nm, nb, up = pl.pallas_call(
        finish,
        grid=(2,),
        out_shape=(
            jax.ShapeDtypeStruct((2, COLS, ROWS), F32),
            jax.ShapeDtypeStruct((2, COLS, RANK), F32),
            jax.ShapeDtypeStruct((2, COLS, ROWS), BF16),
        ),
        in_specs=[one(COLS, ROWS), one(COLS, ROWS), one(ROWS, RANK), one(COLS, RANK), one(NX, 1, RANK)],
        out_specs=(one(COLS, ROWS), one(COLS, RANK), one(COLS, ROWS)),
        compiler_params=pltpu.CompilerParams(vmem_limit_bytes=58 * 2**20),
    )(momentum, grad, q, coeffs, sums)
    return jnp.swapaxes(nm, 1, 2), nb, jnp.swapaxes(up, 1, 2)


def solution(mesh):
    in_specs = (P(None, "fsdp", "tensor"), P(None, "fsdp", "tensor"), P(None, "tensor", None))
    out_specs = (P(None, "fsdp", "tensor"), P(None, "tensor", None), P(None, "fsdp", "tensor"))
    return jax.shard_map(
        on_device, mesh=mesh, in_specs=in_specs, out_specs=out_specs, check_vma=False
    )
```

```python
import functools
import math

import jax
import jax.numpy as jnp
from jax import lax
from jax.experimental import pallas as pl
from jax.experimental.pallas import tpu as pltpu
from jax.sharding import PartitionSpec as P

D = 4096
FF = 1536
RANK = 512
NX, NY, NZ = 4, 4, 8
ROWS = 128
COLS = 192
BLK = 128
NB = 16
F32 = jnp.float32
BF16 = jnp.bfloat16
HIGHEST = lax.Precision.HIGHEST
MESH = pl.DeviceIdType.MESH

PLACE = {(2 * x + h, x): (x, h) for x in range(NX) for h in range(2)}
PLACE.update({(2 * (x + 1 - x // 3) + h, x % 3): (x, 2 + h) for x in range(NX) for h in range(2)})
PLACE.update({(2 * (2 + (x + 1) % 2) + x // 2, (x + 1) % 2): (x, 4) for x in range(NX)})


def dot6(a, b, ca, cb):
    return lax.dot_general(
        a, b, (((ca,), (cb,)), ((), ())), precision=HIGHEST, preferred_element_type=F32
    )


def split(a):
    hi = a.astype(BF16)
    return hi, (a - hi.astype(F32)).astype(BF16)


def dot3(a, b, ca, cb):
    dims = (((ca,), (cb,)), ((), ()))
    ah, al = split(a)
    bh, bl = split(b)
    one = functools.partial(lax.dot_general, dimension_numbers=dims, preferred_element_type=F32)
    return one(ah, bh) + (one(ah, bl) + one(al, bh))


def gram_long(a):
    hi = a.astype(BF16).astype(F32)
    rest = a - hi
    mid = rest.astype(BF16).astype(F32)
    low = rest - mid
    lhs = jnp.concatenate([hi, hi, hi, mid, mid, low], axis=0).astype(BF16)
    rhs = jnp.concatenate([hi, mid, low, hi, mid, hi], axis=0).astype(BF16)
    return lax.dot_general(lhs, rhs, (((0,), (0,)), ((), ())), preferred_element_type=F32)


def invert_factor(m_ref, out_ref, prev, pan, between):
    lane = lax.broadcasted_iota(jnp.int32, (NB, BLK), 1)
    sub = lax.broadcasted_iota(jnp.int32, (NB, BLK), 0)
    lane_all = lax.broadcasted_iota(jnp.int32, (BLK, BLK), 1)
    eye = lax.broadcasted_iota(jnp.int32, (BLK, BLK), 0) == lane_all
    diagonal = jnp.where(eye, m_ref[...], 0.0)
    scale_row = lax.rsqrt(jnp.sum(diagonal, axis=0, keepdims=True))
    scale_col = lax.rsqrt(jnp.sum(diagonal, axis=1, keepdims=True))
    scaled = m_ref[...] * scale_col * scale_row
    m_ref[...] = scaled
    pan[...] = scaled[:NB]
    prev[...] = jnp.zeros_like(prev)

    def columns(rows, rel):
        return [
            jnp.broadcast_to(
                jnp.sum(jnp.where(rel == j, rows, 0.0), axis=1, keepdims=True), (NB, BLK)
            )
            for j in range(NB)
        ]

    def step(b, carry):
        for at, call in between:
            pl.when(b == at)(call)
        r0 = pl.multiple_of(b * NB, NB)
        after = pl.multiple_of(jnp.minimum(r0 + NB, BLK - NB), NB)
        rel = lane - r0
        inside = jnp.logical_and(rel >= 0, rel < NB)
        rel_all = lane_all - r0
        inside_before = jnp.logical_and(rel_all >= -NB, rel_all < 0)

        m_ref[...] = jnp.where(inside_before, 0.0, m_ref[...]) - gram_long(prev[...])

        rows = pan[...]
        cols = jnp.stack(columns(rows, rel))
        full = jnp.where(inside, jnp.where(rel == sub, 1.0, 0.0), rows)
        lower = full
        scale = jnp.zeros((NB, BLK), F32)
        for p in range(0, NB, 2):
            u1, u2 = cols[0], cols[1]
            a, e, d = u1[p : p + 1], u2[p : p + 1], u2[p + 1 : p + 2]
            det = a * d - e * e
            inv = pl.reciprocal(det, approx=True)
            inv = inv * (2.0 - det * inv)
            v1, v2 = d * u1 - e * u2, a * u2 - e * u1
            ia = 1.0 / a
            under = sub > p + 1
            l1 = jnp.where(under, v1 * inv, jnp.where(sub == p + 1, e * ia, 0.0))
            l2 = jnp.where(under, v2 * inv, 0.0)
            lower = lower - (l1 * lower[p : p + 1] + l2 * lower[p + 1 : p + 2])
            scale = jnp.where(sub == p, lax.rsqrt(a), scale)
            scale = jnp.where(sub == p + 1, lax.rsqrt(det * ia), scale)
            v1 = jnp.where(sub == p, det - d, jnp.where(sub == p + 1, e, v1))
            v2 = jnp.where(sub == p, e, jnp.where(sub == p + 1, det - a, v2))
            full = full - (v1 * full[p : p + 1] + v2 * full[p + 1 : p + 2]) * inv
            if p + 2 < NB:
                rest = cols[2:]
                cols = rest - (v1[None] * rest[:, p : p + 1] + v2[None] * rest[:, p + 1 : p + 2]) * inv
        lower = lower * scale
        prev[...] = lower
        out_ref[pl.ds(r0, NB), :] = lower * scale_row

        rows = m_ref[pl.ds(after, NB), :]
        terms = [m * full[j : j + 1] for j, m in enumerate(columns(rows, rel))]
        while len(terms) > 1:
            terms = [terms[i] + terms[i + 1] for i in range(0, len(terms), 2)]
        pan[...] = jnp.where(inside, 0.0, rows) - terms[0]
        return carry

    lax.fori_loop(0, BLK // NB, step, 0)


def kernel(
    mom_hbm, grad_hbm, basis_hbm, q_hbm, c_hbm, n_hbm,
    mom_ref, grad_ref, basis_ref, in_sem, b2, bsend, pown, poth, prcv, psum, pcomb, xrcv, pfull, halves, gp, zrcv, gz, yrcv, gown, gfull,
    wp, wcomb, wyrcv, wy, wzrcv, wfull, afac, xinv, mixed, mblk, iblk, prev, pan, qs, cs, sq, out_sem,
    s_pair, r_pair, s_xr, r_xr, s_xa, r_xa, s_zr, r_zr, s_y, r_y, s_gx, r_gx, s_gz, r_gz,
    s_wy, r_wy, s_wz, r_wz, s_wza, r_wza, s_wya, r_wya, s_end, r_end, s_n, r_n,
):
    f = lax.axis_index("fsdp")
    t = lax.axis_index("tensor")
    z, y = f // NY, f % NY
    x, c = t // 2, t % 2
    o = 1 - c

    pair = (f, x * 2 + o)

    def on_x(k):
        return (f, ((x + k + NX) % NX) * 2 + c)

    def on_y(k):
        return (z * NY + (y + k + NY) % NY, t)

    def on_z(k):
        return (((z + k) % NZ) * NY + y, t)

    s = 1 - 2 * c

    pending = []

    def make(src, dst, ssem, rsem, to):
        return pltpu.make_async_remote_copy(
            src_ref=src, dst_ref=dst, send_sem=ssem, recv_sem=rsem,
            device_id=to, device_id_type=MESH,
        )

    def send(*args):
        copy = make(*args)
        copy.start()
        pending.append(copy)
        return copy

    loads = [
        pltpu.make_async_copy(src, dst, in_sem.at[i])
        for i, (src, dst) in enumerate(
            (
                (mom_hbm, mom_ref),
                (grad_hbm, grad_ref),
                (basis_hbm.at[o], basis_ref.at[o]),
                (basis_hbm.at[c], basis_ref.at[c]),
            )
        )
    ]
    for load in loads:
        load.start()
    barrier = pltpu.get_barrier_semaphore()
    peers = [pair] + [on_x(k) for k in range(1, NX)]
    peers += [(f, ((x + k) % NX) * 2 + o) for k in range(1, NX)]
    peers += [on_y(k) for k in range(1, NY)] + [on_z(k) for k in range(1, NZ)]
    for peer in peers:
        pl.semaphore_signal(barrier, inc=1, device_id=peer, device_id_type=MESH)

    for load in loads[:3]:
        load.wait()
    bsend[...] = mom_ref[o] + grad_ref[o].astype(F32)
    p = dot3(bsend[...], basis_ref[o], 0, 0)
    for b in range(4):
        poth[b] = p[:, b * BLK : (b + 1) * BLK]
    pl.semaphore_wait(barrier, len(peers))
    cp = send(poth, prcv, s_pair.at[0], r_pair.at[0], pair)
    cb = send(bsend, b2.at[c], s_pair.at[1], r_pair.at[1], pair)
    own = mom_ref[c] + grad_ref[c].astype(F32)
    b2[c] = own
    loads[3].wait()
    p = dot3(own, basis_ref[c], 0, 0)
    for b in range(4):
        pown[b] = p[:, b * BLK : (b + 1) * BLK]
    cp.wait_recv()
    for b in range(4):
        psum[b] = pown[b] + prcv[b]

    def sum_start(parts, me, own, own_sem, rcv, rcv_sem, to):
        far = send(parts.at[(me + 2) % 4], rcv.at[0], own_sem.at[0], rcv_sem.at[0], to(s))
        near = send(parts.at[(me - s + 4) % 4], rcv.at[1], own_sem.at[1], rcv_sem.at[1], to(-s))
        return far, near

    def sum_relay(started, parts, me, own, own_sem, rcv, rcv_sem, to):
        started[0].wait_recv()
        own[...] = parts[(me + s + 4) % 4] + rcv[0]
        return started[1], send(own, rcv.at[2], own_sem.at[2], rcv_sem.at[2], to(s))

    def sum_end(started, parts, me, own, own_sem, rcv, rcv_sem, to):
        for copy in started:
            copy.wait_recv()
        return parts[me] + rcv[1] + rcv[2]

    def gather_start(slot, me, ssem, rsem, to):
        return [send(slot(me), slot(me), ssem.at[i], rsem.at[i], to(k)) for i, k in enumerate((s, -s))]

    def gather_relay(started, slot, me, ssem, rsem, to):
        here = slot((me - s + 4) % 4)
        return [started[1], send(here, here, ssem.at[2], rsem.at[2], to(s))]

    args = (psum, x, pcomb, s_xr, xrcv, r_xr, on_x)
    pfull[x] = sum_end(sum_relay(sum_start(*args), *args), *args)
    a_args = (lambda i: pfull.at[i], x, s_xa, r_xa, on_x)
    across = gather_start(*a_args)

    def rows8(k):
        return pl.ds(pl.multiple_of(((z + k) % NZ) * 8, 8), 8)

    first, rest = pl.ds(0, 2), pl.ds(2, 3)
    around = (4, 3, 5, 2, 6, 1, 7)

    def gram_z(part, n):
        return [
            send(
                gp.at[x, n, rows8(k), :], zrcv.at[k - 1, n],
                s_zr.at[part, k - 1], r_zr.at[part, k - 1], on_z(k),
            )
            for k in around
        ]

    def gram_y(part, n, before):
        for copy in before:
            copy.wait_recv()
        total = gp[x, n, rows8(0), :]
        for k in range(NZ - 1):
            total = total + zrcv[k, n]
        gz[n] = total
        return [
            send(gz.at[n], yrcv.at[k - 1, n], s_y.at[part, k - 1], r_y.at[part, k - 1], on_y(k))
            for k in (2, 1, 3)
        ]

    def gram_back_z(part, n):
        here = gfull.at[x, n, rows8(0), :]
        return [
            make(gown.at[n], here, s_gz.at[part, k - 1], r_gz.at[part, k - 1], on_z(k)) for k in around
        ]

    def gram_gather_z(part, n, before):
        for copy in before:
            copy.wait_recv()
        total = gz[n]
        for k in range(NY - 1):
            total = total + yrcv[k, n]
        gown[n] = total
        gfull[x, n, rows8(0), :] = total
        copies = gram_back_z(part, n)
        for copy in copies:
            copy.start()
        return copies

    w_rows = COLS // NZ

    def w_half(h):
        return pl.ds(h * COLS, COLS)

    def w_part(h, k):
        return pl.ds(pl.multiple_of(h * COLS + ((z + k) % NZ) * w_rows, 8), w_rows)

    def w_y(h):
        rows = w_half(h)
        return (
            make(wp.at[(y + 2) % NY, rows, :], wyrcv.at[0, rows, :], s_wy.at[h, 0], r_wy.at[h, 0], on_y(s)),
            make(wp.at[(y - s + NY) % NY, rows, :], wyrcv.at[1, rows, :], s_wy.at[h, 1], r_wy.at[h, 1], on_y(-s)),
            make(wcomb.at[rows, :], wyrcv.at[2, rows, :], s_wy.at[h, 2], r_wy.at[h, 2], on_y(s)),
        )

    def w_z(h):
        return [
            make(wy.at[w_part(h, k), :], wzrcv.at[h, k - 1], s_wz.at[h, k - 1], r_wz.at[h, k - 1], on_z(k))
            for k in around
        ]

    def w_back_z(h):
        here = wfull.at[y, w_part(h, 0), :]
        return [make(here, here, s_wza.at[h, k - 1], r_wza.at[h, k - 1], on_z(k)) for k in around]

    def w_back_y(h):
        here = wfull.at[y, w_half(h), :]
        other = wfull.at[(y - s + NY) % NY, w_half(h), :]
        return (
            make(here, here, s_wya.at[h, 0], r_wya.at[h, 0], on_y(s)),
            make(here, here, s_wya.at[h, 1], r_wya.at[h, 1], on_y(-s)),
            make(other, other, s_wya.at[h, 2], r_wya.at[h, 2], on_y(s)),
        )

    def w_stage(stage, h):
        rows = w_half(h)
        if stage == 1:
            _, _, relay = w_y(h)
            w_y(h)[0].wait_recv()
            wcomb[rows, :] = wp[(y + s + NY) % NY, rows, :] + wyrcv[0, rows, :]
            relay.start()
        if stage == 2:
            for copy in w_y(h)[1:]:
                copy.wait_recv()
            wy[rows, :] = wp[y, rows, :] + wyrcv[1, rows, :] + wyrcv[2, rows, :]
            for copy in w_z(h):
                copy.start()
        if stage == 3:
            for copy in w_z(h):
                copy.wait_recv()
            total = wy[w_part(h, 0), :]
            for k in range(NZ - 1):
                total = total + wzrcv[h, k]
            wfull[y, w_part(h, 0), :] = total
            for copy in w_back_z(h):
                copy.start()
        if stage == 4:
            for copy in w_back_z(h):
                copy.wait_recv()
            for copy in w_back_y(h)[:2]:
                copy.start()
        if stage == 5:
            w_back_y(h)[0].wait_recv()
            w_back_y(h)[2].start()
        if stage == 6:
            for copy in w_back_y(h)[1:]:
                copy.wait_recv()

    g = dot6(pfull[x], pfull[x], 0, 0)
    for h in range(2):
        gp[x, h] = g[h * 64 : (h + 1) * 64]
    g0 = gram_z(0, first)
    across[0].wait_recv()
    far = gather_relay(across, *a_args)[1]
    across[1].wait_recv()
    g = dot6(pfull[x + 1 - x // 3], pfull[x % 3], 0, 0)
    for h in range(2):
        gp[x, 2 + h] = g[h * 64 : (h + 1) * 64]
    between_two = (x + 1) % 2
    g = dot6(pfull[between_two + 2], pfull[between_two], 0, 0)
    for h in range(2):
        halves[h] = g[h * 64 : (h + 1) * 64]
    gp[x, 4] = halves[x // 2]
    g1 = gram_z(1, rest)
    g0 = gram_y(0, first, g0)
    far.wait_recv()
    cb.wait_recv()
    for n, k in enumerate((2, NY - s, NY + s, 0)):
        b = (y + k) % NY
        for h in range(2):
            wp[b, w_half(h), :] = dot3(b2[h], pfull[b], 1, 0)
            if n < 2:
                w_y(h)[n].start()
    g0 = gram_gather_z(0, first, g0)
    g1 = gram_y(1, rest, g1)
    for copy in g0:
        copy.wait_recv()

    def diagonals():
        here = gfull.at[x, first]
        return [make(here, here, s_gx.at[k + 2], r_gx.at[k + 2], on_x(k)) for k in (1, 3, 2)]

    def diagonal_from(chip):
        k = (x - chip + NX) % NX
        here = gfull.at[chip, first]
        return make(here, here, s_gx.at[k + 2], r_gx.at[k + 2], on_x(k))

    @pl.when(x == 0)
    def _():
        for copy in diagonals():
            copy.start()

    gram_gather_z(1, rest, g1)
    w_stage(1, 0)

    @pl.when(x != 0)
    def _():
        for copy in diagonals():
            copy.start()
        diagonal_from(0).wait_recv()

    def rest_x():
        here = gfull.at[x, rest]
        other = gfull.at[(x - s + NX) % NX, rest]
        return (
            make(here, here, s_gx.at[0], r_gx.at[0], on_x(s)),
            make(here, here, s_gx.at[1], r_gx.at[1], on_x(-s)),
            make(other, other, s_gx.at[2], r_gx.at[2], on_x(s)),
        )

    def rest_near():
        for copy in gram_back_z(1, rest):
            copy.wait_recv()
        for copy in rest_x()[:2]:
            copy.start()

    def rest_far():
        rest_x()[0].wait_recv()
        rest_x()[2].start()

    def rest_end():
        for chip in range(1, NX):

            @pl.when(x != chip)
            def _(chip=chip):
                diagonal_from(chip).wait_recv()

        for copy in rest_x()[1:]:
            copy.wait_recv()

    def let_go():
        for copy in pending:
            copy.wait_send()
        pending.clear()

    def stage(n, h):
        return functools.partial(w_stage, n, h)

    between = [
        [(2, stage(1, 1)), (2, rest_near), (5, rest_far), (6, stage(2, 0))],
        [(3, stage(3, 0)), (7, stage(3, 1))],
        [(4, stage(4, 0)), (7, stage(4, 1))],
        [(2, stage(5, 0)), (6, stage(5, 1))],
    ]

    def load(i, j):
        return jnp.concatenate([gfull[PLACE[(2 * i + h, j)]] for h in range(2)], axis=0)

    def lanes(b):
        return slice(b * BLK, (b + 1) * BLK)

    def half(i):
        return pl.ds(pl.multiple_of(i * COLS, 8), COLS)

    tril = lax.broadcasted_iota(jnp.int32, (BLK, BLK), 0) >= lax.broadcasted_iota(
        jnp.int32, (BLK, BLK), 1
    )
    def span(i, j):
        return slice(i * BLK, j * BLK)

    projected = jnp.concatenate([pfull[b] for b in range(4)], axis=1)
    afac[0, 0] = load(0, 0)
    for kb in range(4):
        mblk[...] = afac[kb, kb]
        invert_factor(mblk, iblk, prev, pan, between[kb])
        inv = jnp.where(tril, iblk[...], 0.0)
        xinv[span(kb, kb + 1), span(kb, kb + 1)] = inv
        if kb == 0:
            w_stage(2, 1)
            rest_end()
            for i in range(1, 4):
                for j in range(i + 1):
                    afac[i, j] = load(i, j)
        for i in range(kb + 1, 4):
            afac[i, kb] = dot6(afac[i, kb], inv, 1, 1)
        for i in range(kb + 1, 4):
            for j in range(kb + 1, i + 1):
                afac[i, j] = afac[i, j] - dot6(afac[i, kb], afac[j, kb], 1, 1)
        if kb > 0:
            xinv[span(kb, kb + 1), span(0, kb)] = -dot3(inv, mixed[:, span(0, kb)], 1, 0)
        qs[:, lanes(kb)] = dot3(
            projected[:, span(0, kb + 1)], xinv[span(kb, kb + 1), span(0, kb + 1)], 1, 1
        )
        if kb < 3:
            for j in range(kb + 1):
                mixed[:, span(j, j + 1)] = sum(
                    dot3(afac[kb + 1, i], xinv[span(i, i + 1), span(j, j + 1)], 1, 0)
                    for i in range(j, kb + 1)
                )
        if kb == 1:
            let_go()
    ends = [
        send(qs, q_hbm.at[c], s_end.at[0], r_end.at[0], pair),
        make(cs.at[half(o), :], c_hbm.at[c], s_end.at[1], r_end.at[1], pair),
    ]
    stores = [
        pltpu.make_async_copy(qs, q_hbm.at[c], out_sem.at[0]),
        pltpu.make_async_copy(cs.at[half(c), :], c_hbm.at[c], out_sem.at[1]),
        pltpu.make_async_copy(sq, n_hbm.at[c, x], out_sem.at[2]),
    ]
    stores[0].start()
    for h in range(2):
        w_stage(6, h)
        rows = w_half(h)
        w = jnp.concatenate([wfull[b, rows, :] for b in range(4)], axis=1)
        for kb in range(4):
            cs[rows, lanes(kb)] = dot3(
                w[:, span(0, kb + 1)], xinv[span(kb, kb + 1), span(0, kb + 1)], 1, 1
            )
    ends[1].start()
    stores[1].start()
    sq[...] = jnp.sum(cs[...] * cs[...], axis=0, keepdims=True)
    stores[2].start()
    sums = [
        send(sq, n_hbm.at[c, x], s_n.at[i], r_n.at[i], to)
        for i, to in enumerate(
            [on_x(2), on_x(1), on_x(3)]
            + [(f, ((x + k) % NX) * 2 + o) for k in (2, 1, 3, 0)]
        )
    ]
    for copy in pending[:-len(sums)]:
        copy.wait_send()
    for copy in diagonals() + list(rest_x()) + gram_back_z(0, first) + gram_back_z(1, rest):
        copy.wait_send()
    for h in range(2):
        for copy in list(w_y(h)) + w_z(h) + w_back_z(h) + list(w_back_y(h)):
            copy.wait_send()
    for copy in ends + sums:
        copy.wait_recv()
    ends[1].wait_send()
    for copy in sums:
        copy.wait_send()
    for store in stores:
        store.wait()


def finish(mom_ref, grad_ref, q_ref, c_ref, n_ref, nm_ref, nb_ref, up_ref):
    q, coeffs = q_ref[0], c_ref[0]
    error = lax.dot_general(
        coeffs.astype(BF16), q.astype(BF16), (((1,), (1,)), ((), ())), preferred_element_type=F32
    )
    nm_ref[0] = mom_ref[0] + grad_ref[0].astype(F32) - 0.05 * error
    basis = coeffs * lax.rsqrt(n_ref[0, 0] + n_ref[0, 1] + n_ref[0, 2] + n_ref[0, 3] + 1e-06)
    nb_ref[0] = basis
    up_ref[0] = (math.sqrt(D * FF / RANK) * dot3(basis, q, 1, 1)).astype(BF16)


def on_device(momentum, grad, basis):
    vm = pltpu.VMEM
    chunk = (4, BLK, BLK)
    scratch = [
        vm((2, COLS, ROWS), F32), vm((2, COLS, ROWS), BF16), vm((2, COLS, RANK), F32),
        pltpu.SemaphoreType.DMA((4,)),
        vm((2, COLS, ROWS), F32), vm((COLS, ROWS), F32),
        vm(chunk, F32), vm(chunk, F32), vm(chunk, F32), vm(chunk, F32),
        vm((BLK, BLK), F32), vm((3, BLK, BLK), F32), vm(chunk, F32),
        vm((2, 64, BLK), F32),
        vm((4, 5, 64, BLK), F32), vm((7, 5, 8, BLK), F32), vm((5, 8, BLK), F32),
        vm((3, 5, 8, BLK), F32), vm((5, 8, BLK), F32), vm((4, 5, 64, BLK), F32),
        vm((4, 2 * COLS, BLK), F32), vm((2 * COLS, BLK), F32),
        vm((3, 2 * COLS, BLK), F32), vm((2 * COLS, BLK), F32),
        vm((2, 7, COLS // NZ, BLK), F32), vm((4, 2 * COLS, BLK), F32),
        vm((4, 4, BLK, BLK), F32), vm((RANK, RANK), F32), vm((BLK, RANK), F32),
        *[vm((BLK, BLK), F32)] * 2, *[vm((NB, BLK), F32)] * 2,
        vm((ROWS, RANK), F32), vm((2 * COLS, RANK), F32),
        vm((1, RANK), F32),
        pltpu.SemaphoreType.DMA((3,)),
    ]
    for n in (2, 3, 3, (2, 7), (2, 3), 6, (2, 7), (2, 3), (2, 7), (2, 7), (2, 3), 2, 7):
        shape = n if isinstance(n, tuple) else (n,)
        scratch += [pltpu.SemaphoreType.DMA(shape), pltpu.SemaphoreType.DMA(shape)]
    hbm = pl.BlockSpec(memory_space=pl.ANY)
    momentum, grad = jnp.swapaxes(momentum, 1, 2), jnp.swapaxes(grad, 1, 2)
    q, coeffs, sums = pl.pallas_call(
        kernel,
        out_shape=(
            jax.ShapeDtypeStruct((2, ROWS, RANK), F32),
            jax.ShapeDtypeStruct((2, COLS, RANK), F32),
            jax.ShapeDtypeStruct((2, NX, 1, RANK), F32),
        ),
        in_specs=[hbm] * 3,
        out_specs=(hbm,) * 3,
        scratch_shapes=scratch,
        compiler_params=pltpu.CompilerParams(
            collective_id=0, has_side_effects=True, vmem_limit_bytes=58 * 2**20
        ),
    )(momentum, grad, basis)

    def one(*shape):
        return pl.BlockSpec((1, *shape), lambda i: (i,) + (0,) * len(shape))

    nm, nb, up = pl.pallas_call(
        finish,
        grid=(2,),
        out_shape=(
            jax.ShapeDtypeStruct((2, COLS, ROWS), F32),
            jax.ShapeDtypeStruct((2, COLS, RANK), F32),
            jax.ShapeDtypeStruct((2, COLS, ROWS), BF16),
        ),
        in_specs=[one(COLS, ROWS), one(COLS, ROWS), one(ROWS, RANK), one(COLS, RANK), one(NX, 1, RANK)],
        out_specs=(one(COLS, ROWS), one(COLS, RANK), one(COLS, ROWS)),
        compiler_params=pltpu.CompilerParams(vmem_limit_bytes=58 * 2**20),
    )(momentum, grad, q, coeffs, sums)
    return jnp.swapaxes(nm, 1, 2), nb, jnp.swapaxes(up, 1, 2)


def solution(mesh):
    in_specs = (P(None, "fsdp", "tensor"), P(None, "fsdp", "tensor"), P(None, "tensor", None))
    out_specs = (P(None, "fsdp", "tensor"), P(None, "tensor", None), P(None, "fsdp", "tensor"))
    return jax.shard_map(
        on_device, mesh=mesh, in_specs=in_specs, out_specs=out_specs, check_vma=False
    )
```

```python
import functools
import math

import jax
import jax.numpy as jnp
from jax import lax
from jax.experimental import pallas as pl
from jax.experimental.pallas import tpu as pltpu
from jax.sharding import PartitionSpec as P

D = 4096
FF = 1536
RANK = 512
NX, NY, NZ = 4, 4, 8
ROWS = 128
COLS = 192
BLK = 128
NB = 16
F32 = jnp.float32
BF16 = jnp.bfloat16
HIGHEST = lax.Precision.HIGHEST
MESH = pl.DeviceIdType.MESH

PLACE = {(2 * x + h, x): (x, h) for x in range(NX) for h in range(2)}
PLACE.update({(2 * (x + 1 - x // 3) + h, x % 3): (x, 2 + h) for x in range(NX) for h in range(2)})
PLACE.update({(2 * (2 + (x + 1) % 2) + x // 2, (x + 1) % 2): (x, 4) for x in range(NX)})


def dot6(a, b, ca, cb):
    return lax.dot_general(
        a, b, (((ca,), (cb,)), ((), ())), precision=HIGHEST, preferred_element_type=F32
    )


def split(a):
    hi = a.astype(BF16)
    return hi, (a - hi.astype(F32)).astype(BF16)


def dot3(a, b, ca, cb):
    dims = (((ca,), (cb,)), ((), ()))
    ah, al = split(a)
    bh, bl = split(b)
    one = functools.partial(lax.dot_general, dimension_numbers=dims, preferred_element_type=F32)
    return one(ah, bh) + (one(ah, bl) + one(al, bh))


def gram_long(a):
    hi = a.astype(BF16).astype(F32)
    rest = a - hi
    mid = rest.astype(BF16).astype(F32)
    low = rest - mid
    lhs = jnp.concatenate([hi, hi, hi, mid, mid, low], axis=0).astype(BF16)
    rhs = jnp.concatenate([hi, mid, low, hi, mid, hi], axis=0).astype(BF16)
    return lax.dot_general(lhs, rhs, (((0,), (0,)), ((), ())), preferred_element_type=F32)


def invert_factor(m_ref, out_ref, prev, pan, between):
    lane = lax.broadcasted_iota(jnp.int32, (NB, BLK), 1)
    sub = lax.broadcasted_iota(jnp.int32, (NB, BLK), 0)
    lane_all = lax.broadcasted_iota(jnp.int32, (BLK, BLK), 1)
    eye = lax.broadcasted_iota(jnp.int32, (BLK, BLK), 0) == lane_all
    diagonal = jnp.where(eye, m_ref[...], 0.0)
    scale_row = lax.rsqrt(jnp.sum(diagonal, axis=0, keepdims=True))
    scale_col = lax.rsqrt(jnp.sum(diagonal, axis=1, keepdims=True))
    scaled = m_ref[...] * scale_col * scale_row
    m_ref[...] = scaled
    pan[...] = scaled[:NB]
    prev[...] = jnp.zeros_like(prev)

    def columns(rows, rel):
        return [
            jnp.broadcast_to(
                jnp.sum(jnp.where(rel == j, rows, 0.0), axis=1, keepdims=True), (NB, BLK)
            )
            for j in range(NB)
        ]

    def step(b, carry):
        for at, call in between:
            pl.when(b == at)(call)
        r0 = pl.multiple_of(b * NB, NB)
        after = pl.multiple_of(jnp.minimum(r0 + NB, BLK - NB), NB)
        rel = lane - r0
        inside = jnp.logical_and(rel >= 0, rel < NB)
        rel_all = lane_all - r0
        inside_before = jnp.logical_and(rel_all >= -NB, rel_all < 0)

        m_ref[...] = jnp.where(inside_before, 0.0, m_ref[...]) - gram_long(prev[...])

        rows = pan[...]
        cols = jnp.stack(columns(rows, rel))
        full = jnp.where(inside, jnp.where(rel == sub, 1.0, 0.0), rows)
        lower = full
        scale = jnp.zeros((NB, BLK), F32)
        for p in range(0, NB, 2):
            u1, u2 = cols[0], cols[1]
            a, e, d = u1[p : p + 1], u2[p : p + 1], u2[p + 1 : p + 2]
            det = a * d - e * e
            inv = pl.reciprocal(det, approx=True)
            inv = inv * (2.0 - det * inv)
            v1, v2 = d * u1 - e * u2, a * u2 - e * u1
            ia = 1.0 / a
            under = sub > p + 1
            l1 = jnp.where(under, v1 * inv, jnp.where(sub == p + 1, e * ia, 0.0))
            l2 = jnp.where(under, v2 * inv, 0.0)
            lower = lower - (l1 * lower[p : p + 1] + l2 * lower[p + 1 : p + 2])
            scale = jnp.where(sub == p, lax.rsqrt(a), scale)
            scale = jnp.where(sub == p + 1, lax.rsqrt(det * ia), scale)
            v1 = jnp.where(sub == p, det - d, jnp.where(sub == p + 1, e, v1))
            v2 = jnp.where(sub == p, e, jnp.where(sub == p + 1, det - a, v2))
            full = full - (v1 * full[p : p + 1] + v2 * full[p + 1 : p + 2]) * inv
            if p + 2 < NB:
                rest = cols[2:]
                cols = rest - (v1[None] * rest[:, p : p + 1] + v2[None] * rest[:, p + 1 : p + 2]) * inv
        lower = lower * scale
        prev[...] = lower
        out_ref[pl.ds(r0, NB), :] = lower * scale_row

        rows = m_ref[pl.ds(after, NB), :]
        terms = [m * full[j : j + 1] for j, m in enumerate(columns(rows, rel))]
        while len(terms) > 1:
            terms = [terms[i] + terms[i + 1] for i in range(0, len(terms), 2)]
        pan[...] = jnp.where(inside, 0.0, rows) - terms[0]
        return carry

    lax.fori_loop(0, BLK // NB, step, 0)


def kernel(
    mom_hbm, grad_hbm, basis_hbm, q_hbm, c_hbm, n_hbm,
    mom_ref, grad_ref, basis_ref, in_sem, b2, bsend, pown, poth, prcv, psum, pcomb, xrcv, pfull, halves, gp, zrcv, gz, yrcv, gown, gfull,
    wp, wcomb, wyrcv, wy, wzrcv, wfull, afac, xinv, mixed, mblk, iblk, prev, pan, qs, cs, sq, out_sem,
    s_pair, r_pair, s_xr, r_xr, s_xa, r_xa, s_zr, r_zr, s_y, r_y, s_gx, r_gx, s_gz, r_gz,
    s_wy, r_wy, s_wz, r_wz, s_wza, r_wza, s_wya, r_wya, s_end, r_end, s_n, r_n,
):
    f = lax.axis_index("fsdp")
    t = lax.axis_index("tensor")
    z, y = f // NY, f % NY
    x, c = t // 2, t % 2
    o = 1 - c

    pair = (f, x * 2 + o)

    def on_x(k):
        return (f, ((x + k + NX) % NX) * 2 + c)

    def on_y(k):
        return (z * NY + (y + k + NY) % NY, t)

    def on_z(k):
        return (((z + k) % NZ) * NY + y, t)

    s = 1 - 2 * c

    pending = []

    def make(src, dst, ssem, rsem, to):
        return pltpu.make_async_remote_copy(
            src_ref=src, dst_ref=dst, send_sem=ssem, recv_sem=rsem,
            device_id=to, device_id_type=MESH,
        )

    def send(*args):
        copy = make(*args)
        copy.start()
        pending.append(copy)
        return copy

    loads = [
        pltpu.make_async_copy(src, dst, in_sem.at[i])
        for i, (src, dst) in enumerate(
            (
                (mom_hbm, mom_ref),
                (grad_hbm, grad_ref),
                (basis_hbm.at[o], basis_ref.at[o]),
                (basis_hbm.at[c], basis_ref.at[c]),
            )
        )
    ]
    for load in loads:
        load.start()
    barrier = pltpu.get_barrier_semaphore()
    peers = [pair] + [on_x(k) for k in range(1, NX)]
    peers += [(f, ((x + k) % NX) * 2 + o) for k in range(1, NX)]
    peers += [on_y(k) for k in range(1, NY)] + [on_z(k) for k in range(1, NZ)]
    for peer in peers:
        pl.semaphore_signal(barrier, inc=1, device_id=peer, device_id_type=MESH)

    for load in loads[:3]:
        load.wait()
    bsend[...] = mom_ref[o] + grad_ref[o].astype(F32)
    p = dot3(bsend[...], basis_ref[o], 0, 0)
    for b in range(4):
        poth[b] = p[:, b * BLK : (b + 1) * BLK]
    pl.semaphore_wait(barrier, len(peers))
    cp = send(poth, prcv, s_pair.at[0], r_pair.at[0], pair)
    cb = send(bsend, b2.at[c], s_pair.at[1], r_pair.at[1], pair)
    own = mom_ref[c] + grad_ref[c].astype(F32)
    b2[c] = own
    loads[3].wait()
    p = dot3(own, basis_ref[c], 0, 0)
    for b in range(4):
        pown[b] = p[:, b * BLK : (b + 1) * BLK]
    cp.wait_recv()
    for b in range(4):
        psum[b] = pown[b] + prcv[b]

    def sum_start(parts, me, own, own_sem, rcv, rcv_sem, to):
        far = send(parts.at[(me + 2) % 4], rcv.at[0], own_sem.at[0], rcv_sem.at[0], to(s))
        near = send(parts.at[(me - s + 4) % 4], rcv.at[1], own_sem.at[1], rcv_sem.at[1], to(-s))
        return far, near

    def sum_relay(started, parts, me, own, own_sem, rcv, rcv_sem, to):
        started[0].wait_recv()
        own[...] = parts[(me + s + 4) % 4] + rcv[0]
        return started[1], send(own, rcv.at[2], own_sem.at[2], rcv_sem.at[2], to(s))

    def sum_end(started, parts, me, own, own_sem, rcv, rcv_sem, to):
        for copy in started:
            copy.wait_recv()
        return parts[me] + rcv[1] + rcv[2]

    def gather_start(slot, me, ssem, rsem, to):
        return [send(slot(me), slot(me), ssem.at[i], rsem.at[i], to(k)) for i, k in enumerate((s, -s))]

    def gather_relay(started, slot, me, ssem, rsem, to):
        here = slot((me - s + 4) % 4)
        return [started[1], send(here, here, ssem.at[2], rsem.at[2], to(s))]

    args = (psum, x, pcomb, s_xr, xrcv, r_xr, on_x)
    pfull[x] = sum_end(sum_relay(sum_start(*args), *args), *args)
    a_args = (lambda i: pfull.at[i], x, s_xa, r_xa, on_x)
    across = gather_start(*a_args)

    def rows8(k):
        return pl.ds(pl.multiple_of(((z + k) % NZ) * 8, 8), 8)

    first, rest = pl.ds(0, 2), pl.ds(2, 3)
    around = (4, 3, 5, 2, 6, 1, 7)

    def gram_z(part, n):
        return [
            send(
                gp.at[x, n, rows8(k), :], zrcv.at[k - 1, n],
                s_zr.at[part, k - 1], r_zr.at[part, k - 1], on_z(k),
            )
            for k in around
        ]

    def gram_y(part, n, before):
        for copy in before:
            copy.wait_recv()
        total = gp[x, n, rows8(0), :]
        for k in range(NZ - 1):
            total = total + zrcv[k, n]
        gz[n] = total
        return [
            send(gz.at[n], yrcv.at[k - 1, n], s_y.at[part, k - 1], r_y.at[part, k - 1], on_y(k))
            for k in (2, 1, 3)
        ]

    def gram_back_z(part, n):
        here = gfull.at[x, n, rows8(0), :]
        return [
            make(gown.at[n], here, s_gz.at[part, k - 1], r_gz.at[part, k - 1], on_z(k)) for k in around
        ]

    def gram_gather_z(part, n, before):
        for copy in before:
            copy.wait_recv()
        total = gz[n]
        for k in range(NY - 1):
            total = total + yrcv[k, n]
        gown[n] = total
        gfull[x, n, rows8(0), :] = total
        copies = gram_back_z(part, n)
        for copy in copies:
            copy.start()
        return copies

    w_rows = COLS // NZ

    def w_half(h):
        return pl.ds(h * COLS, COLS)

    def w_part(h, k):
        return pl.ds(pl.multiple_of(h * COLS + ((z + k) % NZ) * w_rows, 8), w_rows)

    def w_y(h):
        rows = w_half(h)
        return (
            make(wp.at[(y + 2) % NY, rows, :], wyrcv.at[0, rows, :], s_wy.at[h, 0], r_wy.at[h, 0], on_y(s)),
            make(wp.at[(y - s + NY) % NY, rows, :], wyrcv.at[1, rows, :], s_wy.at[h, 1], r_wy.at[h, 1], on_y(-s)),
            make(wcomb.at[rows, :], wyrcv.at[2, rows, :], s_wy.at[h, 2], r_wy.at[h, 2], on_y(s)),
        )

    def w_z(h):
        return [
            make(wy.at[w_part(h, k), :], wzrcv.at[h, k - 1], s_wz.at[h, k - 1], r_wz.at[h, k - 1], on_z(k))
            for k in around
        ]

    def w_back_z(h):
        here = wfull.at[y, w_part(h, 0), :]
        return [make(here, here, s_wza.at[h, k - 1], r_wza.at[h, k - 1], on_z(k)) for k in around]

    def w_back_y(h):
        here = wfull.at[y, w_half(h), :]
        other = wfull.at[(y - s + NY) % NY, w_half(h), :]
        return (
            make(here, here, s_wya.at[h, 0], r_wya.at[h, 0], on_y(s)),
            make(here, here, s_wya.at[h, 1], r_wya.at[h, 1], on_y(-s)),
            make(other, other, s_wya.at[h, 2], r_wya.at[h, 2], on_y(s)),
        )

    def w_stage(stage, h):
        rows = w_half(h)
        if stage == 1:
            _, _, relay = w_y(h)
            w_y(h)[0].wait_recv()
            wcomb[rows, :] = wp[(y + s + NY) % NY, rows, :] + wyrcv[0, rows, :]
            relay.start()
        if stage == 2:
            for copy in w_y(h)[1:]:
                copy.wait_recv()
            wy[rows, :] = wp[y, rows, :] + wyrcv[1, rows, :] + wyrcv[2, rows, :]
            for copy in w_z(h):
                copy.start()
        if stage == 3:
            for copy in w_z(h):
                copy.wait_recv()
            total = wy[w_part(h, 0), :]
            for k in range(NZ - 1):
                total = total + wzrcv[h, k]
            wfull[y, w_part(h, 0), :] = total
            for copy in w_back_z(h):
                copy.start()
        if stage == 4:
            for copy in w_back_z(h):
                copy.wait_recv()
            for copy in w_back_y(h)[:2]:
                copy.start()
        if stage == 5:
            w_back_y(h)[0].wait_recv()
            w_back_y(h)[2].start()
        if stage == 6:
            for copy in w_back_y(h)[1:]:
                copy.wait_recv()

    g = dot6(pfull[x], pfull[x], 0, 0)
    for h in range(2):
        gp[x, h] = g[h * 64 : (h + 1) * 64]
    g0 = gram_z(0, first)
    across[0].wait_recv()
    far = gather_relay(across, *a_args)[1]
    across[1].wait_recv()
    g = dot6(pfull[x + 1 - x // 3], pfull[x % 3], 0, 0)
    for h in range(2):
        gp[x, 2 + h] = g[h * 64 : (h + 1) * 64]
    between_two = (x + 1) % 2
    g = dot6(pfull[between_two + 2], pfull[between_two], 0, 0)
    for h in range(2):
        halves[h] = g[h * 64 : (h + 1) * 64]
    gp[x, 4] = halves[x // 2]
    g1 = gram_z(1, rest)
    g0 = gram_y(0, first, g0)
    far.wait_recv()
    cb.wait_recv()
    for n, k in enumerate((2, NY - s, NY + s, 0)):
        b = (y + k) % NY
        for h in range(2):
            wp[b, w_half(h), :] = dot3(b2[h], pfull[b], 1, 0)
            if n < 2:
                w_y(h)[n].start()
    g0 = gram_gather_z(0, first, g0)
    g1 = gram_y(1, rest, g1)
    for copy in g0:
        copy.wait_recv()

    def diagonals():
        here = gfull.at[x, first]
        return [make(here, here, s_gx.at[k + 2], r_gx.at[k + 2], on_x(k)) for k in (1, 3, 2)]

    def diagonal_from(chip):
        k = (x - chip + NX) % NX
        here = gfull.at[chip, first]
        return make(here, here, s_gx.at[k + 2], r_gx.at[k + 2], on_x(k))

    @pl.when(x == 0)
    def _():
        for copy in diagonals():
            copy.start()

    gram_gather_z(1, rest, g1)
    w_stage(1, 0)

    @pl.when(x != 0)
    def _():
        for copy in diagonals():
            copy.start()
        diagonal_from(0).wait_recv()

    def rest_x():
        here = gfull.at[x, rest]
        other = gfull.at[(x - s + NX) % NX, rest]
        return (
            make(here, here, s_gx.at[0], r_gx.at[0], on_x(s)),
            make(here, here, s_gx.at[1], r_gx.at[1], on_x(-s)),
            make(other, other, s_gx.at[2], r_gx.at[2], on_x(s)),
        )

    def rest_near():
        for copy in gram_back_z(1, rest):
            copy.wait_recv()
        for copy in rest_x()[:2]:
            copy.start()

    def rest_far():
        rest_x()[0].wait_recv()
        rest_x()[2].start()

    def rest_end():
        for chip in range(1, NX):

            @pl.when(x != chip)
            def _(chip=chip):
                diagonal_from(chip).wait_recv()

        for copy in rest_x()[1:]:
            copy.wait_recv()

    def let_go():
        for copy in pending:
            copy.wait_send()
        pending.clear()

    def stage(n, h):
        return functools.partial(w_stage, n, h)

    between = [
        [(1, stage(1, 1)), (2, rest_near), (4, stage(2, 0)), (5, rest_far), (7, stage(2, 1))],
        [(1, stage(3, 0)), (4, stage(3, 1)), (7, stage(4, 0))],
        [(1, stage(4, 1)), (4, stage(5, 0)), (7, stage(5, 1))],
        [],
    ]

    def load(i, j):
        return jnp.concatenate([gfull[PLACE[(2 * i + h, j)]] for h in range(2)], axis=0)

    def lanes(b):
        return slice(b * BLK, (b + 1) * BLK)

    def half(i):
        return pl.ds(pl.multiple_of(i * COLS, 8), COLS)

    tril = lax.broadcasted_iota(jnp.int32, (BLK, BLK), 0) >= lax.broadcasted_iota(
        jnp.int32, (BLK, BLK), 1
    )
    def span(i, j):
        return slice(i * BLK, j * BLK)

    projected = jnp.concatenate([pfull[b] for b in range(4)], axis=1)
    afac[0, 0] = load(0, 0)
    for kb in range(4):
        mblk[...] = afac[kb, kb]
        invert_factor(mblk, iblk, prev, pan, between[kb])
        inv = jnp.where(tril, iblk[...], 0.0)
        xinv[span(kb, kb + 1), span(kb, kb + 1)] = inv
        if kb == 0:
            rest_end()
            for i in range(1, 4):
                for j in range(i + 1):
                    afac[i, j] = load(i, j)
        for i in range(kb + 1, 4):
            afac[i, kb] = dot6(afac[i, kb], inv, 1, 1)
        for i in range(kb + 1, 4):
            for j in range(kb + 1, i + 1):
                afac[i, j] = afac[i, j] - dot6(afac[i, kb], afac[j, kb], 1, 1)
        if kb > 0:
            xinv[span(kb, kb + 1), span(0, kb)] = -dot3(inv, mixed[:, span(0, kb)], 1, 0)
        qs[:, lanes(kb)] = dot3(
            projected[:, span(0, kb + 1)], xinv[span(kb, kb + 1), span(0, kb + 1)], 1, 1
        )
        if kb < 3:
            for j in range(kb + 1):
                mixed[:, span(j, j + 1)] = sum(
                    dot3(afac[kb + 1, i], xinv[span(i, i + 1), span(j, j + 1)], 1, 0)
                    for i in range(j, kb + 1)
                )
        if kb == 1:
            let_go()
    ends = [
        send(qs, q_hbm.at[c], s_end.at[0], r_end.at[0], pair),
        make(cs.at[half(o), :], c_hbm.at[c], s_end.at[1], r_end.at[1], pair),
    ]
    stores = [
        pltpu.make_async_copy(qs, q_hbm.at[c], out_sem.at[0]),
        pltpu.make_async_copy(cs.at[half(c), :], c_hbm.at[c], out_sem.at[1]),
        pltpu.make_async_copy(sq, n_hbm.at[c, x], out_sem.at[2]),
    ]
    stores[0].start()
    for h in range(2):
        w_stage(6, h)
        rows = w_half(h)
        w = jnp.concatenate([wfull[b, rows, :] for b in range(4)], axis=1)
        for kb in range(4):
            cs[rows, lanes(kb)] = dot3(
                w[:, span(0, kb + 1)], xinv[span(kb, kb + 1), span(0, kb + 1)], 1, 1
            )
    ends[1].start()
    stores[1].start()
    sq[...] = jnp.sum(cs[...] * cs[...], axis=0, keepdims=True)
    stores[2].start()
    sums = [
        send(sq, n_hbm.at[c, x], s_n.at[i], r_n.at[i], to)
        for i, to in enumerate(
            [on_x(2), on_x(1), on_x(3)]
            + [(f, ((x + k) % NX) * 2 + o) for k in (2, 1, 3, 0)]
        )
    ]
    for copy in pending[:-len(sums)]:
        copy.wait_send()
    for copy in diagonals() + list(rest_x()) + gram_back_z(0, first) + gram_back_z(1, rest):
        copy.wait_send()
    for h in range(2):
        for copy in list(w_y(h)) + w_z(h) + w_back_z(h) + list(w_back_y(h)):
            copy.wait_send()
    for copy in ends + sums:
        copy.wait_recv()
    ends[1].wait_send()
    for copy in sums:
        copy.wait_send()
    for store in stores:
        store.wait()


def finish(mom_ref, grad_ref, q_ref, c_ref, n_ref, nm_ref, nb_ref, up_ref):
    q, coeffs = q_ref[0], c_ref[0]
    error = lax.dot_general(
        coeffs.astype(BF16), q.astype(BF16), (((1,), (1,)), ((), ())), preferred_element_type=F32
    )
    nm_ref[0] = mom_ref[0] + grad_ref[0].astype(F32) - 0.05 * error
    basis = coeffs * lax.rsqrt(n_ref[0, 0] + n_ref[0, 1] + n_ref[0, 2] + n_ref[0, 3] + 1e-06)
    nb_ref[0] = basis
    up_ref[0] = (math.sqrt(D * FF / RANK) * dot3(basis, q, 1, 1)).astype(BF16)


def on_device(momentum, grad, basis):
    vm = pltpu.VMEM
    chunk = (4, BLK, BLK)
    scratch = [
        vm((2, COLS, ROWS), F32), vm((2, COLS, ROWS), BF16), vm((2, COLS, RANK), F32),
        pltpu.SemaphoreType.DMA((4,)),
        vm((2, COLS, ROWS), F32), vm((COLS, ROWS), F32),
        vm(chunk, F32), vm(chunk, F32), vm(chunk, F32), vm(chunk, F32),
        vm((BLK, BLK), F32), vm((3, BLK, BLK), F32), vm(chunk, F32),
        vm((2, 64, BLK), F32),
        vm((4, 5, 64, BLK), F32), vm((7, 5, 8, BLK), F32), vm((5, 8, BLK), F32),
        vm((3, 5, 8, BLK), F32), vm((5, 8, BLK), F32), vm((4, 5, 64, BLK), F32),
        vm((4, 2 * COLS, BLK), F32), vm((2 * COLS, BLK), F32),
        vm((3, 2 * COLS, BLK), F32), vm((2 * COLS, BLK), F32),
        vm((2, 7, COLS // NZ, BLK), F32), vm((4, 2 * COLS, BLK), F32),
        vm((4, 4, BLK, BLK), F32), vm((RANK, RANK), F32), vm((BLK, RANK), F32),
        *[vm((BLK, BLK), F32)] * 2, *[vm((NB, BLK), F32)] * 2,
        vm((ROWS, RANK), F32), vm((2 * COLS, RANK), F32),
        vm((1, RANK), F32),
        pltpu.SemaphoreType.DMA((3,)),
    ]
    for n in (2, 3, 3, (2, 7), (2, 3), 6, (2, 7), (2, 3), (2, 7), (2, 7), (2, 3), 2, 7):
        shape = n if isinstance(n, tuple) else (n,)
        scratch += [pltpu.SemaphoreType.DMA(shape), pltpu.SemaphoreType.DMA(shape)]
    hbm = pl.BlockSpec(memory_space=pl.ANY)
    momentum, grad = jnp.swapaxes(momentum, 1, 2), jnp.swapaxes(grad, 1, 2)
    q, coeffs, sums = pl.pallas_call(
        kernel,
        out_shape=(
            jax.ShapeDtypeStruct((2, ROWS, RANK), F32),
            jax.ShapeDtypeStruct((2, COLS, RANK), F32),
            jax.ShapeDtypeStruct((2, NX, 1, RANK), F32),
        ),
        in_specs=[hbm] * 3,
        out_specs=(hbm,) * 3,
        scratch_shapes=scratch,
        compiler_params=pltpu.CompilerParams(
            collective_id=0, has_side_effects=True, vmem_limit_bytes=58 * 2**20
        ),
    )(momentum, grad, basis)

    def one(*shape):
        return pl.BlockSpec((1, *shape), lambda i: (i,) + (0,) * len(shape))

    nm, nb, up = pl.pallas_call(
        finish,
        grid=(2,),
        out_shape=(
            jax.ShapeDtypeStruct((2, COLS, ROWS), F32),
            jax.ShapeDtypeStruct((2, COLS, RANK), F32),
            jax.ShapeDtypeStruct((2, COLS, ROWS), BF16),
        ),
        in_specs=[one(COLS, ROWS), one(COLS, ROWS), one(ROWS, RANK), one(COLS, RANK), one(NX, 1, RANK)],
        out_specs=(one(COLS, ROWS), one(COLS, RANK), one(COLS, ROWS)),
        compiler_params=pltpu.CompilerParams(vmem_limit_bytes=58 * 2**20),
    )(momentum, grad, q, coeffs, sums)
    return jnp.swapaxes(nm, 1, 2), nb, jnp.swapaxes(up, 1, 2)


def solution(mesh):
    in_specs = (P(None, "fsdp", "tensor"), P(None, "fsdp", "tensor"), P(None, "tensor", None))
    out_specs = (P(None, "fsdp", "tensor"), P(None, "tensor", None), P(None, "fsdp", "tensor"))
    return jax.shard_map(
        on_device, mesh=mesh, in_specs=in_specs, out_specs=out_specs, check_vma=False
    )
```

```python
import functools
import math

import jax
import jax.numpy as jnp
from jax import lax
from jax.experimental import pallas as pl
from jax.experimental.pallas import tpu as pltpu
from jax.sharding import PartitionSpec as P

D = 4096
FF = 1536
RANK = 512
NX, NY, NZ = 4, 4, 8
ROWS = 128
COLS = 192
BLK = 128
NB = 16
F32 = jnp.float32
BF16 = jnp.bfloat16
HIGHEST = lax.Precision.HIGHEST
MESH = pl.DeviceIdType.MESH

PLACE = {(2 * x + h, x): (x, h) for x in range(NX) for h in range(2)}
PLACE.update({(2 * (x + 1 - x // 3) + h, x % 3): (x, 2 + h) for x in range(NX) for h in range(2)})
PLACE.update({(2 * (2 + (x + 1) % 2) + x // 2, (x + 1) % 2): (x, 4) for x in range(NX)})


def dot6(a, b, ca, cb):
    return lax.dot_general(
        a, b, (((ca,), (cb,)), ((), ())), precision=HIGHEST, preferred_element_type=F32
    )


def split(a):
    hi = a.astype(BF16)
    return hi, (a - hi.astype(F32)).astype(BF16)


def dot3(a, b, ca, cb):
    dims = (((ca,), (cb,)), ((), ()))
    ah, al = split(a)
    bh, bl = split(b)
    one = functools.partial(lax.dot_general, dimension_numbers=dims, preferred_element_type=F32)
    return one(ah, bh) + (one(ah, bl) + one(al, bh))


def gram_long(a):
    hi = a.astype(BF16).astype(F32)
    rest = a - hi
    mid = rest.astype(BF16).astype(F32)
    low = rest - mid
    lhs = jnp.concatenate([hi, hi, hi, mid, mid, low], axis=0).astype(BF16)
    rhs = jnp.concatenate([hi, mid, low, hi, mid, hi], axis=0).astype(BF16)
    return lax.dot_general(lhs, rhs, (((0,), (0,)), ((), ())), preferred_element_type=F32)


def invert_factor(m_ref, out_ref, prev, pan, between):
    lane = lax.broadcasted_iota(jnp.int32, (NB, BLK), 1)
    sub = lax.broadcasted_iota(jnp.int32, (NB, BLK), 0)
    lane_all = lax.broadcasted_iota(jnp.int32, (BLK, BLK), 1)
    eye = lax.broadcasted_iota(jnp.int32, (BLK, BLK), 0) == lane_all
    diagonal = jnp.where(eye, m_ref[...], 0.0)
    scale_row = lax.rsqrt(jnp.sum(diagonal, axis=0, keepdims=True))
    scale_col = lax.rsqrt(jnp.sum(diagonal, axis=1, keepdims=True))
    scaled = m_ref[...] * scale_col * scale_row
    m_ref[...] = scaled
    pan[...] = scaled[:NB]
    prev[...] = jnp.zeros_like(prev)

    def columns(rows, rel):
        return [
            jnp.broadcast_to(
                jnp.sum(jnp.where(rel == j, rows, 0.0), axis=1, keepdims=True), (NB, BLK)
            )
            for j in range(NB)
        ]

    def step(b, carry):
        for at, call in between:
            pl.when(b == at)(call)
        r0 = pl.multiple_of(b * NB, NB)
        after = pl.multiple_of(jnp.minimum(r0 + NB, BLK - NB), NB)
        rel = lane - r0
        inside = jnp.logical_and(rel >= 0, rel < NB)
        rel_all = lane_all - r0
        inside_before = jnp.logical_and(rel_all >= -NB, rel_all < 0)

        m_ref[...] = jnp.where(inside_before, 0.0, m_ref[...]) - gram_long(prev[...])

        rows = pan[...]
        cols = jnp.stack(columns(rows, rel))
        full = jnp.where(inside, jnp.where(rel == sub, 1.0, 0.0), rows)
        lower = full
        scale = jnp.zeros((NB, BLK), F32)
        for p in range(0, NB, 2):
            u1, u2 = cols[0], cols[1]
            a, e, d = u1[p : p + 1], u2[p : p + 1], u2[p + 1 : p + 2]
            det = a * d - e * e
            inv = pl.reciprocal(det, approx=True)
            inv = inv * (2.0 - det * inv)
            v1, v2 = d * u1 - e * u2, a * u2 - e * u1
            ia = 1.0 / a
            under = sub > p + 1
            w1, w2 = v1 * inv, v2 * inv
            l1 = jnp.where(under, w1, jnp.where(sub == p + 1, e * ia, 0.0))
            l2 = jnp.where(under, w2, 0.0)
            lower = lower - (l1 * lower[p : p + 1] + l2 * lower[p + 1 : p + 2])
            scale = jnp.where(sub == p, lax.rsqrt(a), scale)
            scale = jnp.where(sub == p + 1, lax.rsqrt(det * ia), scale)
            w1 = jnp.where(sub == p, 1.0 - d * inv, jnp.where(sub == p + 1, e * inv, w1))
            w2 = jnp.where(sub == p, e * inv, jnp.where(sub == p + 1, 1.0 - a * inv, w2))
            if p + 2 < NB:
                rest = cols[2:]
                cols = rest - (w1[None] * rest[:, p : p + 1] + w2[None] * rest[:, p + 1 : p + 2])
            full = full - (w1 * full[p : p + 1] + w2 * full[p + 1 : p + 2])
        lower = lower * scale
        prev[...] = lower
        out_ref[pl.ds(r0, NB), :] = lower * scale_row

        rows = m_ref[pl.ds(after, NB), :]
        terms = [m * full[j : j + 1] for j, m in enumerate(columns(rows, rel))]
        while len(terms) > 1:
            terms = [terms[i] + terms[i + 1] for i in range(0, len(terms), 2)]
        pan[...] = jnp.where(inside, 0.0, rows) - terms[0]
        return carry

    lax.fori_loop(0, BLK // NB, step, 0)


def kernel(
    mom_hbm, grad_hbm, basis_hbm, q_hbm, c_hbm, n_hbm,
    mom_ref, grad_ref, basis_ref, in_sem, b2, bsend, pown, poth, prcv, psum, pcomb, xrcv, pfull, halves, gp, zrcv, gz, yrcv, gown, gfull,
    wp, wcomb, wyrcv, wy, wzrcv, wfull, afac, xinv, mixed, mblk, iblk, prev, pan, qs, cs, sq, out_sem,
    s_pair, r_pair, s_xr, r_xr, s_xa, r_xa, s_zr, r_zr, s_y, r_y, s_gx, r_gx, s_gz, r_gz,
    s_wy, r_wy, s_wz, r_wz, s_wza, r_wza, s_wya, r_wya, s_end, r_end, s_n, r_n,
):
    f = lax.axis_index("fsdp")
    t = lax.axis_index("tensor")
    z, y = f // NY, f % NY
    x, c = t // 2, t % 2
    o = 1 - c

    pair = (f, x * 2 + o)

    def on_x(k):
        return (f, ((x + k + NX) % NX) * 2 + c)

    def on_y(k):
        return (z * NY + (y + k + NY) % NY, t)

    def on_z(k):
        return (((z + k) % NZ) * NY + y, t)

    s = 1 - 2 * c

    pending = []

    def make(src, dst, ssem, rsem, to):
        return pltpu.make_async_remote_copy(
            src_ref=src, dst_ref=dst, send_sem=ssem, recv_sem=rsem,
            device_id=to, device_id_type=MESH,
        )

    def send(*args):
        copy = make(*args)
        copy.start()
        pending.append(copy)
        return copy

    loads = [
        pltpu.make_async_copy(src, dst, in_sem.at[i])
        for i, (src, dst) in enumerate(
            (
                (mom_hbm, mom_ref),
                (grad_hbm, grad_ref),
                (basis_hbm.at[o], basis_ref.at[o]),
                (basis_hbm.at[c], basis_ref.at[c]),
            )
        )
    ]
    for load in loads:
        load.start()
    barrier = pltpu.get_barrier_semaphore()
    peers = [pair] + [on_x(k) for k in range(1, NX)]
    peers += [(f, ((x + k) % NX) * 2 + o) for k in range(1, NX)]
    peers += [on_y(k) for k in range(1, NY)] + [on_z(k) for k in range(1, NZ)]
    for peer in peers:
        pl.semaphore_signal(barrier, inc=1, device_id=peer, device_id_type=MESH)

    for load in loads[:3]:
        load.wait()
    bsend[...] = mom_ref[o] + grad_ref[o].astype(F32)
    p = dot3(bsend[...], basis_ref[o], 0, 0)
    for b in range(4):
        poth[b] = p[:, b * BLK : (b + 1) * BLK]
    pl.semaphore_wait(barrier, len(peers))
    cp = send(poth, prcv, s_pair.at[0], r_pair.at[0], pair)
    cb = send(bsend, b2.at[c], s_pair.at[1], r_pair.at[1], pair)
    own = mom_ref[c] + grad_ref[c].astype(F32)
    b2[c] = own
    loads[3].wait()
    p = dot3(own, basis_ref[c], 0, 0)
    for b in range(4):
        pown[b] = p[:, b * BLK : (b + 1) * BLK]
    cp.wait_recv()
    for b in range(4):
        psum[b] = pown[b] + prcv[b]

    def sum_start(parts, me, own, own_sem, rcv, rcv_sem, to):
        far = send(parts.at[(me + 2) % 4], rcv.at[0], own_sem.at[0], rcv_sem.at[0], to(s))
        near = send(parts.at[(me - s + 4) % 4], rcv.at[1], own_sem.at[1], rcv_sem.at[1], to(-s))
        return far, near

    def sum_relay(started, parts, me, own, own_sem, rcv, rcv_sem, to):
        started[0].wait_recv()
        own[...] = parts[(me + s + 4) % 4] + rcv[0]
        return started[1], send(own, rcv.at[2], own_sem.at[2], rcv_sem.at[2], to(s))

    def sum_end(started, parts, me, own, own_sem, rcv, rcv_sem, to):
        for copy in started:
            copy.wait_recv()
        return parts[me] + rcv[1] + rcv[2]

    def gather_start(slot, me, ssem, rsem, to):
        return [send(slot(me), slot(me), ssem.at[i], rsem.at[i], to(k)) for i, k in enumerate((s, -s))]

    def gather_relay(started, slot, me, ssem, rsem, to):
        here = slot((me - s + 4) % 4)
        return [started[1], send(here, here, ssem.at[2], rsem.at[2], to(s))]

    args = (psum, x, pcomb, s_xr, xrcv, r_xr, on_x)
    pfull[x] = sum_end(sum_relay(sum_start(*args), *args), *args)
    a_args = (lambda i: pfull.at[i], x, s_xa, r_xa, on_x)
    across = gather_start(*a_args)

    def rows8(k):
        return pl.ds(pl.multiple_of(((z + k) % NZ) * 8, 8), 8)

    first, rest = pl.ds(0, 2), pl.ds(2, 3)
    around = (4, 3, 5, 2, 6, 1, 7)

    def gram_z(part, n):
        return [
            send(
                gp.at[x, n, rows8(k), :], zrcv.at[k - 1, n],
                s_zr.at[part, k - 1], r_zr.at[part, k - 1], on_z(k),
            )
            for k in around
        ]

    def gram_y(part, n, before):
        for copy in before:
            copy.wait_recv()
        total = gp[x, n, rows8(0), :]
        for k in range(NZ - 1):
            total = total + zrcv[k, n]
        gz[n] = total
        return [
            send(gz.at[n], yrcv.at[k - 1, n], s_y.at[part, k - 1], r_y.at[part, k - 1], on_y(k))
            for k in (2, 1, 3)
        ]

    def gram_back_z(part, n):
        here = gfull.at[x, n, rows8(0), :]
        return [
            make(gown.at[n], here, s_gz.at[part, k - 1], r_gz.at[part, k - 1], on_z(k)) for k in around
        ]

    def gram_gather_z(part, n, before):
        for copy in before:
            copy.wait_recv()
        total = gz[n]
        for k in range(NY - 1):
            total = total + yrcv[k, n]
        gown[n] = total
        gfull[x, n, rows8(0), :] = total
        copies = gram_back_z(part, n)
        for copy in copies:
            copy.start()
        return copies

    w_rows = COLS // NZ

    def w_half(h):
        return pl.ds(h * COLS, COLS)

    def w_part(h, k):
        return pl.ds(pl.multiple_of(h * COLS + ((z + k) % NZ) * w_rows, 8), w_rows)

    def w_y(h):
        rows = w_half(h)
        return (
            make(wp.at[(y + 2) % NY, rows, :], wyrcv.at[0, rows, :], s_wy.at[h, 0], r_wy.at[h, 0], on_y(s)),
            make(wp.at[(y - s + NY) % NY, rows, :], wyrcv.at[1, rows, :], s_wy.at[h, 1], r_wy.at[h, 1], on_y(-s)),
            make(wcomb.at[rows, :], wyrcv.at[2, rows, :], s_wy.at[h, 2], r_wy.at[h, 2], on_y(s)),
        )

    def w_z(h):
        return [
            make(wy.at[w_part(h, k), :], wzrcv.at[h, k - 1], s_wz.at[h, k - 1], r_wz.at[h, k - 1], on_z(k))
            for k in around
        ]

    def w_back_z(h):
        here = wfull.at[y, w_part(h, 0), :]
        return [make(here, here, s_wza.at[h, k - 1], r_wza.at[h, k - 1], on_z(k)) for k in around]

    def w_back_y(h):
        here = wfull.at[y, w_half(h), :]
        other = wfull.at[(y - s + NY) % NY, w_half(h), :]
        return (
            make(here, here, s_wya.at[h, 0], r_wya.at[h, 0], on_y(s)),
            make(here, here, s_wya.at[h, 1], r_wya.at[h, 1], on_y(-s)),
            make(other, other, s_wya.at[h, 2], r_wya.at[h, 2], on_y(s)),
        )

    def w_stage(stage, h):
        rows = w_half(h)
        if stage == 1:
            _, _, relay = w_y(h)
            w_y(h)[0].wait_recv()
            wcomb[rows, :] = wp[(y + s + NY) % NY, rows, :] + wyrcv[0, rows, :]
            relay.start()
        if stage == 2:
            for copy in w_y(h)[1:]:
                copy.wait_recv()
            wy[rows, :] = wp[y, rows, :] + wyrcv[1, rows, :] + wyrcv[2, rows, :]
            for copy in w_z(h):
                copy.start()
        if stage == 3:
            for copy in w_z(h):
                copy.wait_recv()
            total = wy[w_part(h, 0), :]
            for k in range(NZ - 1):
                total = total + wzrcv[h, k]
            wfull[y, w_part(h, 0), :] = total
            for copy in w_back_z(h):
                copy.start()
        if stage == 4:
            for copy in w_back_z(h):
                copy.wait_recv()
            for copy in w_back_y(h)[:2]:
                copy.start()
        if stage == 5:
            w_back_y(h)[0].wait_recv()
            w_back_y(h)[2].start()
        if stage == 6:
            for copy in w_back_y(h)[1:]:
                copy.wait_recv()

    g = dot6(pfull[x], pfull[x], 0, 0)
    for h in range(2):
        gp[x, h] = g[h * 64 : (h + 1) * 64]
    g0 = gram_z(0, first)
    across[0].wait_recv()
    far = gather_relay(across, *a_args)[1]
    across[1].wait_recv()
    g = dot6(pfull[x + 1 - x // 3], pfull[x % 3], 0, 0)
    for h in range(2):
        gp[x, 2 + h] = g[h * 64 : (h + 1) * 64]
    between_two = (x + 1) % 2
    g = dot6(pfull[between_two + 2], pfull[between_two], 0, 0)
    for h in range(2):
        halves[h] = g[h * 64 : (h + 1) * 64]
    gp[x, 4] = halves[x // 2]
    g1 = gram_z(1, rest)
    g0 = gram_y(0, first, g0)
    far.wait_recv()
    cb.wait_recv()
    for n, k in enumerate((2, NY - s, NY + s, 0)):
        b = (y + k) % NY
        for h in range(2):
            wp[b, w_half(h), :] = dot3(b2[h], pfull[b], 1, 0)
            if n < 2:
                w_y(h)[n].start()
    g0 = gram_gather_z(0, first, g0)
    g1 = gram_y(1, rest, g1)
    for copy in g0:
        copy.wait_recv()

    def diagonals():
        here = gfull.at[x, first]
        return [make(here, here, s_gx.at[k + 2], r_gx.at[k + 2], on_x(k)) for k in (1, 3, 2)]

    def diagonal_from(chip):
        k = (x - chip + NX) % NX
        here = gfull.at[chip, first]
        return make(here, here, s_gx.at[k + 2], r_gx.at[k + 2], on_x(k))

    @pl.when(x == 0)
    def _():
        for copy in diagonals():
            copy.start()

    gram_gather_z(1, rest, g1)
    w_stage(1, 0)

    @pl.when(x != 0)
    def _():
        for copy in diagonals():
            copy.start()
        diagonal_from(0).wait_recv()

    def rest_x():
        here = gfull.at[x, rest]
        other = gfull.at[(x - s + NX) % NX, rest]
        return (
            make(here, here, s_gx.at[0], r_gx.at[0], on_x(s)),
            make(here, here, s_gx.at[1], r_gx.at[1], on_x(-s)),
            make(other, other, s_gx.at[2], r_gx.at[2], on_x(s)),
        )

    def rest_near():
        for copy in gram_back_z(1, rest):
            copy.wait_recv()
        for copy in rest_x()[:2]:
            copy.start()

    def rest_far():
        rest_x()[0].wait_recv()
        rest_x()[2].start()

    def rest_end():
        for chip in range(1, NX):

            @pl.when(x != chip)
            def _(chip=chip):
                diagonal_from(chip).wait_recv()

        for copy in rest_x()[1:]:
            copy.wait_recv()

    def let_go():
        for copy in pending:
            copy.wait_send()
        pending.clear()

    def stage(n, h):
        return functools.partial(w_stage, n, h)

    between = [
        [(2, stage(1, 1)), (2, rest_near), (5, rest_far), (6, stage(2, 0))],
        [(3, stage(3, 0)), (7, stage(3, 1))],
        [(4, stage(4, 0)), (7, stage(4, 1))],
        [(2, stage(5, 0)), (6, stage(5, 1))],
    ]

    def load(i, j):
        return jnp.concatenate([gfull[PLACE[(2 * i + h, j)]] for h in range(2)], axis=0)

    def lanes(b):
        return slice(b * BLK, (b + 1) * BLK)

    def half(i):
        return pl.ds(pl.multiple_of(i * COLS, 8), COLS)

    tril = lax.broadcasted_iota(jnp.int32, (BLK, BLK), 0) >= lax.broadcasted_iota(
        jnp.int32, (BLK, BLK), 1
    )
    def span(i, j):
        return slice(i * BLK, j * BLK)

    xinv[...] = jnp.zeros_like(xinv)
    mblk[...] = load(0, 0)
    for kb in range(4):
        here, below, done = span(kb, kb + 1), span(kb + 1, 4), span(0, kb + 1)
        invert_factor(mblk, iblk, prev, pan, between[kb])
        inv = jnp.where(tril, iblk[...], 0.0)
        xinv[here, here] = inv
        if kb == 0:
            w_stage(2, 1)
            rest_end()
            for i in range(1, 4):
                for j in range(i + 1):
                    afac[span(i, i + 1), span(j, j + 1)] = load(i, j)
        if kb < 3:
            panel = dot6(afac[below, here], inv, 1, 1)
            afac[below, here] = panel
            mblk[...] = afac[span(kb + 1, kb + 2), span(kb + 1, kb + 2)] - dot6(
                panel[:BLK], panel[:BLK], 1, 1
            )
            for j in range(kb + 1, 3):
                under, column = span(j + 1, 4), span(j, j + 1)
                at = (j - kb - 1) * BLK
                afac[under, column] = afac[under, column] - dot6(
                    panel[at + BLK :], panel[at : at + BLK], 1, 1
                )
                corner = span(j + 1, j + 2)
                afac[corner, corner] = afac[corner, corner] - dot6(
                    panel[at + BLK : at + 2 * BLK], panel[at + BLK : at + 2 * BLK], 1, 1
                )
        if kb > 0:
            xinv[here, span(0, kb)] = -dot3(inv, mixed[:, span(0, kb)], 1, 0)
        if kb < 3:
            mixed[:, done] = dot3(afac[span(kb + 1, kb + 2), done], xinv[done, done], 1, 0)
        if kb == 1:
            let_go()
    for h in range(2):
        w_stage(6, h)
    both = jnp.concatenate(
        [jnp.concatenate([pfull[b], wfull[b]], axis=0) for b in range(4)], axis=1
    )
    for kb in range(4):
        done = span(0, kb + 1)
        result = dot3(both[:, done], xinv[span(kb, kb + 1), done], 1, 1)
        qs[:, lanes(kb)] = result[:ROWS]
        cs[:, lanes(kb)] = result[ROWS:]
    ends = [
        send(qs, q_hbm.at[c], s_end.at[0], r_end.at[0], pair),
        make(cs.at[half(o), :], c_hbm.at[c], s_end.at[1], r_end.at[1], pair),
    ]
    stores = [
        pltpu.make_async_copy(qs, q_hbm.at[c], out_sem.at[0]),
        pltpu.make_async_copy(cs.at[half(c), :], c_hbm.at[c], out_sem.at[1]),
        pltpu.make_async_copy(sq, n_hbm.at[c, x], out_sem.at[2]),
    ]
    stores[0].start()
    ends[1].start()
    stores[1].start()
    sq[...] = jnp.sum(cs[...] * cs[...], axis=0, keepdims=True)
    stores[2].start()
    sums = [
        send(sq, n_hbm.at[c, x], s_n.at[i], r_n.at[i], to)
        for i, to in enumerate(
            [on_x(2), on_x(1), on_x(3)]
            + [(f, ((x + k) % NX) * 2 + o) for k in (2, 1, 3, 0)]
        )
    ]
    for copy in pending[:-len(sums)]:
        copy.wait_send()
    for copy in diagonals() + list(rest_x()) + gram_back_z(0, first) + gram_back_z(1, rest):
        copy.wait_send()
    for h in range(2):
        for copy in list(w_y(h)) + w_z(h) + w_back_z(h) + list(w_back_y(h)):
            copy.wait_send()
    for copy in ends + sums:
        copy.wait_recv()
    ends[1].wait_send()
    for copy in sums:
        copy.wait_send()
    for store in stores:
        store.wait()


def finish(mom_ref, grad_ref, q_ref, c_ref, n_ref, nm_ref, nb_ref, up_ref):
    q, coeffs = q_ref[0], c_ref[0]
    error = lax.dot_general(
        coeffs.astype(BF16), q.astype(BF16), (((1,), (1,)), ((), ())), preferred_element_type=F32
    )
    nm_ref[0] = mom_ref[0] + grad_ref[0].astype(F32) - 0.05 * error
    basis = coeffs * lax.rsqrt(n_ref[0, 0] + n_ref[0, 1] + n_ref[0, 2] + n_ref[0, 3] + 1e-06)
    nb_ref[0] = basis
    up_ref[0] = (math.sqrt(D * FF / RANK) * dot3(basis, q, 1, 1)).astype(BF16)


def on_device(momentum, grad, basis):
    vm = pltpu.VMEM
    chunk = (4, BLK, BLK)
    scratch = [
        vm((2, COLS, ROWS), F32), vm((2, COLS, ROWS), BF16), vm((2, COLS, RANK), F32),
        pltpu.SemaphoreType.DMA((4,)),
        vm((2, COLS, ROWS), F32), vm((COLS, ROWS), F32),
        vm(chunk, F32), vm(chunk, F32), vm(chunk, F32), vm(chunk, F32),
        vm((BLK, BLK), F32), vm((3, BLK, BLK), F32), vm(chunk, F32),
        vm((2, 64, BLK), F32),
        vm((4, 5, 64, BLK), F32), vm((7, 5, 8, BLK), F32), vm((5, 8, BLK), F32),
        vm((3, 5, 8, BLK), F32), vm((5, 8, BLK), F32), vm((4, 5, 64, BLK), F32),
        vm((4, 2 * COLS, BLK), F32), vm((2 * COLS, BLK), F32),
        vm((3, 2 * COLS, BLK), F32), vm((2 * COLS, BLK), F32),
        vm((2, 7, COLS // NZ, BLK), F32), vm((4, 2 * COLS, BLK), F32),
        vm((RANK, RANK), F32), vm((RANK, RANK), F32), vm((BLK, RANK), F32),
        *[vm((BLK, BLK), F32)] * 2, *[vm((NB, BLK), F32)] * 2,
        vm((ROWS, RANK), F32), vm((2 * COLS, RANK), F32),
        vm((1, RANK), F32),
        pltpu.SemaphoreType.DMA((3,)),
    ]
    for n in (2, 3, 3, (2, 7), (2, 3), 6, (2, 7), (2, 3), (2, 7), (2, 7), (2, 3), 2, 7):
        shape = n if isinstance(n, tuple) else (n,)
        scratch += [pltpu.SemaphoreType.DMA(shape), pltpu.SemaphoreType.DMA(shape)]
    hbm = pl.BlockSpec(memory_space=pl.ANY)
    momentum, grad = jnp.swapaxes(momentum, 1, 2), jnp.swapaxes(grad, 1, 2)
    q, coeffs, sums = pl.pallas_call(
        kernel,
        out_shape=(
            jax.ShapeDtypeStruct((2, ROWS, RANK), F32),
            jax.ShapeDtypeStruct((2, COLS, RANK), F32),
            jax.ShapeDtypeStruct((2, NX, 1, RANK), F32),
        ),
        in_specs=[hbm] * 3,
        out_specs=(hbm,) * 3,
        scratch_shapes=scratch,
        compiler_params=pltpu.CompilerParams(
            collective_id=0, has_side_effects=True, vmem_limit_bytes=58 * 2**20
        ),
    )(momentum, grad, basis)

    def one(*shape):
        return pl.BlockSpec((1, *shape), lambda i: (i,) + (0,) * len(shape))

    nm, nb, up = pl.pallas_call(
        finish,
        grid=(2,),
        out_shape=(
            jax.ShapeDtypeStruct((2, COLS, ROWS), F32),
            jax.ShapeDtypeStruct((2, COLS, RANK), F32),
            jax.ShapeDtypeStruct((2, COLS, ROWS), BF16),
        ),
        in_specs=[one(COLS, ROWS), one(COLS, ROWS), one(ROWS, RANK), one(COLS, RANK), one(NX, 1, RANK)],
        out_specs=(one(COLS, ROWS), one(COLS, RANK), one(COLS, ROWS)),
        compiler_params=pltpu.CompilerParams(vmem_limit_bytes=58 * 2**20),
    )(momentum, grad, q, coeffs, sums)
    return jnp.swapaxes(nm, 1, 2), nb, jnp.swapaxes(up, 1, 2)


def solution(mesh):
    in_specs = (P(None, "fsdp", "tensor"), P(None, "fsdp", "tensor"), P(None, "tensor", None))
    out_specs = (P(None, "fsdp", "tensor"), P(None, "tensor", None), P(None, "fsdp", "tensor"))
    return jax.shard_map(
        on_device, mesh=mesh, in_specs=in_specs, out_specs=out_specs, check_vma=False
    )
```

```python
import functools
import math

import jax
import jax.numpy as jnp
from jax import lax
from jax.experimental import pallas as pl
from jax.experimental.pallas import tpu as pltpu
from jax.sharding import PartitionSpec as P

D = 4096
FF = 1536
RANK = 512
NX, NY, NZ = 4, 4, 8
ROWS = 128
COLS = 192
BLK = 128
NB = 16
F32 = jnp.float32
BF16 = jnp.bfloat16
HIGHEST = lax.Precision.HIGHEST
MESH = pl.DeviceIdType.MESH

PLACE = {(2 * x + h, x): (x, h) for x in range(NX) for h in range(2)}
PLACE.update({(2 * (x + 1 - x // 3) + h, x % 3): (x, 2 + h) for x in range(NX) for h in range(2)})
PLACE.update({(2 * (2 + (x + 1) % 2) + x // 2, (x + 1) % 2): (x, 4) for x in range(NX)})


def dot6(a, b, ca, cb):
    return lax.dot_general(
        a, b, (((ca,), (cb,)), ((), ())), precision=HIGHEST, preferred_element_type=F32
    )


def split(a):
    hi = a.astype(BF16)
    return hi, (a - hi.astype(F32)).astype(BF16)


def dot3(a, b, ca, cb):
    dims = (((ca,), (cb,)), ((), ()))
    ah, al = split(a)
    bh, bl = split(b)
    one = functools.partial(lax.dot_general, dimension_numbers=dims, preferred_element_type=F32)
    return one(ah, bh) + (one(ah, bl) + one(al, bh))


def gram_long(a):
    hi = a.astype(BF16).astype(F32)
    rest = a - hi
    mid = rest.astype(BF16).astype(F32)
    low = rest - mid
    lhs = jnp.concatenate([hi, hi, hi, mid, mid, low], axis=0).astype(BF16)
    rhs = jnp.concatenate([hi, mid, low, hi, mid, hi], axis=0).astype(BF16)
    return lax.dot_general(lhs, rhs, (((0,), (0,)), ((), ())), preferred_element_type=F32)


def invert_factor(m_ref, out_ref, prev, pan, between):
    lane = lax.broadcasted_iota(jnp.int32, (NB, BLK), 1)
    sub = lax.broadcasted_iota(jnp.int32, (NB, BLK), 0)
    lane_all = lax.broadcasted_iota(jnp.int32, (BLK, BLK), 1)
    eye = lax.broadcasted_iota(jnp.int32, (BLK, BLK), 0) == lane_all
    diagonal = jnp.where(eye, m_ref[...], 0.0)
    scale_row = lax.rsqrt(jnp.sum(diagonal, axis=0, keepdims=True))
    scale_col = lax.rsqrt(jnp.sum(diagonal, axis=1, keepdims=True))
    scaled = m_ref[...] * scale_col * scale_row
    m_ref[...] = scaled
    pan[...] = scaled[:NB]
    prev[...] = jnp.zeros_like(prev)

    def columns(rows, rel):
        return [
            jnp.broadcast_to(
                jnp.sum(jnp.where(rel == j, rows, 0.0), axis=1, keepdims=True), (NB, BLK)
            )
            for j in range(NB)
        ]

    def step(b, carry):
        for at, call in between:
            pl.when(b == at)(call)
        r0 = pl.multiple_of(b * NB, NB)
        after = pl.multiple_of(jnp.minimum(r0 + NB, BLK - NB), NB)
        rel = lane - r0
        inside = jnp.logical_and(rel >= 0, rel < NB)
        rel_all = lane_all - r0
        inside_before = jnp.logical_and(rel_all >= -NB, rel_all < 0)

        m_ref[...] = jnp.where(inside_before, 0.0, m_ref[...]) - gram_long(prev[...])

        rows = pan[...]
        cols = jnp.stack(columns(rows, rel))
        full = jnp.where(inside, jnp.where(rel == sub, 1.0, 0.0), rows)
        lower = full
        scale = jnp.zeros((NB, BLK), F32)
        for p in range(0, NB, 2):
            u1, u2 = cols[0], cols[1]
            a, e, d = u1[p : p + 1], u2[p : p + 1], u2[p + 1 : p + 2]
            det = a * d - e * e
            inv = pl.reciprocal(det, approx=True)
            inv = inv * (2.0 - det * inv)
            v1, v2 = d * u1 - e * u2, a * u2 - e * u1
            ia = 1.0 / a
            under = sub > p + 1
            w1, w2 = v1 * inv, v2 * inv
            l1 = jnp.where(under, w1, jnp.where(sub == p + 1, e * ia, 0.0))
            l2 = jnp.where(under, w2, 0.0)
            lower = lower - (l1 * lower[p : p + 1] + l2 * lower[p + 1 : p + 2])
            scale = jnp.where(sub == p, lax.rsqrt(a), scale)
            scale = jnp.where(sub == p + 1, lax.rsqrt(det * ia), scale)
            w1 = jnp.where(sub == p, 1.0 - d * inv, jnp.where(sub == p + 1, e * inv, w1))
            w2 = jnp.where(sub == p, e * inv, jnp.where(sub == p + 1, 1.0 - a * inv, w2))
            if p + 2 < NB:
                rest = cols[2:]
                cols = rest - (w1[None] * rest[:, p : p + 1] + w2[None] * rest[:, p + 1 : p + 2])
            full = full - (w1 * full[p : p + 1] + w2 * full[p + 1 : p + 2])
        lower = lower * scale
        prev[...] = lower
        out_ref[pl.ds(r0, NB), :] = lower * scale_row

        rows = m_ref[pl.ds(after, NB), :]
        terms = [m * full[j : j + 1] for j, m in enumerate(columns(rows, rel))]
        while len(terms) > 1:
            terms = [terms[i] + terms[i + 1] for i in range(0, len(terms), 2)]
        pan[...] = jnp.where(inside, 0.0, rows) - terms[0]
        return carry

    lax.fori_loop(0, BLK // NB, step, 0)


def kernel(
    mom_hbm, grad_hbm, basis_hbm, q_hbm, c_hbm, n_hbm,
    mom_ref, grad_ref, basis_ref, in_sem, b2, bsend, pown, poth, prcv, psum, pcomb, xrcv, pfull, halves, gp, zrcv, gz, yrcv, gown, gfull, g10,
    wp, wyrcv, wy, wzrcv, wfull, afac, xinv, mixed, mblk, iblk, prev, pan, qs, cs, sq, out_sem,
    s_pair, r_pair, s_xr, r_xr, s_xa, r_xa, s_zr, r_zr, s_y, r_y, s_gx, r_gx, s_gz, r_gz,
    s_wy, r_wy, s_wz, r_wz, s_wza, r_wza, s_wya, r_wya, s_end, r_end, s_n, r_n,
):
    f = lax.axis_index("fsdp")
    t = lax.axis_index("tensor")
    z, y = f // NY, f % NY
    x, c = t // 2, t % 2
    o = 1 - c

    pair = (f, x * 2 + o)

    def on_x(k):
        return (f, ((x + k + NX) % NX) * 2 + c)

    def on_y(k):
        return (z * NY + (y + k + NY) % NY, t)

    def on_z(k):
        return (((z + k) % NZ) * NY + y, t)

    s = 1 - 2 * c

    pending = []

    def make(src, dst, ssem, rsem, to):
        return pltpu.make_async_remote_copy(
            src_ref=src, dst_ref=dst, send_sem=ssem, recv_sem=rsem,
            device_id=to, device_id_type=MESH,
        )

    def send(*args):
        copy = make(*args)
        copy.start()
        pending.append(copy)
        return copy

    loads = [
        pltpu.make_async_copy(src, dst, in_sem.at[i])
        for i, (src, dst) in enumerate(
            (
                (mom_hbm, mom_ref),
                (grad_hbm, grad_ref),
                (basis_hbm.at[o], basis_ref.at[o]),
                (basis_hbm.at[c], basis_ref.at[c]),
            )
        )
    ]
    for load in loads:
        load.start()
    barrier = pltpu.get_barrier_semaphore()
    peers = [pair] + [on_x(k) for k in range(1, NX)]
    peers += [(f, ((x + k) % NX) * 2 + o) for k in range(1, NX)]
    peers += [on_y(k) for k in range(1, NY)] + [on_z(k) for k in range(1, NZ)]
    for peer in peers:
        pl.semaphore_signal(barrier, inc=1, device_id=peer, device_id_type=MESH)

    for load in loads[:3]:
        load.wait()
    bsend[...] = mom_ref[o] + grad_ref[o].astype(F32)
    p = dot3(bsend[...], basis_ref[o], 0, 0)
    for b in range(4):
        poth[b] = p[:, b * BLK : (b + 1) * BLK]
    pl.semaphore_wait(barrier, len(peers))
    cp = send(poth, prcv, s_pair.at[0], r_pair.at[0], pair)
    cb = send(bsend, b2.at[c], s_pair.at[1], r_pair.at[1], pair)
    own = mom_ref[c] + grad_ref[c].astype(F32)
    b2[c] = own
    loads[3].wait()
    p = dot3(own, basis_ref[c], 0, 0)
    for b in range(4):
        pown[b] = p[:, b * BLK : (b + 1) * BLK]
    cp.wait_recv()
    for b in range(4):
        psum[b] = pown[b] + prcv[b]

    def sum_start(parts, me, own, own_sem, rcv, rcv_sem, to):
        far = send(parts.at[(me + 2) % 4], rcv.at[0], own_sem.at[0], rcv_sem.at[0], to(s))
        near = send(parts.at[(me - s + 4) % 4], rcv.at[1], own_sem.at[1], rcv_sem.at[1], to(-s))
        return far, near

    def sum_relay(started, parts, me, own, own_sem, rcv, rcv_sem, to):
        started[0].wait_recv()
        own[...] = parts[(me + s + 4) % 4] + rcv[0]
        return started[1], send(own, rcv.at[2], own_sem.at[2], rcv_sem.at[2], to(s))

    def sum_end(started, parts, me, own, own_sem, rcv, rcv_sem, to):
        for copy in started:
            copy.wait_recv()
        return parts[me] + rcv[1] + rcv[2]

    def gather_start(slot, me, ssem, rsem, to):
        return [send(slot(me), slot(me), ssem.at[i], rsem.at[i], to(k)) for i, k in enumerate((s, -s))]

    def gather_relay(started, slot, me, ssem, rsem, to):
        here = slot((me - s + 4) % 4)
        return [started[1], send(here, here, ssem.at[2], rsem.at[2], to(s))]

    args = (psum, x, pcomb, s_xr, xrcv, r_xr, on_x)
    pfull[x] = sum_end(sum_relay(sum_start(*args), *args), *args)
    a_args = (lambda i: pfull.at[i], x, s_xa, r_xa, on_x)
    across = gather_start(*a_args)

    def rows8(k):
        return pl.ds(pl.multiple_of(((z + k) % NZ) * 8, 8), 8)

    first, rest = pl.ds(0, 2), pl.ds(2, 3)
    around = (4, 3, 5, 2, 6, 1, 7)

    def gram_z(part, n):
        return [
            send(
                gp.at[x, n, rows8(k), :], zrcv.at[k - 1, n],
                s_zr.at[part, k - 1], r_zr.at[part, k - 1], on_z(k),
            )
            for k in around
        ]

    def gram_y(part, n, before):
        for copy in before:
            copy.wait_recv()
        total = gp[x, n, rows8(0), :]
        for k in range(NZ - 1):
            total = total + zrcv[k, n]
        gz[n] = total
        return [
            send(gz.at[n], yrcv.at[k - 1, n], s_y.at[part, k - 1], r_y.at[part, k - 1], on_y(k))
            for k in (2, 1, 3)
        ]

    def gram_back_z(part, n):
        here = gfull.at[x, n, rows8(0), :]
        return [
            make(gown.at[n], here, s_gz.at[part, k - 1], r_gz.at[part, k - 1], on_z(k)) for k in around
        ]

    def gram_gather_z(part, n, before):
        for copy in before:
            copy.wait_recv()
        total = gz[n]
        for k in range(NY - 1):
            total = total + yrcv[k, n]
        gown[n] = total
        gfull[x, n, rows8(0), :] = total
        copies = gram_back_z(part, n)
        for copy in copies:
            copy.start()
        return copies

    w_rows = COLS // NZ

    def w_half(h):
        return pl.ds(h * COLS, COLS)

    def w_part(h, k):
        return pl.ds(pl.multiple_of(h * COLS + ((z + k) % NZ) * w_rows, 8), w_rows)

    opposite_first = (2, 1, 3)

    def w_y(h):
        rows = w_half(h)
        return [
            make(
                wp.at[(y + k) % NY, rows, :], wyrcv.at[k - 1, rows, :],
                s_wy.at[h, k - 1], r_wy.at[h, k - 1], on_y(k),
            )
            for k in opposite_first
        ]

    def w_z(h):
        return [
            make(wy.at[w_part(h, k), :], wzrcv.at[h, k - 1], s_wz.at[h, k - 1], r_wz.at[h, k - 1], on_z(k))
            for k in around
        ]

    def w_back_z(h):
        here = wfull.at[y, w_part(h, 0), :]
        return [make(here, here, s_wza.at[h, k - 1], r_wza.at[h, k - 1], on_z(k)) for k in around]

    def w_back_y(h):
        here = wfull.at[y, w_half(h), :]
        return [
            make(here, here, s_wya.at[h, k - 1], r_wya.at[h, k - 1], on_y(k)) for k in opposite_first
        ]

    def w_to_z(h):
        rows = w_half(h)
        for copy in w_y(h):
            copy.wait_recv()
        wy[rows, :] = wp[y, rows, :] + wyrcv[0, rows, :] + wyrcv[1, rows, :] + wyrcv[2, rows, :]
        for copy in w_z(h):
            copy.start()

    def w_from_z(h):
        for copy in w_z(h):
            copy.wait_recv()
        total = wy[w_part(h, 0), :]
        for k in range(NZ - 1):
            total = total + wzrcv[h, k]
        wfull[y, w_part(h, 0), :] = total
        for copy in w_back_z(h):
            copy.start()

    def w_to_y(h):
        for copy in w_back_z(h):
            copy.wait_recv()
        for copy in w_back_y(h):
            copy.start()

    def w_end(h):
        for copy in w_back_y(h):
            copy.wait_recv()

    g = dot6(pfull[x], pfull[x], 0, 0)
    for h in range(2):
        gp[x, h] = g[h * 64 : (h + 1) * 64]
    g0 = gram_z(0, first)
    across[0].wait_recv()
    far = gather_relay(across, *a_args)[1]
    across[1].wait_recv()
    g = dot6(pfull[x + 1 - x // 3], pfull[x % 3], 0, 0)
    for h in range(2):
        gp[x, 2 + h] = g[h * 64 : (h + 1) * 64]
    between_two = (x + 1) % 2
    g = dot6(pfull[between_two + 2], pfull[between_two], 0, 0)
    for h in range(2):
        halves[h] = g[h * 64 : (h + 1) * 64]
    gp[x, 4] = halves[x // 2]
    g1 = gram_z(1, rest)
    g0 = gram_y(0, first, g0)
    far.wait_recv()
    cb.wait_recv()
    for n, k in enumerate((*opposite_first, 0)):
        b = (y + k) % NY
        for h in range(2):
            wp[b, w_half(h), :] = dot3(b2[h], pfull[b], 1, 0)
            if n < 3:
                w_y(h)[n].start()
    g0 = gram_gather_z(0, first, g0)
    g1 = gram_y(1, rest, g1)
    for copy in g0:
        copy.wait_recv()

    def diagonals():
        here = gfull.at[x, first]
        return [make(here, here, s_gx.at[k + 2], r_gx.at[k + 2], on_x(k)) for k in (1, 3, 2)]

    def diagonal_from(chip):
        k = (x - chip + NX) % NX
        here = gfull.at[chip, first]
        return make(here, here, s_gx.at[k + 2], r_gx.at[k + 2], on_x(k))

    @pl.when(x == 0)
    def _():
        for copy in diagonals():
            copy.start()

    gram_gather_z(1, rest, g1)
    w_to_z(0)

    @pl.when(x != 0)
    def _():
        for copy in diagonals():
            copy.start()
        diagonal_from(0).wait_recv()

    def span(i, j):
        return slice(i * BLK, j * BLK)

    def rest_x():
        here = gfull.at[x, rest]
        other = gfull.at[(x - s + NX) % NX, rest]
        return (
            make(here, here, s_gx.at[0], r_gx.at[0], on_x(s)),
            make(here, here, s_gx.at[1], r_gx.at[1], on_x(-s)),
            make(other, other, s_gx.at[2], r_gx.at[2], on_x(s)),
        )

    def early():
        here = gfull.at[0, pl.ds(2, 2)]
        return [make(here, g10, s_gx.at[k + 5], r_gx.at[k + 5], on_x(k)) for k in (1, 3, 2)]

    def rest_near():
        for copy in gram_back_z(1, rest):
            copy.wait_recv()

        @pl.when(x == 0)
        def _():
            for copy in early():
                copy.start()
            g10[...] = gfull[0, 2:4]

        for copy in rest_x()[:2]:
            copy.start()

    def rest_far():
        rest_x()[0].wait_recv()
        rest_x()[2].start()

    def diagonal_end(chip):
        @pl.when(x != chip)
        def _():
            diagonal_from(chip).wait_recv()

    def early_end():
        @pl.when(x != 0)
        def _():
            here = gfull.at[0, pl.ds(2, 2)]
            make(here, g10, s_gx.at[x + 5], r_gx.at[x + 5], on_x(x)).wait_recv()

    def rest_end():
        diagonal_end(2)
        diagonal_end(3)
        for copy in rest_x()[1:]:
            copy.wait_recv()
        for i in range(2, 4):
            for j in range(i + 1):
                afac[span(i, i + 1), span(j, j + 1)] = load(i, j)
        panel = dot6(afac[span(2, 4), span(0, 1)], xinv[span(0, 1), span(0, 1)], 1, 1)
        afac[span(2, 4), span(0, 1)] = panel
        afac[span(2, 4), span(1, 2)] = afac[span(2, 4), span(1, 2)] - dot6(
            panel, afac[span(1, 2), span(0, 1)], 1, 1
        )

    def let_go():
        for copy in pending:
            copy.wait_send()
        pending.clear()

    def call(f, h):
        return functools.partial(f, h)

    between = [
        [(2, call(w_to_z, 1)), (2, rest_near), (5, rest_far)],
        [(0, call(w_from_z, 0)), (4, call(w_from_z, 1)), (6, rest_end)],
        [(2, call(w_to_y, 0)), (6, call(w_to_y, 1))],
        [],
    ]

    def load(i, j):
        return jnp.concatenate([gfull[PLACE[(2 * i + h, j)]] for h in range(2)], axis=0)

    def lanes(b):
        return slice(b * BLK, (b + 1) * BLK)

    def half(i):
        return pl.ds(pl.multiple_of(i * COLS, 8), COLS)

    tril = lax.broadcasted_iota(jnp.int32, (BLK, BLK), 0) >= lax.broadcasted_iota(
        jnp.int32, (BLK, BLK), 1
    )
    xinv[...] = jnp.zeros_like(xinv)
    projected = jnp.concatenate([pfull[b] for b in range(4)], axis=1)
    mblk[...] = load(0, 0)
    for kb in range(4):
        here, below, done = span(kb, kb + 1), span(kb + 1, 4), span(0, kb + 1)
        invert_factor(mblk, iblk, prev, pan, between[kb])
        inv = jnp.where(tril, iblk[...], 0.0)
        xinv[here, here] = inv
        if kb == 0:
            early_end()
            diagonal_end(1)
            panel = dot6(g10[...].reshape(BLK, BLK), inv, 1, 1)
            afac[span(1, 2), here] = panel
            mblk[...] = load(1, 1) - dot6(panel, panel, 1, 1)
        if kb == 1:
            afac[below, here] = dot6(afac[below, here], inv, 1, 1)
            left = afac[below, done]
            mblk[...] = afac[span(2, 3), span(2, 3)] - dot6(left[:BLK], left[:BLK], 1, 1)
            under = afac[span(3, 4), span(2, 4)] - dot6(left[BLK:], left, 1, 1)
            afac[span(3, 4), span(2, 4)] = under
        if kb == 2:
            panel = dot6(afac[below, here], inv, 1, 1)
            afac[below, here] = panel
            mblk[...] = afac[below, below] - dot6(panel, panel, 1, 1)
        if kb > 0:
            xinv[here, span(0, kb)] = -dot3(inv, mixed[:, span(0, kb)], 1, 0)
        if kb < 3:
            mixed[:, done] = dot3(afac[span(kb + 1, kb + 2), done], xinv[done, done], 1, 0)
        qs[:, lanes(kb)] = dot3(projected[:, done], xinv[here, done], 1, 1)
        if kb == 1:
            let_go()
    ends = [
        send(qs, q_hbm.at[c], s_end.at[0], r_end.at[0], pair),
        make(cs.at[half(o), :], c_hbm.at[c], s_end.at[1], r_end.at[1], pair),
    ]
    stores = [
        pltpu.make_async_copy(qs, q_hbm.at[c], out_sem.at[0]),
        pltpu.make_async_copy(cs.at[half(c), :], c_hbm.at[c], out_sem.at[1]),
        pltpu.make_async_copy(sq, n_hbm.at[c, x], out_sem.at[2]),
    ]
    stores[0].start()
    for h in range(2):
        w_end(h)
        rows = w_half(h)
        w = jnp.concatenate([wfull[b, rows, :] for b in range(4)], axis=1)
        for kb in range(4):
            done = span(0, kb + 1)
            cs[rows, lanes(kb)] = dot3(w[:, done], xinv[span(kb, kb + 1), done], 1, 1)
    ends[1].start()
    stores[1].start()
    sq[...] = jnp.sum(cs[...] * cs[...], axis=0, keepdims=True)
    stores[2].start()
    sums = [
        send(sq, n_hbm.at[c, x], s_n.at[i], r_n.at[i], to)
        for i, to in enumerate(
            [on_x(2), on_x(1), on_x(3)]
            + [(f, ((x + k) % NX) * 2 + o) for k in (2, 1, 3, 0)]
        )
    ]
    for copy in pending[:-len(sums)]:
        copy.wait_send()
    @pl.when(x == 0)
    def _():
        for copy in early():
            copy.wait_send()

    for copy in diagonals() + list(rest_x()) + gram_back_z(0, first) + gram_back_z(1, rest):
        copy.wait_send()
    for h in range(2):
        for copy in list(w_y(h)) + w_z(h) + w_back_z(h) + list(w_back_y(h)):
            copy.wait_send()
    for copy in ends + sums:
        copy.wait_recv()
    ends[1].wait_send()
    for copy in sums:
        copy.wait_send()
    for store in stores:
        store.wait()


def finish(mom_ref, grad_ref, q_ref, c_ref, n_ref, nm_ref, nb_ref, up_ref):
    q, coeffs = q_ref[0], c_ref[0]
    error = lax.dot_general(
        coeffs.astype(BF16), q.astype(BF16), (((1,), (1,)), ((), ())), preferred_element_type=F32
    )
    nm_ref[0] = mom_ref[0] + grad_ref[0].astype(F32) - 0.05 * error
    basis = coeffs * lax.rsqrt(n_ref[0, 0] + n_ref[0, 1] + n_ref[0, 2] + n_ref[0, 3] + 1e-06)
    nb_ref[0] = basis
    up_ref[0] = (math.sqrt(D * FF / RANK) * dot3(basis, q, 1, 1)).astype(BF16)


def on_device(momentum, grad, basis):
    vm = pltpu.VMEM
    chunk = (4, BLK, BLK)
    scratch = [
        vm((2, COLS, ROWS), F32), vm((2, COLS, ROWS), BF16), vm((2, COLS, RANK), F32),
        pltpu.SemaphoreType.DMA((4,)),
        vm((2, COLS, ROWS), F32), vm((COLS, ROWS), F32),
        vm(chunk, F32), vm(chunk, F32), vm(chunk, F32), vm(chunk, F32),
        vm((BLK, BLK), F32), vm((3, BLK, BLK), F32), vm(chunk, F32),
        vm((2, 64, BLK), F32),
        vm((4, 5, 64, BLK), F32), vm((7, 5, 8, BLK), F32), vm((5, 8, BLK), F32),
        vm((3, 5, 8, BLK), F32), vm((5, 8, BLK), F32), vm((4, 5, 64, BLK), F32), vm((2, 64, BLK), F32),
        vm((4, 2 * COLS, BLK), F32),
        vm((3, 2 * COLS, BLK), F32), vm((2 * COLS, BLK), F32),
        vm((2, 7, COLS // NZ, BLK), F32), vm((4, 2 * COLS, BLK), F32),
        vm((RANK, RANK), F32), vm((RANK, RANK), F32), vm((BLK, RANK), F32),
        *[vm((BLK, BLK), F32)] * 2, *[vm((NB, BLK), F32)] * 2,
        vm((ROWS, RANK), F32), vm((2 * COLS, RANK), F32),
        vm((1, RANK), F32),
        pltpu.SemaphoreType.DMA((3,)),
    ]
    for n in (2, 3, 3, (2, 7), (2, 3), 9, (2, 7), (2, 3), (2, 7), (2, 7), (2, 3), 2, 7):
        shape = n if isinstance(n, tuple) else (n,)
        scratch += [pltpu.SemaphoreType.DMA(shape), pltpu.SemaphoreType.DMA(shape)]
    hbm = pl.BlockSpec(memory_space=pl.ANY)
    momentum, grad = jnp.swapaxes(momentum, 1, 2), jnp.swapaxes(grad, 1, 2)
    q, coeffs, sums = pl.pallas_call(
        kernel,
        out_shape=(
            jax.ShapeDtypeStruct((2, ROWS, RANK), F32),
            jax.ShapeDtypeStruct((2, COLS, RANK), F32),
            jax.ShapeDtypeStruct((2, NX, 1, RANK), F32),
        ),
        in_specs=[hbm] * 3,
        out_specs=(hbm,) * 3,
        scratch_shapes=scratch,
        compiler_params=pltpu.CompilerParams(
            collective_id=0, has_side_effects=True, vmem_limit_bytes=58 * 2**20
        ),
    )(momentum, grad, basis)

    def one(*shape):
        return pl.BlockSpec((1, *shape), lambda i: (i,) + (0,) * len(shape))

    nm, nb, up = pl.pallas_call(
        finish,
        grid=(2,),
        out_shape=(
            jax.ShapeDtypeStruct((2, COLS, ROWS), F32),
            jax.ShapeDtypeStruct((2, COLS, RANK), F32),
            jax.ShapeDtypeStruct((2, COLS, ROWS), BF16),
        ),
        in_specs=[one(COLS, ROWS), one(COLS, ROWS), one(ROWS, RANK), one(COLS, RANK), one(NX, 1, RANK)],
        out_specs=(one(COLS, ROWS), one(COLS, RANK), one(COLS, ROWS)),
        compiler_params=pltpu.CompilerParams(vmem_limit_bytes=58 * 2**20),
    )(momentum, grad, q, coeffs, sums)
    return jnp.swapaxes(nm, 1, 2), nb, jnp.swapaxes(up, 1, 2)


def solution(mesh):
    in_specs = (P(None, "fsdp", "tensor"), P(None, "fsdp", "tensor"), P(None, "tensor", None))
    out_specs = (P(None, "fsdp", "tensor"), P(None, "tensor", None), P(None, "fsdp", "tensor"))
    return jax.shard_map(
        on_device, mesh=mesh, in_specs=in_specs, out_specs=out_specs, check_vma=False
    )
```

```python
import functools
import math

import jax
import jax.numpy as jnp
from jax import lax
from jax.experimental import pallas as pl
from jax.experimental.pallas import tpu as pltpu
from jax.sharding import PartitionSpec as P

D = 4096
FF = 1536
RANK = 512
NX, NY, NZ = 4, 4, 8
ROWS = 128
COLS = 192
BLK = 128
NB = 16
F32 = jnp.float32
BF16 = jnp.bfloat16
HIGHEST = lax.Precision.HIGHEST
MESH = pl.DeviceIdType.MESH

PLACE = {(2 * x + h, x): (x, h) for x in range(NX) for h in range(2)}
PLACE.update({(2 * (x + 1 - x // 3) + h, x % 3): (x, 2 + h) for x in range(NX) for h in range(2)})
PLACE.update({(2 * (2 + (x + 1) % 2) + x // 2, (x + 1) % 2): (x, 4) for x in range(NX)})


def dot6(a, b, ca, cb):
    return lax.dot_general(
        a, b, (((ca,), (cb,)), ((), ())), precision=HIGHEST, preferred_element_type=F32
    )


def split(a):
    hi = a.astype(BF16)
    return hi, (a - hi.astype(F32)).astype(BF16)


def dot3(a, b, ca, cb):
    dims = (((ca,), (cb,)), ((), ()))
    ah, al = split(a)
    bh, bl = split(b)
    one = functools.partial(lax.dot_general, dimension_numbers=dims, preferred_element_type=F32)
    return one(ah, bh) + (one(ah, bl) + one(al, bh))


def gram_long(a):
    hi = a.astype(BF16).astype(F32)
    rest = a - hi
    mid = rest.astype(BF16).astype(F32)
    low = rest - mid
    lhs = jnp.concatenate([hi, hi, hi, mid, mid, low], axis=0).astype(BF16)
    rhs = jnp.concatenate([hi, mid, low, hi, mid, hi], axis=0).astype(BF16)
    return lax.dot_general(lhs, rhs, (((0,), (0,)), ((), ())), preferred_element_type=F32)


def invert_factor(m_ref, out_ref, prev, pan, between):
    lane = lax.broadcasted_iota(jnp.int32, (NB, BLK), 1)
    sub = lax.broadcasted_iota(jnp.int32, (NB, BLK), 0)
    lane_all = lax.broadcasted_iota(jnp.int32, (BLK, BLK), 1)
    eye = lax.broadcasted_iota(jnp.int32, (BLK, BLK), 0) == lane_all
    diagonal = jnp.where(eye, m_ref[...], 0.0)
    scale_row = lax.rsqrt(jnp.sum(diagonal, axis=0, keepdims=True))
    scale_col = lax.rsqrt(jnp.sum(diagonal, axis=1, keepdims=True))
    scaled = m_ref[...] * scale_col * scale_row
    m_ref[...] = scaled
    pan[...] = scaled[:NB]
    prev[...] = jnp.zeros_like(prev)

    def columns(rows, rel):
        return [
            jnp.broadcast_to(
                jnp.sum(jnp.where(rel == j, rows, 0.0), axis=1, keepdims=True), (NB, BLK)
            )
            for j in range(NB)
        ]

    def step(b, carry):
        for at, call in between:
            pl.when(b == at)(call)
        r0 = pl.multiple_of(b * NB, NB)
        after = pl.multiple_of(jnp.minimum(r0 + NB, BLK - NB), NB)
        rel = lane - r0
        inside = jnp.logical_and(rel >= 0, rel < NB)
        rel_all = lane_all - r0
        inside_before = jnp.logical_and(rel_all >= -NB, rel_all < 0)

        m_ref[...] = jnp.where(inside_before, 0.0, m_ref[...]) - gram_long(prev[...])

        rows = pan[...]
        cols = jnp.stack(columns(rows, rel))
        full = jnp.where(inside, jnp.where(rel == sub, 1.0, 0.0), rows)
        lower = full
        scale = jnp.zeros((NB, BLK), F32)
        for p in range(0, NB, 2):
            u1, u2 = cols[0], cols[1]
            a, e, d = u1[p : p + 1], u2[p : p + 1], u2[p + 1 : p + 2]
            det = a * d - e * e
            inv = pl.reciprocal(det, approx=True)
            inv = inv * (2.0 - det * inv)
            v1, v2 = d * u1 - e * u2, a * u2 - e * u1
            ia = 1.0 / a
            under = sub > p + 1
            w1, w2 = v1 * inv, v2 * inv
            l1 = jnp.where(under, w1, jnp.where(sub == p + 1, e * ia, 0.0))
            l2 = jnp.where(under, w2, 0.0)
            lower = lower - (l1 * lower[p : p + 1] + l2 * lower[p + 1 : p + 2])
            scale = jnp.where(sub == p, lax.rsqrt(a), scale)
            scale = jnp.where(sub == p + 1, lax.rsqrt(det * ia), scale)
            w1 = jnp.where(sub == p, 1.0 - d * inv, jnp.where(sub == p + 1, e * inv, w1))
            w2 = jnp.where(sub == p, e * inv, jnp.where(sub == p + 1, 1.0 - a * inv, w2))
            if p + 2 < NB:
                rest = cols[2:]
                cols = rest - (w1[None] * rest[:, p : p + 1] + w2[None] * rest[:, p + 1 : p + 2])
            full = full - (w1 * full[p : p + 1] + w2 * full[p + 1 : p + 2])
        lower = lower * scale
        prev[...] = lower
        out_ref[pl.ds(r0, NB), :] = lower * scale_row

        rows = m_ref[pl.ds(after, NB), :]
        terms = [m * full[j : j + 1] for j, m in enumerate(columns(rows, rel))]
        while len(terms) > 1:
            terms = [terms[i] + terms[i + 1] for i in range(0, len(terms), 2)]
        pan[...] = jnp.where(inside, 0.0, rows) - terms[0]
        return carry

    lax.fori_loop(0, BLK // NB, step, 0)


def kernel(
    mom_hbm, grad_hbm, basis_hbm, q_hbm, c_hbm, n_hbm,
    mom_ref, grad_ref, basis_ref, in_sem, b2, bsend, pown, poth, prcv, psum, pcomb, xrcv, pfull, halves, gp, zrcv, gz, yrcv, gown, gfull, g10,
    wp, wyrcv, wy, wzrcv, wfull, afac, xinv, mixed, mblk, iblk, prev, pan, qs, cs, sq, out_sem,
    s_pair, r_pair, s_xr, r_xr, s_xa, r_xa, s_zr, r_zr, s_y, r_y, s_gx, r_gx, s_gz, r_gz,
    s_wy, r_wy, s_wz, r_wz, s_wza, r_wza, s_wya, r_wya, s_end, r_end, s_n, r_n,
):
    f = lax.axis_index("fsdp")
    t = lax.axis_index("tensor")
    z, y = f // NY, f % NY
    x, c = t // 2, t % 2
    o = 1 - c

    pair = (f, x * 2 + o)

    def on_x(k):
        return (f, ((x + k + NX) % NX) * 2 + c)

    def on_y(k):
        return (z * NY + (y + k + NY) % NY, t)

    def on_z(k):
        return (((z + k) % NZ) * NY + y, t)

    s = 1 - 2 * c

    pending = []

    def make(src, dst, ssem, rsem, to):
        return pltpu.make_async_remote_copy(
            src_ref=src, dst_ref=dst, send_sem=ssem, recv_sem=rsem,
            device_id=to, device_id_type=MESH,
        )

    def send(*args):
        copy = make(*args)
        copy.start()
        pending.append(copy)
        return copy

    loads = [
        pltpu.make_async_copy(src, dst, in_sem.at[i])
        for i, (src, dst) in enumerate(
            (
                (mom_hbm, mom_ref),
                (grad_hbm, grad_ref),
                (basis_hbm.at[o], basis_ref.at[o]),
                (basis_hbm.at[c], basis_ref.at[c]),
            )
        )
    ]
    for load in loads:
        load.start()
    barrier = pltpu.get_barrier_semaphore()
    peers = [pair] + [on_x(k) for k in range(1, NX)]
    peers += [(f, ((x + k) % NX) * 2 + o) for k in range(1, NX)]
    peers += [on_y(k) for k in range(1, NY)] + [on_z(k) for k in range(1, NZ)]
    for peer in peers:
        pl.semaphore_signal(barrier, inc=1, device_id=peer, device_id_type=MESH)

    for load in loads[:3]:
        load.wait()
    bsend[...] = mom_ref[o] + grad_ref[o].astype(F32)
    p = dot3(bsend[...], basis_ref[o], 0, 0)
    for b in range(4):
        poth[b] = p[:, b * BLK : (b + 1) * BLK]
    pl.semaphore_wait(barrier, len(peers))
    cp = send(poth, prcv, s_pair.at[0], r_pair.at[0], pair)
    cb = send(bsend, b2.at[c], s_pair.at[1], r_pair.at[1], pair)
    own = mom_ref[c] + grad_ref[c].astype(F32)
    b2[c] = own
    loads[3].wait()
    p = dot3(own, basis_ref[c], 0, 0)
    for b in range(4):
        pown[b] = p[:, b * BLK : (b + 1) * BLK]
    cp.wait_recv()
    for b in range(4):
        psum[b] = pown[b] + prcv[b]

    def sum_start(parts, me, own, own_sem, rcv, rcv_sem, to):
        far = send(parts.at[(me + 2) % 4], rcv.at[0], own_sem.at[0], rcv_sem.at[0], to(s))
        near = send(parts.at[(me - s + 4) % 4], rcv.at[1], own_sem.at[1], rcv_sem.at[1], to(-s))
        return far, near

    def sum_relay(started, parts, me, own, own_sem, rcv, rcv_sem, to):
        started[0].wait_recv()
        own[...] = parts[(me + s + 4) % 4] + rcv[0]
        return started[1], send(own, rcv.at[2], own_sem.at[2], rcv_sem.at[2], to(s))

    def sum_end(started, parts, me, own, own_sem, rcv, rcv_sem, to):
        for copy in started:
            copy.wait_recv()
        return parts[me] + rcv[1] + rcv[2]

    def gather_start(slot, me, ssem, rsem, to):
        return [send(slot(me), slot(me), ssem.at[i], rsem.at[i], to(k)) for i, k in enumerate((s, -s))]

    def gather_relay(started, slot, me, ssem, rsem, to):
        here = slot((me - s + 4) % 4)
        return [started[1], send(here, here, ssem.at[2], rsem.at[2], to(s))]

    args = (psum, x, pcomb, s_xr, xrcv, r_xr, on_x)
    pfull[x] = sum_end(sum_relay(sum_start(*args), *args), *args)
    a_args = (lambda i: pfull.at[i], x, s_xa, r_xa, on_x)
    across = gather_start(*a_args)

    def rows8(k):
        return pl.ds(pl.multiple_of(((z + k) % NZ) * 8, 8), 8)

    first, rest = pl.ds(0, 2), pl.ds(2, 3)
    around = (4, 3, 5, 2, 6, 1, 7)

    def gram_z(part, n):
        return [
            send(
                gp.at[x, n, rows8(k), :], zrcv.at[k - 1, n],
                s_zr.at[part, k - 1], r_zr.at[part, k - 1], on_z(k),
            )
            for k in around
        ]

    def gram_y(part, n, before):
        for copy in before:
            copy.wait_recv()
        total = gp[x, n, rows8(0), :]
        for k in range(NZ - 1):
            total = total + zrcv[k, n]
        gz[n] = total
        return [
            send(gz.at[n], yrcv.at[k - 1, n], s_y.at[part, k - 1], r_y.at[part, k - 1], on_y(k))
            for k in (2, 1, 3)
        ]

    def gram_back_z(part, n):
        here = gfull.at[x, n, rows8(0), :]
        return [
            make(gown.at[n], here, s_gz.at[part, k - 1], r_gz.at[part, k - 1], on_z(k)) for k in around
        ]

    def gram_gather_z(part, n, before):
        for copy in before:
            copy.wait_recv()
        total = gz[n]
        for k in range(NY - 1):
            total = total + yrcv[k, n]
        gown[n] = total
        gfull[x, n, rows8(0), :] = total
        copies = gram_back_z(part, n)
        for copy in copies:
            copy.start()
        return copies

    w_rows = COLS // NZ

    def w_half(h):
        return pl.ds(h * COLS, COLS)

    def w_part(h, k):
        return pl.ds(pl.multiple_of(h * COLS + ((z + k) % NZ) * w_rows, 8), w_rows)

    opposite_first = (2, 1, 3)

    def w_y(h):
        rows = w_half(h)
        return [
            make(
                wp.at[(y + k) % NY, rows, :], wyrcv.at[k - 1, rows, :],
                s_wy.at[h, k - 1], r_wy.at[h, k - 1], on_y(k),
            )
            for k in opposite_first
        ]

    def w_z(h):
        return [
            make(wy.at[w_part(h, k), :], wzrcv.at[h, k - 1], s_wz.at[h, k - 1], r_wz.at[h, k - 1], on_z(k))
            for k in around
        ]

    def w_back_z(h):
        here = wfull.at[y, w_part(h, 0), :]
        return [make(here, here, s_wza.at[h, k - 1], r_wza.at[h, k - 1], on_z(k)) for k in around]

    def w_back_y(h):
        here = wfull.at[y, w_half(h), :]
        return [
            make(here, here, s_wya.at[h, k - 1], r_wya.at[h, k - 1], on_y(k)) for k in opposite_first
        ]

    def w_to_z(h):
        rows = w_half(h)
        for copy in w_y(h):
            copy.wait_recv()
        wy[rows, :] = wp[y, rows, :] + wyrcv[0, rows, :] + wyrcv[1, rows, :] + wyrcv[2, rows, :]
        for copy in w_z(h):
            copy.start()

    def w_from_z(h):
        for copy in w_z(h):
            copy.wait_recv()
        total = wy[w_part(h, 0), :]
        for k in range(NZ - 1):
            total = total + wzrcv[h, k]
        wfull[y, w_part(h, 0), :] = total
        for copy in w_back_z(h):
            copy.start()

    def w_to_y(h):
        for copy in w_back_z(h):
            copy.wait_recv()
        for copy in w_back_y(h):
            copy.start()

    def w_end(h):
        for copy in w_back_y(h):
            copy.wait_recv()

    g = dot6(pfull[x], pfull[x], 0, 0)
    for h in range(2):
        gp[x, h] = g[h * 64 : (h + 1) * 64]
    g0 = gram_z(0, first)
    across[0].wait_recv()
    far = gather_relay(across, *a_args)[1]
    across[1].wait_recv()
    g = dot6(pfull[x + 1 - x // 3], pfull[x % 3], 0, 0)
    for h in range(2):
        gp[x, 2 + h] = g[h * 64 : (h + 1) * 64]
    between_two = (x + 1) % 2
    g = dot6(pfull[between_two + 2], pfull[between_two], 0, 0)
    for h in range(2):
        halves[h] = g[h * 64 : (h + 1) * 64]
    gp[x, 4] = halves[x // 2]
    g1 = gram_z(1, rest)
    g0 = gram_y(0, first, g0)
    far.wait_recv()
    cb.wait_recv()
    for n, k in enumerate((*opposite_first, 0)):
        b = (y + k) % NY
        for h in range(2):
            wp[b, w_half(h), :] = dot3(b2[h], pfull[b], 1, 0)
            if n < 3:
                w_y(h)[n].start()
    g0 = gram_gather_z(0, first, g0)
    g1 = gram_y(1, rest, g1)
    for copy in g0:
        copy.wait_recv()

    def diagonals():
        here = gfull.at[x, first]
        return [make(here, here, s_gx.at[k + 2], r_gx.at[k + 2], on_x(k)) for k in (1, 3, 2)]

    def diagonal_from(chip):
        k = (x - chip + NX) % NX
        here = gfull.at[chip, first]
        return make(here, here, s_gx.at[k + 2], r_gx.at[k + 2], on_x(k))

    @pl.when(x == 0)
    def _():
        for copy in diagonals():
            copy.start()

    gram_gather_z(1, rest, g1)

    @pl.when(x != 0)
    def _():
        for copy in diagonals():
            copy.start()
        diagonal_from(0).wait_recv()

    def span(i, j):
        return slice(i * BLK, j * BLK)

    def rest_x():
        here = gfull.at[x, rest]
        other = gfull.at[(x - s + NX) % NX, rest]
        return (
            make(here, here, s_gx.at[0], r_gx.at[0], on_x(s)),
            make(here, here, s_gx.at[1], r_gx.at[1], on_x(-s)),
            make(other, other, s_gx.at[2], r_gx.at[2], on_x(s)),
        )

    def early():
        here = gfull.at[0, pl.ds(2, 2)]
        return [make(here, g10, s_gx.at[k + 5], r_gx.at[k + 5], on_x(k)) for k in (1, 3, 2)]

    def rest_near():
        for copy in gram_back_z(1, rest):
            copy.wait_recv()

        @pl.when(x == 0)
        def _():
            for copy in early():
                copy.start()
            g10[...] = gfull[0, 2:4]

        for copy in rest_x()[:2]:
            copy.start()

    def rest_far():
        rest_x()[0].wait_recv()
        rest_x()[2].start()

    def diagonal_end(chip):
        @pl.when(x != chip)
        def _():
            diagonal_from(chip).wait_recv()

    def early_end():
        @pl.when(x != 0)
        def _():
            here = gfull.at[0, pl.ds(2, 2)]
            make(here, g10, s_gx.at[x + 5], r_gx.at[x + 5], on_x(x)).wait_recv()

    def rest_end():
        diagonal_end(2)
        diagonal_end(3)
        for copy in rest_x()[1:]:
            copy.wait_recv()
        for i in range(2, 4):
            for j in range(i + 1):
                afac[span(i, i + 1), span(j, j + 1)] = load(i, j)
        panel = dot6(afac[span(2, 4), span(0, 1)], xinv[span(0, 1), span(0, 1)], 1, 1)
        afac[span(2, 4), span(0, 1)] = panel
        afac[span(2, 4), span(1, 2)] = afac[span(2, 4), span(1, 2)] - dot6(
            panel, afac[span(1, 2), span(0, 1)], 1, 1
        )

    def let_go():
        for copy in pending:
            copy.wait_send()
        pending.clear()

    def call(f, h):
        return functools.partial(f, h)

    between = [
        [(2, call(w_to_z, 0)), (4, rest_near), (5, call(w_to_z, 1)), (7, rest_far)],
        [(2, call(w_from_z, 0)), (5, call(w_from_z, 1)), (7, rest_end)],
        [(3, call(w_to_y, 0)), (6, call(w_to_y, 1))],
        [],
    ]

    def load(i, j):
        return jnp.concatenate([gfull[PLACE[(2 * i + h, j)]] for h in range(2)], axis=0)

    def lanes(b):
        return slice(b * BLK, (b + 1) * BLK)

    def half(i):
        return pl.ds(pl.multiple_of(i * COLS, 8), COLS)

    tril = lax.broadcasted_iota(jnp.int32, (BLK, BLK), 0) >= lax.broadcasted_iota(
        jnp.int32, (BLK, BLK), 1
    )
    xinv[...] = jnp.zeros_like(xinv)
    projected = jnp.concatenate([pfull[b] for b in range(4)], axis=1)
    mblk[...] = load(0, 0)
    for kb in range(4):
        here, below, done = span(kb, kb + 1), span(kb + 1, 4), span(0, kb + 1)
        invert_factor(mblk, iblk, prev, pan, between[kb])
        inv = jnp.where(tril, iblk[...], 0.0)
        xinv[here, here] = inv
        if kb == 0:
            early_end()
            diagonal_end(1)
            panel = dot6(g10[...].reshape(BLK, BLK), inv, 1, 1)
            afac[span(1, 2), here] = panel
            mblk[...] = load(1, 1) - dot6(panel, panel, 1, 1)
        if kb == 1:
            afac[below, here] = dot6(afac[below, here], inv, 1, 1)
            left = afac[below, done]
            mblk[...] = afac[span(2, 3), span(2, 3)] - dot6(left[:BLK], left[:BLK], 1, 1)
            under = afac[span(3, 4), span(2, 4)] - dot6(left[BLK:], left, 1, 1)
            afac[span(3, 4), span(2, 4)] = under
        if kb == 2:
            panel = dot6(afac[below, here], inv, 1, 1)
            afac[below, here] = panel
            mblk[...] = afac[below, below] - dot6(panel, panel, 1, 1)
        if kb > 0:
            xinv[here, span(0, kb)] = -dot3(inv, mixed[:, span(0, kb)], 1, 0)
        if kb < 3:
            mixed[:, done] = dot3(afac[span(kb + 1, kb + 2), done], xinv[done, done], 1, 0)
        qs[:, lanes(kb)] = dot3(projected[:, done], xinv[here, done], 1, 1)
        if kb == 1:
            let_go()
    ends = [
        send(qs, q_hbm.at[c], s_end.at[0], r_end.at[0], pair),
        make(cs.at[half(o), :], c_hbm.at[c], s_end.at[1], r_end.at[1], pair),
    ]
    stores = [
        pltpu.make_async_copy(qs, q_hbm.at[c], out_sem.at[0]),
        pltpu.make_async_copy(cs.at[half(c), :], c_hbm.at[c], out_sem.at[1]),
        pltpu.make_async_copy(sq, n_hbm.at[c, x], out_sem.at[2]),
    ]
    stores[0].start()
    for h in range(2):
        w_end(h)
        rows = w_half(h)
        w = jnp.concatenate([wfull[b, rows, :] for b in range(4)], axis=1)
        for kb in range(4):
            done = span(0, kb + 1)
            cs[rows, lanes(kb)] = dot3(w[:, done], xinv[span(kb, kb + 1), done], 1, 1)
    ends[1].start()
    stores[1].start()
    sq[...] = jnp.sum(cs[...] * cs[...], axis=0, keepdims=True)
    stores[2].start()
    sums = [
        send(sq, n_hbm.at[c, x], s_n.at[i], r_n.at[i], to)
        for i, to in enumerate(
            [on_x(2), on_x(1), on_x(3)]
            + [(f, ((x + k) % NX) * 2 + o) for k in (2, 1, 3, 0)]
        )
    ]
    for copy in pending[:-len(sums)]:
        copy.wait_send()
    @pl.when(x == 0)
    def _():
        for copy in early():
            copy.wait_send()

    for copy in diagonals() + list(rest_x()) + gram_back_z(0, first) + gram_back_z(1, rest):
        copy.wait_send()
    for h in range(2):
        for copy in list(w_y(h)) + w_z(h) + w_back_z(h) + list(w_back_y(h)):
            copy.wait_send()
    for copy in ends + sums:
        copy.wait_recv()
    ends[1].wait_send()
    for copy in sums:
        copy.wait_send()
    for store in stores:
        store.wait()


def finish(mom_ref, grad_ref, q_ref, c_ref, n_ref, nm_ref, nb_ref, up_ref):
    q, coeffs = q_ref[0], c_ref[0]
    error = lax.dot_general(
        coeffs.astype(BF16), q.astype(BF16), (((1,), (1,)), ((), ())), preferred_element_type=F32
    )
    nm_ref[0] = mom_ref[0] + grad_ref[0].astype(F32) - 0.05 * error
    basis = coeffs * lax.rsqrt(n_ref[0, 0] + n_ref[0, 1] + n_ref[0, 2] + n_ref[0, 3] + 1e-06)
    nb_ref[0] = basis
    up_ref[0] = (math.sqrt(D * FF / RANK) * dot3(basis, q, 1, 1)).astype(BF16)


def on_device(momentum, grad, basis):
    vm = pltpu.VMEM
    chunk = (4, BLK, BLK)
    scratch = [
        vm((2, COLS, ROWS), F32), vm((2, COLS, ROWS), BF16), vm((2, COLS, RANK), F32),
        pltpu.SemaphoreType.DMA((4,)),
        vm((2, COLS, ROWS), F32), vm((COLS, ROWS), F32),
        vm(chunk, F32), vm(chunk, F32), vm(chunk, F32), vm(chunk, F32),
        vm((BLK, BLK), F32), vm((3, BLK, BLK), F32), vm(chunk, F32),
        vm((2, 64, BLK), F32),
        vm((4, 5, 64, BLK), F32), vm((7, 5, 8, BLK), F32), vm((5, 8, BLK), F32),
        vm((3, 5, 8, BLK), F32), vm((5, 8, BLK), F32), vm((4, 5, 64, BLK), F32), vm((2, 64, BLK), F32),
        vm((4, 2 * COLS, BLK), F32),
        vm((3, 2 * COLS, BLK), F32), vm((2 * COLS, BLK), F32),
        vm((2, 7, COLS // NZ, BLK), F32), vm((4, 2 * COLS, BLK), F32),
        vm((RANK, RANK), F32), vm((RANK, RANK), F32), vm((BLK, RANK), F32),
        *[vm((BLK, BLK), F32)] * 2, *[vm((NB, BLK), F32)] * 2,
        vm((ROWS, RANK), F32), vm((2 * COLS, RANK), F32),
        vm((1, RANK), F32),
        pltpu.SemaphoreType.DMA((3,)),
    ]
    for n in (2, 3, 3, (2, 7), (2, 3), 9, (2, 7), (2, 3), (2, 7), (2, 7), (2, 3), 2, 7):
        shape = n if isinstance(n, tuple) else (n,)
        scratch += [pltpu.SemaphoreType.DMA(shape), pltpu.SemaphoreType.DMA(shape)]
    hbm = pl.BlockSpec(memory_space=pl.ANY)
    momentum, grad = jnp.swapaxes(momentum, 1, 2), jnp.swapaxes(grad, 1, 2)
    q, coeffs, sums = pl.pallas_call(
        kernel,
        out_shape=(
            jax.ShapeDtypeStruct((2, ROWS, RANK), F32),
            jax.ShapeDtypeStruct((2, COLS, RANK), F32),
            jax.ShapeDtypeStruct((2, NX, 1, RANK), F32),
        ),
        in_specs=[hbm] * 3,
        out_specs=(hbm,) * 3,
        scratch_shapes=scratch,
        compiler_params=pltpu.CompilerParams(
            collective_id=0, has_side_effects=True, vmem_limit_bytes=58 * 2**20
        ),
    )(momentum, grad, basis)

    def one(*shape):
        return pl.BlockSpec((1, *shape), lambda i: (i,) + (0,) * len(shape))

    nm, nb, up = pl.pallas_call(
        finish,
        grid=(2,),
        out_shape=(
            jax.ShapeDtypeStruct((2, COLS, ROWS), F32),
            jax.ShapeDtypeStruct((2, COLS, RANK), F32),
            jax.ShapeDtypeStruct((2, COLS, ROWS), BF16),
        ),
        in_specs=[one(COLS, ROWS), one(COLS, ROWS), one(ROWS, RANK), one(COLS, RANK), one(NX, 1, RANK)],
        out_specs=(one(COLS, ROWS), one(COLS, RANK), one(COLS, ROWS)),
        compiler_params=pltpu.CompilerParams(vmem_limit_bytes=58 * 2**20),
    )(momentum, grad, q, coeffs, sums)
    return jnp.swapaxes(nm, 1, 2), nb, jnp.swapaxes(up, 1, 2)


def solution(mesh):
    in_specs = (P(None, "fsdp", "tensor"), P(None, "fsdp", "tensor"), P(None, "tensor", None))
    out_specs = (P(None, "fsdp", "tensor"), P(None, "tensor", None), P(None, "fsdp", "tensor"))
    return jax.shard_map(
        on_device, mesh=mesh, in_specs=in_specs, out_specs=out_specs, check_vma=False
    )
```

```python
import functools
import math

import jax
import jax.numpy as jnp
from jax import lax
from jax.experimental import pallas as pl
from jax.experimental.pallas import tpu as pltpu
from jax.sharding import PartitionSpec as P

D = 4096
FF = 1536
RANK = 512
NX, NY, NZ = 4, 4, 8
ROWS = 128
COLS = 192
BLK = 128
NB = 16
F32 = jnp.float32
BF16 = jnp.bfloat16
HIGHEST = lax.Precision.HIGHEST
MESH = pl.DeviceIdType.MESH

PLACE = {(2 * x + h, x): (x, h) for x in range(NX) for h in range(2)}
PLACE.update({(2 * (x + 1 - x // 3) + h, x % 3): (x, 2 + h) for x in range(NX) for h in range(2)})
PLACE.update({(2 * (2 + (x + 1) % 2) + x // 2, (x + 1) % 2): (x, 4) for x in range(NX)})


def dot6(a, b, ca, cb):
    return lax.dot_general(
        a, b, (((ca,), (cb,)), ((), ())), precision=HIGHEST, preferred_element_type=F32
    )


def split(a):
    hi = a.astype(BF16)
    return hi, (a - hi.astype(F32)).astype(BF16)


def dot3(a, b, ca, cb):
    dims = (((ca,), (cb,)), ((), ()))
    ah, al = split(a)
    bh, bl = split(b)
    one = functools.partial(lax.dot_general, dimension_numbers=dims, preferred_element_type=F32)
    return one(ah, bh) + (one(ah, bl) + one(al, bh))


def dot_long(a, b):
    def pieces(v):
        hi = v.astype(BF16).astype(F32)
        rest = v - hi
        mid = rest.astype(BF16).astype(F32)
        return hi, mid, rest - mid

    a0, a1, a2 = pieces(a)
    b0, b1, b2 = pieces(b)
    lhs = jnp.concatenate([a0, a0, a0, a1, a1, a2], axis=0).astype(BF16)
    rhs = jnp.concatenate([b0, b1, b2, b0, b1, b0], axis=0).astype(BF16)
    return lax.dot_general(lhs, rhs, (((0,), (0,)), ((), ())), preferred_element_type=F32)


def flat(a):
    return a.reshape(NB, BLK)


def tall(a):
    return a.reshape(NB // 8, 8, BLK)


def at_row(v, p):
    return jnp.broadcast_to(v[p // 8, p % 8 : p % 8 + 1, :], (8, BLK))


def at_rows(v, p):
    return jnp.broadcast_to(
        v[:, p // 8 : p // 8 + 1, p % 8 : p % 8 + 1, :], (v.shape[0], 1, 8, BLK)
    )


def at_lane(v, j):
    return tall(jnp.broadcast_to(flat(v)[:, j : j + 1], (NB, BLK)))


def rolled(v, shift):
    return tall(pltpu.roll(flat(v), shift, 1))


def invert_factor(m_ref, out_ref, pan, prev, between):
    shape = (NB // 8, 8, BLK)
    lane = lax.broadcasted_iota(jnp.int32, shape, 2)
    sub = lax.broadcasted_iota(jnp.int32, shape, 0) * 8 + lax.broadcasted_iota(jnp.int32, shape, 1)
    row_all = lax.broadcasted_iota(jnp.int32, (BLK, BLK), 0)
    lane_all = lax.broadcasted_iota(jnp.int32, (BLK, BLK), 1)
    block = m_ref[...]
    diagonal = jnp.where(row_all == lane_all, block, 0.0)
    scale_row = lax.rsqrt(jnp.sum(diagonal, axis=0, keepdims=True))
    scale_col = lax.rsqrt(jnp.sum(diagonal, axis=1, keepdims=True))
    scaled = pltpu.roll(block * scale_col * scale_row, NB, 1)
    m_ref[...] = scaled
    pan[...] = tall(scaled[:NB])
    prev[...] = jnp.zeros_like(prev)
    steps = BLK // NB
    inside = lane < NB

    def step(b, carry):
        for at, call in between:
            pl.when(b == at)(call)
        r0 = pl.multiple_of(b * NB, NB)
        after = pl.multiple_of(jnp.minimum(r0 + NB, BLK - NB), NB)
        was = lane_all < jnp.where(b > 0, NB, 0)
        update = dot_long(prev[0], prev[1])
        m_ref[...] = pltpu.roll(jnp.where(was, 0.0, m_ref[...]) - update, BLK - NB, 1)

        rows = pan[...]
        cols = jnp.stack([at_lane(rows, NB + j) for j in range(NB)])
        full = jnp.where(inside, jnp.where(lane == sub, 1.0, 0.0), rolled(rows, BLK - NB))
        lower = full
        scale = jnp.zeros(shape, F32)
        for p in range(0, NB, 2):
            u1, u2 = cols[0], cols[1]
            a, e, d = at_row(u1, p), at_row(u2, p), at_row(u2, p + 1)
            det = a * d - e * e
            inv = pl.reciprocal(det, approx=True)
            inv = inv * (2.0 - det * inv)
            v1, v2 = d * u1 - e * u2, a * u2 - e * u1
            root = lax.rsqrt(a)
            ia = root * root
            under = sub > p + 1
            w1, w2 = v1 * inv, v2 * inv
            pivots1 = jnp.where(sub == p, 1.0 - d * inv, jnp.where(sub == p + 1, e * inv, w1))
            pivots2 = jnp.where(sub == p, e * inv, jnp.where(sub == p + 1, 1.0 - a * inv, w2))
            if p + 2 < NB:
                rest = cols[2:]
                cols = rest - (pivots1[None] * at_rows(rest, p) + pivots2[None] * at_rows(rest, p + 1))
            full = full - (pivots1 * at_row(full, p) + pivots2 * at_row(full, p + 1))
            l1 = jnp.where(under, w1, jnp.where(sub == p + 1, e * ia, 0.0))
            l2 = jnp.where(under, w2, 0.0)
            lower = lower - (l1 * at_row(lower, p) + l2 * at_row(lower, p + 1))
            scale = jnp.where(sub == p, root, scale)
            scale = jnp.where(sub == p + 1, lax.rsqrt(det * ia), scale)
        lower = flat(lower * scale)
        unturned = pltpu.roll(lower, r0, 1)
        prev[0] = unturned
        prev[1] = lower
        out_ref[pl.ds(r0, NB), :] = unturned

        old = tall(m_ref[pl.ds(after, NB), :])
        terms = [at_lane(old, j) * at_row(full, j) for j in range(NB)]
        while len(terms) > 1:
            terms = [terms[i] + terms[i + 1] for i in range(0, len(terms), 2)]
        pan[...] = jnp.where(inside, 0.0, old) - terms[0]
        return carry

    lax.fori_loop(0, steps, step, 0)
    out_ref[...] = jnp.where(row_all >= lane_all, out_ref[...] * scale_row, 0.0)


def kernel(
    mom_hbm, grad_hbm, basis_hbm, q_hbm, c_hbm, n_hbm,
    mom_ref, grad_ref, basis_ref, in_sem, b2, bsend, pown, poth, prcv, psum, pcomb, xrcv, pfull, halves, gp, zrcv, gz, yrcv, gown, gfull, g10,
    wp, wyrcv, wy, wzrcv, wfull, afac, xinv, mixed, mblk, iblk, prev, pan, qs, cs, sq, out_sem,
    s_pair, r_pair, s_xr, r_xr, s_xa, r_xa, s_zr, r_zr, s_y, r_y, s_gx, r_gx, s_gz, r_gz,
    s_wy, r_wy, s_wz, r_wz, s_wza, r_wza, s_wya, r_wya, s_end, r_end, s_n, r_n,
):
    f = lax.axis_index("fsdp")
    t = lax.axis_index("tensor")
    z, y = f // NY, f % NY
    x, c = t // 2, t % 2
    o = 1 - c

    pair = (f, x * 2 + o)

    def on_x(k):
        return (f, ((x + k + NX) % NX) * 2 + c)

    def on_y(k):
        return (z * NY + (y + k + NY) % NY, t)

    def on_z(k):
        return (((z + k) % NZ) * NY + y, t)

    s = 1 - 2 * c

    pending = []

    def make(src, dst, ssem, rsem, to):
        return pltpu.make_async_remote_copy(
            src_ref=src, dst_ref=dst, send_sem=ssem, recv_sem=rsem,
            device_id=to, device_id_type=MESH,
        )

    def send(*args):
        copy = make(*args)
        copy.start()
        pending.append(copy)
        return copy

    loads = [
        pltpu.make_async_copy(src, dst, in_sem.at[i])
        for i, (src, dst) in enumerate(
            (
                (mom_hbm, mom_ref),
                (grad_hbm, grad_ref),
                (basis_hbm.at[o], basis_ref.at[o]),
                (basis_hbm.at[c], basis_ref.at[c]),
            )
        )
    ]
    for load in loads:
        load.start()
    barrier = pltpu.get_barrier_semaphore()
    peers = [pair] + [on_x(k) for k in range(1, NX)]
    peers += [(f, ((x + k) % NX) * 2 + o) for k in range(1, NX)]
    peers += [on_y(k) for k in range(1, NY)] + [on_z(k) for k in range(1, NZ)]
    for peer in peers:
        pl.semaphore_signal(barrier, inc=1, device_id=peer, device_id_type=MESH)

    for load in loads[:3]:
        load.wait()
    bsend[...] = mom_ref[o] + grad_ref[o].astype(F32)
    p = dot3(bsend[...], basis_ref[o], 0, 0)
    for b in range(4):
        poth[b] = p[:, b * BLK : (b + 1) * BLK]
    pl.semaphore_wait(barrier, len(peers))
    cp = send(poth, prcv, s_pair.at[0], r_pair.at[0], pair)
    cb = send(bsend, b2.at[c], s_pair.at[1], r_pair.at[1], pair)
    own = mom_ref[c] + grad_ref[c].astype(F32)
    b2[c] = own
    loads[3].wait()
    p = dot3(own, basis_ref[c], 0, 0)
    for b in range(4):
        pown[b] = p[:, b * BLK : (b + 1) * BLK]
    cp.wait_recv()
    for b in range(4):
        psum[b] = pown[b] + prcv[b]

    def sum_start(parts, me, own, own_sem, rcv, rcv_sem, to):
        far = send(parts.at[(me + 2) % 4], rcv.at[0], own_sem.at[0], rcv_sem.at[0], to(s))
        near = send(parts.at[(me - s + 4) % 4], rcv.at[1], own_sem.at[1], rcv_sem.at[1], to(-s))
        return far, near

    def sum_relay(started, parts, me, own, own_sem, rcv, rcv_sem, to):
        started[0].wait_recv()
        own[...] = parts[(me + s + 4) % 4] + rcv[0]
        return started[1], send(own, rcv.at[2], own_sem.at[2], rcv_sem.at[2], to(s))

    def sum_end(started, parts, me, own, own_sem, rcv, rcv_sem, to):
        for copy in started:
            copy.wait_recv()
        return parts[me] + rcv[1] + rcv[2]

    def gather_start(slot, me, ssem, rsem, to):
        return [send(slot(me), slot(me), ssem.at[i], rsem.at[i], to(k)) for i, k in enumerate((s, -s))]

    def gather_relay(started, slot, me, ssem, rsem, to):
        here = slot((me - s + 4) % 4)
        return [started[1], send(here, here, ssem.at[2], rsem.at[2], to(s))]

    args = (psum, x, pcomb, s_xr, xrcv, r_xr, on_x)
    pfull[x] = sum_end(sum_relay(sum_start(*args), *args), *args)
    a_args = (lambda i: pfull.at[i], x, s_xa, r_xa, on_x)
    across = gather_start(*a_args)

    def rows8(k):
        return pl.ds(pl.multiple_of(((z + k) % NZ) * 8, 8), 8)

    first, rest = pl.ds(0, 2), pl.ds(2, 3)
    around = (4, 3, 5, 2, 6, 1, 7)

    def gram_z(part, n):
        return [
            send(
                gp.at[x, n, rows8(k), :], zrcv.at[k - 1, n],
                s_zr.at[part, k - 1], r_zr.at[part, k - 1], on_z(k),
            )
            for k in around
        ]

    def gram_y(part, n, before):
        for copy in before:
            copy.wait_recv()
        total = gp[x, n, rows8(0), :]
        for k in range(NZ - 1):
            total = total + zrcv[k, n]
        gz[n] = total
        return [
            send(gz.at[n], yrcv.at[k - 1, n], s_y.at[part, k - 1], r_y.at[part, k - 1], on_y(k))
            for k in (2, 1, 3)
        ]

    def gram_back_z(part, n):
        here = gfull.at[x, n, rows8(0), :]
        return [
            make(gown.at[n], here, s_gz.at[part, k - 1], r_gz.at[part, k - 1], on_z(k)) for k in around
        ]

    def gram_gather_z(part, n, before):
        for copy in before:
            copy.wait_recv()
        total = gz[n]
        for k in range(NY - 1):
            total = total + yrcv[k, n]
        gown[n] = total
        gfull[x, n, rows8(0), :] = total
        copies = gram_back_z(part, n)
        for copy in copies:
            copy.start()
        return copies

    w_rows = COLS // NZ

    def w_half(h):
        return pl.ds(h * COLS, COLS)

    def w_part(h, k):
        return pl.ds(pl.multiple_of(h * COLS + ((z + k) % NZ) * w_rows, 8), w_rows)

    opposite_first = (2, 1, 3)

    def w_y(h):
        rows = w_half(h)
        return [
            make(
                wp.at[(y + k) % NY, rows, :], wyrcv.at[k - 1, rows, :],
                s_wy.at[h, k - 1], r_wy.at[h, k - 1], on_y(k),
            )
            for k in opposite_first
        ]

    def w_z(h):
        return [
            make(wy.at[w_part(h, k), :], wzrcv.at[h, k - 1], s_wz.at[h, k - 1], r_wz.at[h, k - 1], on_z(k))
            for k in around
        ]

    def w_back_z(h):
        here = wfull.at[y, w_part(h, 0), :]
        return [make(here, here, s_wza.at[h, k - 1], r_wza.at[h, k - 1], on_z(k)) for k in around]

    def w_back_y(h):
        here = wfull.at[y, w_half(h), :]
        return [
            make(here, here, s_wya.at[h, k - 1], r_wya.at[h, k - 1], on_y(k)) for k in opposite_first
        ]

    def w_to_z(h):
        rows = w_half(h)
        for copy in w_y(h):
            copy.wait_recv()
        wy[rows, :] = wp[y, rows, :] + wyrcv[0, rows, :] + wyrcv[1, rows, :] + wyrcv[2, rows, :]
        for copy in w_z(h):
            copy.start()

    def w_from_z(h):
        for copy in w_z(h):
            copy.wait_recv()
        total = wy[w_part(h, 0), :]
        for k in range(NZ - 1):
            total = total + wzrcv[h, k]
        wfull[y, w_part(h, 0), :] = total
        for copy in w_back_z(h):
            copy.start()

    def w_to_y(h):
        for copy in w_back_z(h):
            copy.wait_recv()
        for copy in w_back_y(h):
            copy.start()

    def w_end(h):
        for copy in w_back_y(h):
            copy.wait_recv()

    g = dot6(pfull[x], pfull[x], 0, 0)
    for h in range(2):
        gp[x, h] = g[h * 64 : (h + 1) * 64]
    g0 = gram_z(0, first)
    across[0].wait_recv()
    far = gather_relay(across, *a_args)[1]
    across[1].wait_recv()
    g = dot6(pfull[x + 1 - x // 3], pfull[x % 3], 0, 0)
    for h in range(2):
        gp[x, 2 + h] = g[h * 64 : (h + 1) * 64]
    between_two = (x + 1) % 2
    g = dot6(pfull[between_two + 2], pfull[between_two], 0, 0)
    for h in range(2):
        halves[h] = g[h * 64 : (h + 1) * 64]
    gp[x, 4] = halves[x // 2]
    g1 = gram_z(1, rest)
    g0 = gram_y(0, first, g0)
    far.wait_recv()
    cb.wait_recv()
    for n, k in enumerate((*opposite_first, 0)):
        b = (y + k) % NY
        for h in range(2):
            wp[b, w_half(h), :] = dot3(b2[h], pfull[b], 1, 0)
            if n < 3:
                w_y(h)[n].start()
    g0 = gram_gather_z(0, first, g0)
    g1 = gram_y(1, rest, g1)
    for copy in g0:
        copy.wait_recv()

    def diagonals():
        here = gfull.at[x, first]
        return [make(here, here, s_gx.at[k + 2], r_gx.at[k + 2], on_x(k)) for k in (1, 3, 2)]

    def diagonal_from(chip):
        k = (x - chip + NX) % NX
        here = gfull.at[chip, first]
        return make(here, here, s_gx.at[k + 2], r_gx.at[k + 2], on_x(k))

    @pl.when(x == 0)
    def _():
        for copy in diagonals():
            copy.start()

    gram_gather_z(1, rest, g1)

    @pl.when(x != 0)
    def _():
        for copy in diagonals():
            copy.start()
        diagonal_from(0).wait_recv()

    def span(i, j):
        return slice(i * BLK, j * BLK)

    def rest_x():
        here = gfull.at[x, rest]
        other = gfull.at[(x - s + NX) % NX, rest]
        return (
            make(here, here, s_gx.at[0], r_gx.at[0], on_x(s)),
            make(here, here, s_gx.at[1], r_gx.at[1], on_x(-s)),
            make(other, other, s_gx.at[2], r_gx.at[2], on_x(s)),
        )

    def early():
        here = gfull.at[0, pl.ds(2, 2)]
        return [make(here, g10, s_gx.at[k + 5], r_gx.at[k + 5], on_x(k)) for k in (1, 3, 2)]

    def rest_near():
        for copy in gram_back_z(1, rest):
            copy.wait_recv()

        @pl.when(x == 0)
        def _():
            for copy in early():
                copy.start()
            g10[...] = gfull[0, 2:4]

        for copy in rest_x()[:2]:
            copy.start()

    def rest_far():
        rest_x()[0].wait_recv()
        rest_x()[2].start()

    def diagonal_end(chip):
        @pl.when(x != chip)
        def _():
            diagonal_from(chip).wait_recv()

    def early_end():
        @pl.when(x != 0)
        def _():
            here = gfull.at[0, pl.ds(2, 2)]
            make(here, g10, s_gx.at[x + 5], r_gx.at[x + 5], on_x(x)).wait_recv()

    def rest_end():
        diagonal_end(2)
        diagonal_end(3)
        for copy in rest_x()[1:]:
            copy.wait_recv()
        for i in range(2, 4):
            for j in range(i + 1):
                afac[span(i, i + 1), span(j, j + 1)] = load(i, j)
        panel = dot6(afac[span(2, 4), span(0, 1)], xinv[span(0, 1), span(0, 1)], 1, 1)
        afac[span(2, 4), span(0, 1)] = panel
        afac[span(2, 4), span(1, 2)] = afac[span(2, 4), span(1, 2)] - dot6(
            panel, afac[span(1, 2), span(0, 1)], 1, 1
        )

    def let_go():
        for copy in pending:
            copy.wait_send()
        pending.clear()

    def call(f, h):
        return functools.partial(f, h)

    between = [
        [(2, call(w_to_z, 0)), (4, rest_near), (5, call(w_to_z, 1)), (7, rest_far)],
        [(2, call(w_from_z, 0)), (5, call(w_from_z, 1)), (7, rest_end)],
        [(3, call(w_to_y, 0)), (6, call(w_to_y, 1))],
        [],
    ]

    def load(i, j):
        return jnp.concatenate([gfull[PLACE[(2 * i + h, j)]] for h in range(2)], axis=0)

    def lanes(b):
        return slice(b * BLK, (b + 1) * BLK)

    def half(i):
        return pl.ds(pl.multiple_of(i * COLS, 8), COLS)

    tril = lax.broadcasted_iota(jnp.int32, (BLK, BLK), 0) >= lax.broadcasted_iota(
        jnp.int32, (BLK, BLK), 1
    )
    xinv[...] = jnp.zeros_like(xinv)
    projected = jnp.concatenate([pfull[b] for b in range(4)], axis=1)
    mblk[...] = load(0, 0)
    for kb in range(4):
        here, below, done = span(kb, kb + 1), span(kb + 1, 4), span(0, kb + 1)
        invert_factor(mblk, iblk, pan, prev, between[kb])
        inv = jnp.where(tril, iblk[...], 0.0)
        xinv[here, here] = inv
        if kb == 0:
            early_end()
            diagonal_end(1)
            panel = dot6(g10[...].reshape(BLK, BLK), inv, 1, 1)
            afac[span(1, 2), here] = panel
            mblk[...] = load(1, 1) - dot6(panel, panel, 1, 1)
        if kb == 1:
            afac[below, here] = dot6(afac[below, here], inv, 1, 1)
            left = afac[below, done]
            mblk[...] = afac[span(2, 3), span(2, 3)] - dot6(left[:BLK], left[:BLK], 1, 1)
            under = afac[span(3, 4), span(2, 4)] - dot6(left[BLK:], left, 1, 1)
            afac[span(3, 4), span(2, 4)] = under
        if kb == 2:
            panel = dot6(afac[below, here], inv, 1, 1)
            afac[below, here] = panel
            mblk[...] = afac[below, below] - dot6(panel, panel, 1, 1)
        if kb > 0:
            xinv[here, span(0, kb)] = -dot3(inv, mixed[:, span(0, kb)], 1, 0)
        if kb < 3:
            mixed[:, done] = dot3(afac[span(kb + 1, kb + 2), done], xinv[done, done], 1, 0)
        qs[:, lanes(kb)] = dot3(projected[:, done], xinv[here, done], 1, 1)
        if kb == 1:
            let_go()
    ends = [
        send(qs, q_hbm.at[c], s_end.at[0], r_end.at[0], pair),
        make(cs.at[half(o), :], c_hbm.at[c], s_end.at[1], r_end.at[1], pair),
    ]
    stores = [
        pltpu.make_async_copy(qs, q_hbm.at[c], out_sem.at[0]),
        pltpu.make_async_copy(cs.at[half(c), :], c_hbm.at[c], out_sem.at[1]),
        pltpu.make_async_copy(sq, n_hbm.at[c, x], out_sem.at[2]),
    ]
    stores[0].start()
    for h in range(2):
        w_end(h)
        rows = w_half(h)
        w = jnp.concatenate([wfull[b, rows, :] for b in range(4)], axis=1)
        for kb in range(4):
            done = span(0, kb + 1)
            cs[rows, lanes(kb)] = dot3(w[:, done], xinv[span(kb, kb + 1), done], 1, 1)
    ends[1].start()
    stores[1].start()
    sq[...] = jnp.sum(cs[...] * cs[...], axis=0, keepdims=True)
    stores[2].start()
    sums = [
        send(sq, n_hbm.at[c, x], s_n.at[i], r_n.at[i], to)
        for i, to in enumerate(
            [on_x(2), on_x(1), on_x(3)]
            + [(f, ((x + k) % NX) * 2 + o) for k in (2, 1, 3, 0)]
        )
    ]
    for copy in pending[:-len(sums)]:
        copy.wait_send()
    @pl.when(x == 0)
    def _():
        for copy in early():
            copy.wait_send()

    for copy in diagonals() + list(rest_x()) + gram_back_z(0, first) + gram_back_z(1, rest):
        copy.wait_send()
    for h in range(2):
        for copy in list(w_y(h)) + w_z(h) + w_back_z(h) + list(w_back_y(h)):
            copy.wait_send()
    for copy in ends + sums:
        copy.wait_recv()
    ends[1].wait_send()
    for copy in sums:
        copy.wait_send()
    for store in stores:
        store.wait()


def finish(mom_ref, grad_ref, q_ref, c_ref, n_ref, nm_ref, nb_ref, up_ref):
    q, coeffs = q_ref[0], c_ref[0]
    error = lax.dot_general(
        coeffs.astype(BF16), q.astype(BF16), (((1,), (1,)), ((), ())), preferred_element_type=F32
    )
    nm_ref[0] = mom_ref[0] + grad_ref[0].astype(F32) - 0.05 * error
    basis = coeffs * lax.rsqrt(n_ref[0, 0] + n_ref[0, 1] + n_ref[0, 2] + n_ref[0, 3] + 1e-06)
    nb_ref[0] = basis
    up_ref[0] = (math.sqrt(D * FF / RANK) * dot3(basis, q, 1, 1)).astype(BF16)


def on_device(momentum, grad, basis):
    vm = pltpu.VMEM
    chunk = (4, BLK, BLK)
    scratch = [
        vm((2, COLS, ROWS), F32), vm((2, COLS, ROWS), BF16), vm((2, COLS, RANK), F32),
        pltpu.SemaphoreType.DMA((4,)),
        vm((2, COLS, ROWS), F32), vm((COLS, ROWS), F32),
        vm(chunk, F32), vm(chunk, F32), vm(chunk, F32), vm(chunk, F32),
        vm((BLK, BLK), F32), vm((3, BLK, BLK), F32), vm(chunk, F32),
        vm((2, 64, BLK), F32),
        vm((4, 5, 64, BLK), F32), vm((7, 5, 8, BLK), F32), vm((5, 8, BLK), F32),
        vm((3, 5, 8, BLK), F32), vm((5, 8, BLK), F32), vm((4, 5, 64, BLK), F32), vm((2, 64, BLK), F32),
        vm((4, 2 * COLS, BLK), F32),
        vm((3, 2 * COLS, BLK), F32), vm((2 * COLS, BLK), F32),
        vm((2, 7, COLS // NZ, BLK), F32), vm((4, 2 * COLS, BLK), F32),
        vm((RANK, RANK), F32), vm((RANK, RANK), F32), vm((BLK, RANK), F32),
        *[vm((BLK, BLK), F32)] * 2, vm((2, NB, BLK), F32), vm((NB // 8, 8, BLK), F32),
        vm((ROWS, RANK), F32), vm((2 * COLS, RANK), F32),
        vm((1, RANK), F32),
        pltpu.SemaphoreType.DMA((3,)),
    ]
    for n in (2, 3, 3, (2, 7), (2, 3), 9, (2, 7), (2, 3), (2, 7), (2, 7), (2, 3), 2, 7):
        shape = n if isinstance(n, tuple) else (n,)
        scratch += [pltpu.SemaphoreType.DMA(shape), pltpu.SemaphoreType.DMA(shape)]
    hbm = pl.BlockSpec(memory_space=pl.ANY)
    momentum, grad = jnp.swapaxes(momentum, 1, 2), jnp.swapaxes(grad, 1, 2)
    q, coeffs, sums = pl.pallas_call(
        kernel,
        out_shape=(
            jax.ShapeDtypeStruct((2, ROWS, RANK), F32),
            jax.ShapeDtypeStruct((2, COLS, RANK), F32),
            jax.ShapeDtypeStruct((2, NX, 1, RANK), F32),
        ),
        in_specs=[hbm] * 3,
        out_specs=(hbm,) * 3,
        scratch_shapes=scratch,
        compiler_params=pltpu.CompilerParams(
            collective_id=0, has_side_effects=True, vmem_limit_bytes=58 * 2**20
        ),
    )(momentum, grad, basis)

    def one(*shape):
        return pl.BlockSpec((1, *shape), lambda i: (i,) + (0,) * len(shape))

    nm, nb, up = pl.pallas_call(
        finish,
        grid=(2,),
        out_shape=(
            jax.ShapeDtypeStruct((2, COLS, ROWS), F32),
            jax.ShapeDtypeStruct((2, COLS, RANK), F32),
            jax.ShapeDtypeStruct((2, COLS, ROWS), BF16),
        ),
        in_specs=[one(COLS, ROWS), one(COLS, ROWS), one(ROWS, RANK), one(COLS, RANK), one(NX, 1, RANK)],
        out_specs=(one(COLS, ROWS), one(COLS, RANK), one(COLS, ROWS)),
        compiler_params=pltpu.CompilerParams(vmem_limit_bytes=58 * 2**20),
    )(momentum, grad, q, coeffs, sums)
    return jnp.swapaxes(nm, 1, 2), nb, jnp.swapaxes(up, 1, 2)


def solution(mesh):
    in_specs = (P(None, "fsdp", "tensor"), P(None, "fsdp", "tensor"), P(None, "tensor", None))
    out_specs = (P(None, "fsdp", "tensor"), P(None, "tensor", None), P(None, "fsdp", "tensor"))
    return jax.shard_map(
        on_device, mesh=mesh, in_specs=in_specs, out_specs=out_specs, check_vma=False
    )
```

```python
import functools
import math

import jax
import jax.numpy as jnp
from jax import lax
from jax.experimental import pallas as pl
from jax.experimental.pallas import tpu as pltpu
from jax.sharding import PartitionSpec as P

D = 4096
FF = 1536
RANK = 512
NX, NY, NZ = 4, 4, 8
ROWS = 128
COLS = 192
BLK = 128
NB = 16
F32 = jnp.float32
BF16 = jnp.bfloat16
HIGHEST = lax.Precision.HIGHEST
MESH = pl.DeviceIdType.MESH

PLACE = {(2 * x + h, x): (x, h) for x in range(NX) for h in range(2)}
PLACE.update({(2 * (x + 1 - x // 3) + h, x % 3): (x, 2 + h) for x in range(NX) for h in range(2)})
PLACE.update({(2 * (2 + (x + 1) % 2) + x // 2, (x + 1) % 2): (x, 4) for x in range(NX)})


def dot6(a, b, ca, cb):
    return lax.dot_general(
        a, b, (((ca,), (cb,)), ((), ())), precision=HIGHEST, preferred_element_type=F32
    )


def split(a):
    hi = a.astype(BF16)
    return hi, (a - hi.astype(F32)).astype(BF16)


def dot3(a, b, ca, cb):
    dims = (((ca,), (cb,)), ((), ()))
    ah, al = split(a)
    bh, bl = split(b)
    one = functools.partial(lax.dot_general, dimension_numbers=dims, preferred_element_type=F32)
    return one(ah, bh) + (one(ah, bl) + one(al, bh))


def gram_long(a):
    hi = a.astype(BF16).astype(F32)
    rest = a - hi
    mid = rest.astype(BF16).astype(F32)
    low = rest - mid
    lhs = jnp.concatenate([hi, hi, hi, mid, mid, low], axis=0).astype(BF16)
    rhs = jnp.concatenate([hi, mid, low, hi, mid, hi], axis=0).astype(BF16)
    return lax.dot_general(lhs, rhs, (((0,), (0,)), ((), ())), preferred_element_type=F32)


def invert_factor(m_ref, out_ref, between):
    lane = lax.broadcasted_iota(jnp.int32, (NB, BLK), 1)
    sub = lax.broadcasted_iota(jnp.int32, (NB, BLK), 0)
    lane_all = lax.broadcasted_iota(jnp.int32, (BLK, BLK), 1)
    eye = lax.broadcasted_iota(jnp.int32, (BLK, BLK), 0) == lane_all
    diagonal = jnp.where(eye, m_ref[...], 0.0)
    scale_row = lax.rsqrt(jnp.sum(diagonal, axis=0, keepdims=True))
    scale_col = lax.rsqrt(jnp.sum(diagonal, axis=1, keepdims=True))
    scaled = m_ref[...] * scale_col * scale_row
    m_ref[...] = scaled

    def columns(rows, rel):
        return [
            jnp.broadcast_to(
                jnp.sum(jnp.where(rel == j, rows, 0.0), axis=1, keepdims=True), (NB, BLK)
            )
            for j in range(NB)
        ]

    def step(b, carry):
        rows, previous = carry
        r0 = pl.multiple_of(b * NB, NB)
        after = pl.multiple_of(jnp.minimum(r0 + NB, BLK - NB), NB)
        rel = lane - r0
        inside = jnp.logical_and(rel >= 0, rel < NB)
        rel_all = lane_all - r0
        inside_before = jnp.logical_and(rel_all >= -NB, rel_all < 0)

        m_ref[...] = jnp.where(inside_before, 0.0, m_ref[...]) - gram_long(previous)

        cols = jnp.stack(columns(rows, rel))
        full = jnp.where(inside, jnp.where(rel == sub, 1.0, 0.0), rows)
        lower = full
        scale = jnp.zeros((NB, BLK), F32)
        for p in range(0, NB, 2):
            u1, u2 = cols[0], cols[1]
            a, e, d = u1[p : p + 1], u2[p : p + 1], u2[p + 1 : p + 2]
            det = a * d - e * e
            inv = pl.reciprocal(det, approx=True)
            inv = inv * (2.0 - det * inv)
            v1, v2 = d * u1 - e * u2, a * u2 - e * u1
            ia = 1.0 / a
            under = sub > p + 1
            w1, w2 = v1 * inv, v2 * inv
            l1 = jnp.where(under, w1, jnp.where(sub == p + 1, e * ia, 0.0))
            l2 = jnp.where(under, w2, 0.0)
            lower = lower - (l1 * lower[p : p + 1] + l2 * lower[p + 1 : p + 2])
            scale = jnp.where(sub == p, lax.rsqrt(a), scale)
            scale = jnp.where(sub == p + 1, lax.rsqrt(det * ia), scale)
            w1 = jnp.where(sub == p, 1.0 - d * inv, jnp.where(sub == p + 1, e * inv, w1))
            w2 = jnp.where(sub == p, e * inv, jnp.where(sub == p + 1, 1.0 - a * inv, w2))
            if p + 2 < NB:
                rest = cols[2:]
                cols = rest - (w1[None] * rest[:, p : p + 1] + w2[None] * rest[:, p + 1 : p + 2])
            full = full - (w1 * full[p : p + 1] + w2 * full[p + 1 : p + 2])
        lower = lower * scale
        out_ref[pl.ds(r0, NB), :] = lower * scale_row

        old = m_ref[pl.ds(after, NB), :]
        terms = [m * full[j : j + 1] for j, m in enumerate(columns(old, rel))]
        while len(terms) > 1:
            terms = [terms[i] + terms[i + 1] for i in range(0, len(terms), 2)]
        return jnp.where(inside, 0.0, old) - terms[0], lower

    def two_steps(i, carry):
        for at, call in between:
            pl.when(2 * i == at)(call)
        return step(2 * i + 1, step(2 * i, carry))

    lax.fori_loop(0, BLK // NB // 2, two_steps, (scaled[:NB], jnp.zeros((NB, BLK), F32)))


def kernel(
    mom_hbm, grad_hbm, basis_hbm, q_hbm, c_hbm, n_hbm,
    mom_ref, grad_ref, basis_ref, in_sem, b2, bsend, pown, poth, prcv, psum, pcomb, xrcv, pfull, halves, gp, zrcv, gz, yrcv, gown, gfull, g10,
    wp, wyrcv, wy, wzrcv, wfull, afac, xinv, mixed, mblk, iblk, qs, cs, sq, out_sem,
    s_pair, r_pair, s_xr, r_xr, s_xa, r_xa, s_zr, r_zr, s_y, r_y, s_gx, r_gx, s_gz, r_gz,
    s_wy, r_wy, s_wz, r_wz, s_wza, r_wza, s_wya, r_wya, s_end, r_end, s_n, r_n,
):
    f = lax.axis_index("fsdp")
    t = lax.axis_index("tensor")
    z, y = f // NY, f % NY
    x, c = t // 2, t % 2
    o = 1 - c

    pair = (f, x * 2 + o)

    def on_x(k):
        return (f, ((x + k + NX) % NX) * 2 + c)

    def on_y(k):
        return (z * NY + (y + k + NY) % NY, t)

    def on_z(k):
        return (((z + k) % NZ) * NY + y, t)

    s = 1 - 2 * c

    pending = []

    def make(src, dst, ssem, rsem, to):
        return pltpu.make_async_remote_copy(
            src_ref=src, dst_ref=dst, send_sem=ssem, recv_sem=rsem,
            device_id=to, device_id_type=MESH,
        )

    def send(*args):
        copy = make(*args)
        copy.start()
        pending.append(copy)
        return copy

    loads = [
        pltpu.make_async_copy(src, dst, in_sem.at[i])
        for i, (src, dst) in enumerate(
            (
                (mom_hbm, mom_ref),
                (grad_hbm, grad_ref),
                (basis_hbm.at[o], basis_ref.at[o]),
                (basis_hbm.at[c], basis_ref.at[c]),
            )
        )
    ]
    for load in loads:
        load.start()
    barrier = pltpu.get_barrier_semaphore()
    peers = [pair] + [on_x(k) for k in range(1, NX)]
    peers += [(f, ((x + k) % NX) * 2 + o) for k in range(1, NX)]
    peers += [on_y(k) for k in range(1, NY)] + [on_z(k) for k in range(1, NZ)]
    for peer in peers:
        pl.semaphore_signal(barrier, inc=1, device_id=peer, device_id_type=MESH)

    for load in loads[:3]:
        load.wait()
    bsend[...] = mom_ref[o] + grad_ref[o].astype(F32)
    p = dot3(bsend[...], basis_ref[o], 0, 0)
    for b in range(4):
        poth[b] = p[:, b * BLK : (b + 1) * BLK]
    pl.semaphore_wait(barrier, len(peers))
    cp = send(poth, prcv, s_pair.at[0], r_pair.at[0], pair)
    cb = send(bsend, b2.at[c], s_pair.at[1], r_pair.at[1], pair)
    own = mom_ref[c] + grad_ref[c].astype(F32)
    b2[c] = own
    loads[3].wait()
    p = dot3(own, basis_ref[c], 0, 0)
    for b in range(4):
        pown[b] = p[:, b * BLK : (b + 1) * BLK]
    cp.wait_recv()
    for b in range(4):
        psum[b] = pown[b] + prcv[b]

    def sum_start(parts, me, own, own_sem, rcv, rcv_sem, to):
        far = send(parts.at[(me + 2) % 4], rcv.at[0], own_sem.at[0], rcv_sem.at[0], to(s))
        near = send(parts.at[(me - s + 4) % 4], rcv.at[1], own_sem.at[1], rcv_sem.at[1], to(-s))
        return far, near

    def sum_relay(started, parts, me, own, own_sem, rcv, rcv_sem, to):
        started[0].wait_recv()
        own[...] = parts[(me + s + 4) % 4] + rcv[0]
        return started[1], send(own, rcv.at[2], own_sem.at[2], rcv_sem.at[2], to(s))

    def sum_end(started, parts, me, own, own_sem, rcv, rcv_sem, to):
        for copy in started:
            copy.wait_recv()
        return parts[me] + rcv[1] + rcv[2]

    def gather_start(slot, me, ssem, rsem, to):
        return [send(slot(me), slot(me), ssem.at[i], rsem.at[i], to(k)) for i, k in enumerate((s, -s))]

    def gather_relay(started, slot, me, ssem, rsem, to):
        here = slot((me - s + 4) % 4)
        return [started[1], send(here, here, ssem.at[2], rsem.at[2], to(s))]

    args = (psum, x, pcomb, s_xr, xrcv, r_xr, on_x)
    pfull[x] = sum_end(sum_relay(sum_start(*args), *args), *args)
    a_args = (lambda i: pfull.at[i], x, s_xa, r_xa, on_x)
    across = gather_start(*a_args)

    def rows8(k):
        return pl.ds(pl.multiple_of(((z + k) % NZ) * 8, 8), 8)

    first, rest = pl.ds(0, 2), pl.ds(2, 3)
    around = (4, 3, 5, 2, 6, 1, 7)

    def gram_z(part, n):
        return [
            send(
                gp.at[x, n, rows8(k), :], zrcv.at[k - 1, n],
                s_zr.at[part, k - 1], r_zr.at[part, k - 1], on_z(k),
            )
            for k in around
        ]

    def gram_y(part, n, before):
        for copy in before:
            copy.wait_recv()
        total = gp[x, n, rows8(0), :]
        for k in range(NZ - 1):
            total = total + zrcv[k, n]
        gz[n] = total
        return [
            send(gz.at[n], yrcv.at[k - 1, n], s_y.at[part, k - 1], r_y.at[part, k - 1], on_y(k))
            for k in (2, 1, 3)
        ]

    def gram_back_z(part, n):
        here = gfull.at[x, n, rows8(0), :]
        return [
            make(gown.at[n], here, s_gz.at[part, k - 1], r_gz.at[part, k - 1], on_z(k)) for k in around
        ]

    def gram_gather_z(part, n, before):
        for copy in before:
            copy.wait_recv()
        total = gz[n]
        for k in range(NY - 1):
            total = total + yrcv[k, n]
        gown[n] = total
        gfull[x, n, rows8(0), :] = total
        copies = gram_back_z(part, n)
        for copy in copies:
            copy.start()
        return copies

    w_rows = COLS // NZ

    def w_half(h):
        return pl.ds(h * COLS, COLS)

    def w_part(h, k):
        return pl.ds(pl.multiple_of(h * COLS + ((z + k) % NZ) * w_rows, 8), w_rows)

    opposite_first = (2, 1, 3)

    def w_y(h):
        rows = w_half(h)
        return [
            make(
                wp.at[(y + k) % NY, rows, :], wyrcv.at[k - 1, rows, :],
                s_wy.at[h, k - 1], r_wy.at[h, k - 1], on_y(k),
            )
            for k in opposite_first
        ]

    def w_z(h):
        return [
            make(wy.at[w_part(h, k), :], wzrcv.at[h, k - 1], s_wz.at[h, k - 1], r_wz.at[h, k - 1], on_z(k))
            for k in around
        ]

    def w_back_z(h):
        here = wfull.at[y, w_part(h, 0), :]
        return [make(here, here, s_wza.at[h, k - 1], r_wza.at[h, k - 1], on_z(k)) for k in around]

    def w_back_y(h):
        here = wfull.at[y, w_half(h), :]
        return [
            make(here, here, s_wya.at[h, k - 1], r_wya.at[h, k - 1], on_y(k)) for k in opposite_first
        ]

    def w_to_z(h):
        rows = w_half(h)
        for copy in w_y(h):
            copy.wait_recv()
        wy[rows, :] = wp[y, rows, :] + wyrcv[0, rows, :] + wyrcv[1, rows, :] + wyrcv[2, rows, :]
        for copy in w_z(h):
            copy.start()

    def w_from_z(h):
        for copy in w_z(h):
            copy.wait_recv()
        total = wy[w_part(h, 0), :]
        for k in range(NZ - 1):
            total = total + wzrcv[h, k]
        wfull[y, w_part(h, 0), :] = total
        for copy in w_back_z(h):
            copy.start()

    def w_to_y(h):
        for copy in w_back_z(h):
            copy.wait_recv()
        for copy in w_back_y(h):
            copy.start()

    def w_end(h):
        for copy in w_back_y(h):
            copy.wait_recv()

    g = dot6(pfull[x], pfull[x], 0, 0)
    for h in range(2):
        gp[x, h] = g[h * 64 : (h + 1) * 64]
    g0 = gram_z(0, first)
    across[0].wait_recv()
    far = gather_relay(across, *a_args)[1]
    across[1].wait_recv()
    g = dot6(pfull[x + 1 - x // 3], pfull[x % 3], 0, 0)
    for h in range(2):
        gp[x, 2 + h] = g[h * 64 : (h + 1) * 64]
    between_two = (x + 1) % 2
    g = dot6(pfull[between_two + 2], pfull[between_two], 0, 0)
    for h in range(2):
        halves[h] = g[h * 64 : (h + 1) * 64]
    gp[x, 4] = halves[x // 2]
    g1 = gram_z(1, rest)
    g0 = gram_y(0, first, g0)
    far.wait_recv()
    cb.wait_recv()
    for n, k in enumerate((*opposite_first, 0)):
        b = (y + k) % NY
        for h in range(2):
            wp[b, w_half(h), :] = dot3(b2[h], pfull[b], 1, 0)
            if n < 3:
                w_y(h)[n].start()
    g0 = gram_gather_z(0, first, g0)
    g1 = gram_y(1, rest, g1)
    for copy in g0:
        copy.wait_recv()

    def diagonals():
        here = gfull.at[x, first]
        return [make(here, here, s_gx.at[k + 2], r_gx.at[k + 2], on_x(k)) for k in (1, 3, 2)]

    def diagonal_from(chip):
        k = (x - chip + NX) % NX
        here = gfull.at[chip, first]
        return make(here, here, s_gx.at[k + 2], r_gx.at[k + 2], on_x(k))

    @pl.when(x == 0)
    def _():
        for copy in diagonals():
            copy.start()

    gram_gather_z(1, rest, g1)

    @pl.when(x != 0)
    def _():
        for copy in diagonals():
            copy.start()
        diagonal_from(0).wait_recv()

    def span(i, j):
        return slice(i * BLK, j * BLK)

    def rest_x():
        here = gfull.at[x, rest]
        other = gfull.at[(x - s + NX) % NX, rest]
        return (
            make(here, here, s_gx.at[0], r_gx.at[0], on_x(s)),
            make(here, here, s_gx.at[1], r_gx.at[1], on_x(-s)),
            make(other, other, s_gx.at[2], r_gx.at[2], on_x(s)),
        )

    def early():
        here = gfull.at[0, pl.ds(2, 2)]
        return [make(here, g10, s_gx.at[k + 5], r_gx.at[k + 5], on_x(k)) for k in (1, 3, 2)]

    def rest_near():
        for copy in gram_back_z(1, rest):
            copy.wait_recv()

        @pl.when(x == 0)
        def _():
            for copy in early():
                copy.start()
            g10[...] = gfull[0, 2:4]

        for copy in rest_x()[:2]:
            copy.start()

    def rest_far():
        rest_x()[0].wait_recv()
        rest_x()[2].start()

    def diagonal_end(chip):
        @pl.when(x != chip)
        def _():
            diagonal_from(chip).wait_recv()

    def early_end():
        @pl.when(x != 0)
        def _():
            here = gfull.at[0, pl.ds(2, 2)]
            make(here, g10, s_gx.at[x + 5], r_gx.at[x + 5], on_x(x)).wait_recv()

    def rest_end():
        diagonal_end(2)
        diagonal_end(3)
        for copy in rest_x()[1:]:
            copy.wait_recv()
        for i in range(2, 4):
            for j in range(i + 1):
                afac[span(i, i + 1), span(j, j + 1)] = load(i, j)
        panel = dot6(afac[span(2, 4), span(0, 1)], xinv[span(0, 1), span(0, 1)], 1, 1)
        afac[span(2, 4), span(0, 1)] = panel
        afac[span(2, 4), span(1, 2)] = afac[span(2, 4), span(1, 2)] - dot6(
            panel, afac[span(1, 2), span(0, 1)], 1, 1
        )

    def let_go():
        for copy in pending:
            copy.wait_send()
        pending.clear()

    def call(f, h):
        return functools.partial(f, h)

    between = [
        [(2, call(w_to_z, 0)), (4, rest_near), (4, call(w_to_z, 1)), (6, rest_far)],
        [(2, call(w_from_z, 0)), (4, call(w_from_z, 1)), (6, rest_end)],
        [(2, call(w_to_y, 0)), (6, call(w_to_y, 1))],
        [],
    ]

    def load(i, j):
        return jnp.concatenate([gfull[PLACE[(2 * i + h, j)]] for h in range(2)], axis=0)

    def lanes(b):
        return slice(b * BLK, (b + 1) * BLK)

    def half(i):
        return pl.ds(pl.multiple_of(i * COLS, 8), COLS)

    tril = lax.broadcasted_iota(jnp.int32, (BLK, BLK), 0) >= lax.broadcasted_iota(
        jnp.int32, (BLK, BLK), 1
    )
    xinv[...] = jnp.zeros_like(xinv)
    projected = jnp.concatenate([pfull[b] for b in range(4)], axis=1)
    mblk[...] = load(0, 0)
    for kb in range(4):
        here, below, done = span(kb, kb + 1), span(kb + 1, 4), span(0, kb + 1)
        invert_factor(mblk, iblk, between[kb])
        inv = jnp.where(tril, iblk[...], 0.0)
        xinv[here, here] = inv
        if kb == 0:
            early_end()
            diagonal_end(1)
            panel = dot6(g10[...].reshape(BLK, BLK), inv, 1, 1)
            afac[span(1, 2), here] = panel
            mblk[...] = load(1, 1) - dot6(panel, panel, 1, 1)
        if kb == 1:
            afac[below, here] = dot6(afac[below, here], inv, 1, 1)
            left = afac[below, done]
            mblk[...] = afac[span(2, 3), span(2, 3)] - dot6(left[:BLK], left[:BLK], 1, 1)
            under = afac[span(3, 4), span(2, 4)] - dot6(left[BLK:], left, 1, 1)
            afac[span(3, 4), span(2, 4)] = under
        if kb == 2:
            panel = dot6(afac[below, here], inv, 1, 1)
            afac[below, here] = panel
            mblk[...] = afac[below, below] - dot6(panel, panel, 1, 1)
        if kb > 0:
            xinv[here, span(0, kb)] = -dot3(inv, mixed[:, span(0, kb)], 1, 0)
        if kb < 3:
            mixed[:, done] = dot3(afac[span(kb + 1, kb + 2), done], xinv[done, done], 1, 0)
        qs[:, lanes(kb)] = dot3(projected[:, done], xinv[here, done], 1, 1)
        if kb == 1:
            let_go()
    ends = [
        send(qs, q_hbm.at[c], s_end.at[0], r_end.at[0], pair),
        make(cs.at[half(o), :], c_hbm.at[c], s_end.at[1], r_end.at[1], pair),
    ]
    stores = [
        pltpu.make_async_copy(qs, q_hbm.at[c], out_sem.at[0]),
        pltpu.make_async_copy(cs.at[half(c), :], c_hbm.at[c], out_sem.at[1]),
        pltpu.make_async_copy(sq, n_hbm.at[c, x], out_sem.at[2]),
    ]
    stores[0].start()
    for h in range(2):
        w_end(h)
        rows = w_half(h)
        w = jnp.concatenate([wfull[b, rows, :] for b in range(4)], axis=1)
        for kb in range(4):
            done = span(0, kb + 1)
            cs[rows, lanes(kb)] = dot3(w[:, done], xinv[span(kb, kb + 1), done], 1, 1)
    ends[1].start()
    stores[1].start()
    sq[...] = jnp.sum(cs[...] * cs[...], axis=0, keepdims=True)
    stores[2].start()
    sums = [
        send(sq, n_hbm.at[c, x], s_n.at[i], r_n.at[i], to)
        for i, to in enumerate(
            [on_x(2), on_x(1), on_x(3)]
            + [(f, ((x + k) % NX) * 2 + o) for k in (2, 1, 3, 0)]
        )
    ]
    for copy in pending[:-len(sums)]:
        copy.wait_send()
    @pl.when(x == 0)
    def _():
        for copy in early():
            copy.wait_send()

    for copy in diagonals() + list(rest_x()) + gram_back_z(0, first) + gram_back_z(1, rest):
        copy.wait_send()
    for h in range(2):
        for copy in list(w_y(h)) + w_z(h) + w_back_z(h) + list(w_back_y(h)):
            copy.wait_send()
    for copy in ends + sums:
        copy.wait_recv()
    ends[1].wait_send()
    for copy in sums:
        copy.wait_send()
    for store in stores:
        store.wait()


def finish(mom_ref, grad_ref, q_ref, c_ref, n_ref, nm_ref, nb_ref, up_ref):
    q, coeffs = q_ref[0], c_ref[0]
    error = lax.dot_general(
        coeffs.astype(BF16), q.astype(BF16), (((1,), (1,)), ((), ())), preferred_element_type=F32
    )
    nm_ref[0] = mom_ref[0] + grad_ref[0].astype(F32) - 0.05 * error
    basis = coeffs * lax.rsqrt(n_ref[0, 0] + n_ref[0, 1] + n_ref[0, 2] + n_ref[0, 3] + 1e-06)
    nb_ref[0] = basis
    up_ref[0] = (math.sqrt(D * FF / RANK) * dot3(basis, q, 1, 1)).astype(BF16)


def on_device(momentum, grad, basis):
    vm = pltpu.VMEM
    chunk = (4, BLK, BLK)
    scratch = [
        vm((2, COLS, ROWS), F32), vm((2, COLS, ROWS), BF16), vm((2, COLS, RANK), F32),
        pltpu.SemaphoreType.DMA((4,)),
        vm((2, COLS, ROWS), F32), vm((COLS, ROWS), F32),
        vm(chunk, F32), vm(chunk, F32), vm(chunk, F32), vm(chunk, F32),
        vm((BLK, BLK), F32), vm((3, BLK, BLK), F32), vm(chunk, F32),
        vm((2, 64, BLK), F32),
        vm((4, 5, 64, BLK), F32), vm((7, 5, 8, BLK), F32), vm((5, 8, BLK), F32),
        vm((3, 5, 8, BLK), F32), vm((5, 8, BLK), F32), vm((4, 5, 64, BLK), F32), vm((2, 64, BLK), F32),
        vm((4, 2 * COLS, BLK), F32),
        vm((3, 2 * COLS, BLK), F32), vm((2 * COLS, BLK), F32),
        vm((2, 7, COLS // NZ, BLK), F32), vm((4, 2 * COLS, BLK), F32),
        vm((RANK, RANK), F32), vm((RANK, RANK), F32), vm((BLK, RANK), F32),
        *[vm((BLK, BLK), F32)] * 2,
        vm((ROWS, RANK), F32), vm((2 * COLS, RANK), F32),
        vm((1, RANK), F32),
        pltpu.SemaphoreType.DMA((3,)),
    ]
    for n in (2, 3, 3, (2, 7), (2, 3), 9, (2, 7), (2, 3), (2, 7), (2, 7), (2, 3), 2, 7):
        shape = n if isinstance(n, tuple) else (n,)
        scratch += [pltpu.SemaphoreType.DMA(shape), pltpu.SemaphoreType.DMA(shape)]
    hbm = pl.BlockSpec(memory_space=pl.ANY)
    momentum, grad = jnp.swapaxes(momentum, 1, 2), jnp.swapaxes(grad, 1, 2)
    q, coeffs, sums = pl.pallas_call(
        kernel,
        out_shape=(
            jax.ShapeDtypeStruct((2, ROWS, RANK), F32),
            jax.ShapeDtypeStruct((2, COLS, RANK), F32),
            jax.ShapeDtypeStruct((2, NX, 1, RANK), F32),
        ),
        in_specs=[hbm] * 3,
        out_specs=(hbm,) * 3,
        scratch_shapes=scratch,
        compiler_params=pltpu.CompilerParams(
            collective_id=0, has_side_effects=True, vmem_limit_bytes=58 * 2**20
        ),
    )(momentum, grad, basis)

    def one(*shape):
        return pl.BlockSpec((1, *shape), lambda i: (i,) + (0,) * len(shape))

    nm, nb, up = pl.pallas_call(
        finish,
        grid=(2,),
        out_shape=(
            jax.ShapeDtypeStruct((2, COLS, ROWS), F32),
            jax.ShapeDtypeStruct((2, COLS, RANK), F32),
            jax.ShapeDtypeStruct((2, COLS, ROWS), BF16),
        ),
        in_specs=[one(COLS, ROWS), one(COLS, ROWS), one(ROWS, RANK), one(COLS, RANK), one(NX, 1, RANK)],
        out_specs=(one(COLS, ROWS), one(COLS, RANK), one(COLS, ROWS)),
        compiler_params=pltpu.CompilerParams(vmem_limit_bytes=58 * 2**20),
    )(momentum, grad, q, coeffs, sums)
    return jnp.swapaxes(nm, 1, 2), nb, jnp.swapaxes(up, 1, 2)


def solution(mesh):
    in_specs = (P(None, "fsdp", "tensor"), P(None, "fsdp", "tensor"), P(None, "tensor", None))
    out_specs = (P(None, "fsdp", "tensor"), P(None, "tensor", None), P(None, "fsdp", "tensor"))
    return jax.shard_map(
        on_device, mesh=mesh, in_specs=in_specs, out_specs=out_specs, check_vma=False
    )
```

```python
import functools
import math

import jax
import jax.numpy as jnp
from jax import lax
from jax.experimental import pallas as pl
from jax.experimental.pallas import tpu as pltpu
from jax.sharding import PartitionSpec as P

D = 4096
FF = 1536
RANK = 512
NX, NY, NZ = 4, 4, 8
ROWS = 128
COLS = 192
BLK = 128
NB = 8
F32 = jnp.float32
BF16 = jnp.bfloat16
HIGHEST = lax.Precision.HIGHEST
MESH = pl.DeviceIdType.MESH

PLACE = {(2 * x + h, x): (x, h) for x in range(NX) for h in range(2)}
PLACE.update({(2 * (x + 1 - x // 3) + h, x % 3): (x, 2 + h) for x in range(NX) for h in range(2)})
PLACE.update({(2 * (2 + (x + 1) % 2) + x // 2, (x + 1) % 2): (x, 4) for x in range(NX)})


def dot6(a, b, ca, cb):
    return lax.dot_general(
        a, b, (((ca,), (cb,)), ((), ())), precision=HIGHEST, preferred_element_type=F32
    )


def split(a):
    hi = a.astype(BF16)
    return hi, (a - hi.astype(F32)).astype(BF16)


def dot3(a, b, ca, cb):
    dims = (((ca,), (cb,)), ((), ()))
    ah, al = split(a)
    bh, bl = split(b)
    one = functools.partial(lax.dot_general, dimension_numbers=dims, preferred_element_type=F32)
    return one(ah, bh) + (one(ah, bl) + one(al, bh))


def gram_long(a):
    hi = a.astype(BF16).astype(F32)
    rest = a - hi
    mid = rest.astype(BF16).astype(F32)
    low = rest - mid
    lhs = jnp.concatenate([hi, hi, hi, mid, mid, low], axis=0).astype(BF16)
    rhs = jnp.concatenate([hi, mid, low, hi, mid, hi], axis=0).astype(BF16)
    return lax.dot_general(lhs, rhs, (((0,), (0,)), ((), ())), preferred_element_type=F32)


def invert_factor(m_ref, out_ref, between):
    lane = lax.broadcasted_iota(jnp.int32, (NB, BLK), 1)
    sub = lax.broadcasted_iota(jnp.int32, (NB, BLK), 0)
    lane_all = lax.broadcasted_iota(jnp.int32, (BLK, BLK), 1)
    eye = lax.broadcasted_iota(jnp.int32, (BLK, BLK), 0) == lane_all
    diagonal = jnp.where(eye, m_ref[...], 0.0)
    scale_row = lax.rsqrt(jnp.sum(diagonal, axis=0, keepdims=True))
    scale_col = lax.rsqrt(jnp.sum(diagonal, axis=1, keepdims=True))
    scaled = m_ref[...] * scale_col * scale_row
    m_ref[...] = scaled

    def columns(rows, rel):
        return [
            jnp.broadcast_to(
                jnp.sum(jnp.where(rel == j, rows, 0.0), axis=1, keepdims=True), (NB, BLK)
            )
            for j in range(NB)
        ]

    def step(b, carry):
        rows, previous = carry
        r0 = pl.multiple_of(b * NB, NB)
        after = pl.multiple_of(jnp.minimum(r0 + NB, BLK - NB), NB)
        rel = lane - r0
        inside = jnp.logical_and(rel >= 0, rel < NB)
        rel_all = lane_all - r0
        inside_before = jnp.logical_and(rel_all >= -NB, rel_all < 0)

        m_ref[...] = jnp.where(inside_before, 0.0, m_ref[...]) - gram_long(previous)

        cols = jnp.stack(columns(rows, rel))
        full = jnp.where(inside, jnp.where(rel == sub, 1.0, 0.0), rows)
        lower = full
        scale = jnp.zeros((NB, BLK), F32)
        for p in range(0, NB, 2):
            u1, u2 = cols[0], cols[1]
            a, e, d = u1[p : p + 1], u2[p : p + 1], u2[p + 1 : p + 2]
            det = a * d - e * e
            inv = pl.reciprocal(det, approx=True)
            inv = inv * (2.0 - det * inv)
            v1, v2 = d * u1 - e * u2, a * u2 - e * u1
            ia = 1.0 / a
            under = sub > p + 1
            w1, w2 = v1 * inv, v2 * inv
            l1 = jnp.where(under, w1, jnp.where(sub == p + 1, e * ia, 0.0))
            l2 = jnp.where(under, w2, 0.0)
            lower = lower - (l1 * lower[p : p + 1] + l2 * lower[p + 1 : p + 2])
            scale = jnp.where(sub == p, lax.rsqrt(a), scale)
            scale = jnp.where(sub == p + 1, lax.rsqrt(det * ia), scale)
            w1 = jnp.where(sub == p, 1.0 - d * inv, jnp.where(sub == p + 1, e * inv, w1))
            w2 = jnp.where(sub == p, e * inv, jnp.where(sub == p + 1, 1.0 - a * inv, w2))
            if p + 2 < NB:
                rest = cols[2:]
                cols = rest - (w1[None] * rest[:, p : p + 1] + w2[None] * rest[:, p + 1 : p + 2])
            full = full - (w1 * full[p : p + 1] + w2 * full[p + 1 : p + 2])
        lower = lower * scale
        out_ref[pl.ds(r0, NB), :] = lower * scale_row

        old = m_ref[pl.ds(after, NB), :]
        terms = [m * full[j : j + 1] for j, m in enumerate(columns(old, rel))]
        while len(terms) > 1:
            terms = [terms[i] + terms[i + 1] for i in range(0, len(terms), 2)]
        return jnp.where(inside, 0.0, old) - terms[0], lower

    def two_steps(i, carry):
        for at, call in between:
            pl.when(2 * i == at)(call)
        return step(2 * i + 1, step(2 * i, carry))

    lax.fori_loop(0, BLK // NB // 2, two_steps, (scaled[:NB], jnp.zeros((NB, BLK), F32)))


def kernel(
    mom_hbm, grad_hbm, basis_hbm, q_hbm, c_hbm, n_hbm,
    mom_ref, grad_ref, basis_ref, in_sem, b2, bsend, pown, poth, prcv, psum, pcomb, xrcv, pfull, halves, gp, zrcv, gz, yrcv, gown, gfull, g10,
    wp, wyrcv, wy, wzrcv, wfull, afac, xinv, mixed, mblk, iblk, qs, cs, sq, out_sem,
    s_pair, r_pair, s_xr, r_xr, s_xa, r_xa, s_zr, r_zr, s_y, r_y, s_gx, r_gx, s_gz, r_gz,
    s_wy, r_wy, s_wz, r_wz, s_wza, r_wza, s_wya, r_wya, s_end, r_end, s_n, r_n,
):
    f = lax.axis_index("fsdp")
    t = lax.axis_index("tensor")
    z, y = f // NY, f % NY
    x, c = t // 2, t % 2
    o = 1 - c

    pair = (f, x * 2 + o)

    def on_x(k):
        return (f, ((x + k + NX) % NX) * 2 + c)

    def on_y(k):
        return (z * NY + (y + k + NY) % NY, t)

    def on_z(k):
        return (((z + k) % NZ) * NY + y, t)

    s = 1 - 2 * c

    pending = []

    def make(src, dst, ssem, rsem, to):
        return pltpu.make_async_remote_copy(
            src_ref=src, dst_ref=dst, send_sem=ssem, recv_sem=rsem,
            device_id=to, device_id_type=MESH,
        )

    def send(*args):
        copy = make(*args)
        copy.start()
        pending.append(copy)
        return copy

    loads = [
        pltpu.make_async_copy(src, dst, in_sem.at[i])
        for i, (src, dst) in enumerate(
            (
                (mom_hbm, mom_ref),
                (grad_hbm, grad_ref),
                (basis_hbm.at[o], basis_ref.at[o]),
                (basis_hbm.at[c], basis_ref.at[c]),
            )
        )
    ]
    for load in loads:
        load.start()
    barrier = pltpu.get_barrier_semaphore()
    peers = [pair] + [on_x(k) for k in range(1, NX)]
    peers += [(f, ((x + k) % NX) * 2 + o) for k in range(1, NX)]
    peers += [on_y(k) for k in range(1, NY)] + [on_z(k) for k in range(1, NZ)]
    for peer in peers:
        pl.semaphore_signal(barrier, inc=1, device_id=peer, device_id_type=MESH)

    for load in loads[:3]:
        load.wait()
    bsend[...] = mom_ref[o] + grad_ref[o].astype(F32)
    p = dot3(bsend[...], basis_ref[o], 0, 0)
    for b in range(4):
        poth[b] = p[:, b * BLK : (b + 1) * BLK]
    pl.semaphore_wait(barrier, len(peers))
    cp = send(poth, prcv, s_pair.at[0], r_pair.at[0], pair)
    cb = send(bsend, b2.at[c], s_pair.at[1], r_pair.at[1], pair)
    own = mom_ref[c] + grad_ref[c].astype(F32)
    b2[c] = own
    loads[3].wait()
    p = dot3(own, basis_ref[c], 0, 0)
    for b in range(4):
        pown[b] = p[:, b * BLK : (b + 1) * BLK]
    cp.wait_recv()
    for b in range(4):
        psum[b] = pown[b] + prcv[b]

    def sum_start(parts, me, own, own_sem, rcv, rcv_sem, to):
        far = send(parts.at[(me + 2) % 4], rcv.at[0], own_sem.at[0], rcv_sem.at[0], to(s))
        near = send(parts.at[(me - s + 4) % 4], rcv.at[1], own_sem.at[1], rcv_sem.at[1], to(-s))
        return far, near

    def sum_relay(started, parts, me, own, own_sem, rcv, rcv_sem, to):
        started[0].wait_recv()
        own[...] = parts[(me + s + 4) % 4] + rcv[0]
        return started[1], send(own, rcv.at[2], own_sem.at[2], rcv_sem.at[2], to(s))

    def sum_end(started, parts, me, own, own_sem, rcv, rcv_sem, to):
        for copy in started:
            copy.wait_recv()
        return parts[me] + rcv[1] + rcv[2]

    def gather_start(slot, me, ssem, rsem, to):
        return [send(slot(me), slot(me), ssem.at[i], rsem.at[i], to(k)) for i, k in enumerate((s, -s))]

    def gather_relay(started, slot, me, ssem, rsem, to):
        here = slot((me - s + 4) % 4)
        return [started[1], send(here, here, ssem.at[2], rsem.at[2], to(s))]

    args = (psum, x, pcomb, s_xr, xrcv, r_xr, on_x)
    pfull[x] = sum_end(sum_relay(sum_start(*args), *args), *args)
    a_args = (lambda i: pfull.at[i], x, s_xa, r_xa, on_x)
    across = gather_start(*a_args)

    def rows8(k):
        return pl.ds(pl.multiple_of(((z + k) % NZ) * 8, 8), 8)

    first, rest = pl.ds(0, 2), pl.ds(2, 3)
    around = (4, 3, 5, 2, 6, 1, 7)

    def gram_z(part, n):
        return [
            send(
                gp.at[x, n, rows8(k), :], zrcv.at[k - 1, n],
                s_zr.at[part, k - 1], r_zr.at[part, k - 1], on_z(k),
            )
            for k in around
        ]

    def gram_y(part, n, before):
        for copy in before:
            copy.wait_recv()
        total = gp[x, n, rows8(0), :]
        for k in range(NZ - 1):
            total = total + zrcv[k, n]
        gz[n] = total
        return [
            send(gz.at[n], yrcv.at[k - 1, n], s_y.at[part, k - 1], r_y.at[part, k - 1], on_y(k))
            for k in (2, 1, 3)
        ]

    def gram_back_z(part, n):
        here = gfull.at[x, n, rows8(0), :]
        return [
            make(gown.at[n], here, s_gz.at[part, k - 1], r_gz.at[part, k - 1], on_z(k)) for k in around
        ]

    def gram_gather_z(part, n, before):
        for copy in before:
            copy.wait_recv()
        total = gz[n]
        for k in range(NY - 1):
            total = total + yrcv[k, n]
        gown[n] = total
        gfull[x, n, rows8(0), :] = total
        copies = gram_back_z(part, n)
        for copy in copies:
            copy.start()
        return copies

    w_rows = COLS // NZ

    def w_half(h):
        return pl.ds(h * COLS, COLS)

    def w_part(h, k):
        return pl.ds(pl.multiple_of(h * COLS + ((z + k) % NZ) * w_rows, 8), w_rows)

    opposite_first = (2, 1, 3)

    def w_y(h):
        rows = w_half(h)
        return [
            make(
                wp.at[(y + k) % NY, rows, :], wyrcv.at[k - 1, rows, :],
                s_wy.at[h, k - 1], r_wy.at[h, k - 1], on_y(k),
            )
            for k in opposite_first
        ]

    def w_z(h):
        return [
            make(wy.at[w_part(h, k), :], wzrcv.at[h, k - 1], s_wz.at[h, k - 1], r_wz.at[h, k - 1], on_z(k))
            for k in around
        ]

    def w_back_z(h):
        here = wfull.at[y, w_part(h, 0), :]
        return [make(here, here, s_wza.at[h, k - 1], r_wza.at[h, k - 1], on_z(k)) for k in around]

    def w_back_y(h):
        here = wfull.at[y, w_half(h), :]
        return [
            make(here, here, s_wya.at[h, k - 1], r_wya.at[h, k - 1], on_y(k)) for k in opposite_first
        ]

    def w_to_z(h):
        rows = w_half(h)
        for copy in w_y(h):
            copy.wait_recv()
        wy[rows, :] = wp[y, rows, :] + wyrcv[0, rows, :] + wyrcv[1, rows, :] + wyrcv[2, rows, :]
        for copy in w_z(h):
            copy.start()

    def w_from_z(h):
        for copy in w_z(h):
            copy.wait_recv()
        total = wy[w_part(h, 0), :]
        for k in range(NZ - 1):
            total = total + wzrcv[h, k]
        wfull[y, w_part(h, 0), :] = total
        for copy in w_back_z(h):
            copy.start()

    def w_to_y(h):
        for copy in w_back_z(h):
            copy.wait_recv()
        for copy in w_back_y(h):
            copy.start()

    def w_end(h):
        for copy in w_back_y(h):
            copy.wait_recv()

    g = dot6(pfull[x], pfull[x], 0, 0)
    for h in range(2):
        gp[x, h] = g[h * 64 : (h + 1) * 64]
    g0 = gram_z(0, first)
    across[0].wait_recv()
    far = gather_relay(across, *a_args)[1]
    across[1].wait_recv()
    g = dot6(pfull[x + 1 - x // 3], pfull[x % 3], 0, 0)
    for h in range(2):
        gp[x, 2 + h] = g[h * 64 : (h + 1) * 64]
    between_two = (x + 1) % 2
    g = dot6(pfull[between_two + 2], pfull[between_two], 0, 0)
    for h in range(2):
        halves[h] = g[h * 64 : (h + 1) * 64]
    gp[x, 4] = halves[x // 2]
    g1 = gram_z(1, rest)
    g0 = gram_y(0, first, g0)
    far.wait_recv()
    cb.wait_recv()
    for n, k in enumerate((*opposite_first, 0)):
        b = (y + k) % NY
        for h in range(2):
            wp[b, w_half(h), :] = dot3(b2[h], pfull[b], 1, 0)
            if n < 3:
                w_y(h)[n].start()
    g0 = gram_gather_z(0, first, g0)
    g1 = gram_y(1, rest, g1)
    for copy in g0:
        copy.wait_recv()

    def diagonals():
        here = gfull.at[x, first]
        return [make(here, here, s_gx.at[k + 2], r_gx.at[k + 2], on_x(k)) for k in (1, 3, 2)]

    def diagonal_from(chip):
        k = (x - chip + NX) % NX
        here = gfull.at[chip, first]
        return make(here, here, s_gx.at[k + 2], r_gx.at[k + 2], on_x(k))

    @pl.when(x == 0)
    def _():
        for copy in diagonals():
            copy.start()

    gram_gather_z(1, rest, g1)

    @pl.when(x != 0)
    def _():
        for copy in diagonals():
            copy.start()
        diagonal_from(0).wait_recv()

    def span(i, j):
        return slice(i * BLK, j * BLK)

    def rest_x():
        here = gfull.at[x, rest]
        other = gfull.at[(x - s + NX) % NX, rest]
        return (
            make(here, here, s_gx.at[0], r_gx.at[0], on_x(s)),
            make(here, here, s_gx.at[1], r_gx.at[1], on_x(-s)),
            make(other, other, s_gx.at[2], r_gx.at[2], on_x(s)),
        )

    def early():
        here = gfull.at[0, pl.ds(2, 2)]
        return [make(here, g10, s_gx.at[k + 5], r_gx.at[k + 5], on_x(k)) for k in (1, 3, 2)]

    def rest_near():
        for copy in gram_back_z(1, rest):
            copy.wait_recv()

        @pl.when(x == 0)
        def _():
            for copy in early():
                copy.start()
            g10[...] = gfull[0, 2:4]

        for copy in rest_x()[:2]:
            copy.start()

    def rest_far():
        rest_x()[0].wait_recv()
        rest_x()[2].start()

    def diagonal_end(chip):
        @pl.when(x != chip)
        def _():
            diagonal_from(chip).wait_recv()

    def early_end():
        @pl.when(x != 0)
        def _():
            here = gfull.at[0, pl.ds(2, 2)]
            make(here, g10, s_gx.at[x + 5], r_gx.at[x + 5], on_x(x)).wait_recv()

    def rest_end():
        diagonal_end(2)
        diagonal_end(3)
        for copy in rest_x()[1:]:
            copy.wait_recv()
        for i in range(2, 4):
            for j in range(i + 1):
                afac[span(i, i + 1), span(j, j + 1)] = load(i, j)
        panel = dot6(afac[span(2, 4), span(0, 1)], xinv[span(0, 1), span(0, 1)], 1, 1)
        afac[span(2, 4), span(0, 1)] = panel
        afac[span(2, 4), span(1, 2)] = afac[span(2, 4), span(1, 2)] - dot6(
            panel, afac[span(1, 2), span(0, 1)], 1, 1
        )

    def let_go():
        for copy in pending:
            copy.wait_send()
        pending.clear()

    def call(f, h):
        return functools.partial(f, h)

    between = [
        [(4, call(w_to_z, 0)), (8, rest_near), (10, call(w_to_z, 1)), (14, rest_far)],
        [(4, call(w_from_z, 0)), (10, call(w_from_z, 1)), (14, rest_end)],
        [(6, call(w_to_y, 0)), (12, call(w_to_y, 1))],
        [],
    ]

    def load(i, j):
        return jnp.concatenate([gfull[PLACE[(2 * i + h, j)]] for h in range(2)], axis=0)

    def lanes(b):
        return slice(b * BLK, (b + 1) * BLK)

    def half(i):
        return pl.ds(pl.multiple_of(i * COLS, 8), COLS)

    tril = lax.broadcasted_iota(jnp.int32, (BLK, BLK), 0) >= lax.broadcasted_iota(
        jnp.int32, (BLK, BLK), 1
    )
    xinv[...] = jnp.zeros_like(xinv)
    projected = jnp.concatenate([pfull[b] for b in range(4)], axis=1)
    mblk[...] = load(0, 0)
    for kb in range(4):
        here, below, done = span(kb, kb + 1), span(kb + 1, 4), span(0, kb + 1)
        invert_factor(mblk, iblk, between[kb])
        inv = jnp.where(tril, iblk[...], 0.0)
        xinv[here, here] = inv
        if kb == 0:
            early_end()
            diagonal_end(1)
            panel = dot6(g10[...].reshape(BLK, BLK), inv, 1, 1)
            afac[span(1, 2), here] = panel
            mblk[...] = load(1, 1) - dot6(panel, panel, 1, 1)
        if kb == 1:
            afac[below, here] = dot6(afac[below, here], inv, 1, 1)
            left = afac[below, done]
            mblk[...] = afac[span(2, 3), span(2, 3)] - dot6(left[:BLK], left[:BLK], 1, 1)
            under = afac[span(3, 4), span(2, 4)] - dot6(left[BLK:], left, 1, 1)
            afac[span(3, 4), span(2, 4)] = under
        if kb == 2:
            panel = dot6(afac[below, here], inv, 1, 1)
            afac[below, here] = panel
            mblk[...] = afac[below, below] - dot6(panel, panel, 1, 1)
        if kb > 0:
            xinv[here, span(0, kb)] = -dot3(inv, mixed[:, span(0, kb)], 1, 0)
        if kb < 3:
            mixed[:, done] = dot3(afac[span(kb + 1, kb + 2), done], xinv[done, done], 1, 0)
        qs[:, lanes(kb)] = dot3(projected[:, done], xinv[here, done], 1, 1)
        if kb == 1:
            let_go()
    ends = [
        send(qs, q_hbm.at[c], s_end.at[0], r_end.at[0], pair),
        make(cs.at[half(o), :], c_hbm.at[c], s_end.at[1], r_end.at[1], pair),
    ]
    stores = [
        pltpu.make_async_copy(qs, q_hbm.at[c], out_sem.at[0]),
        pltpu.make_async_copy(cs.at[half(c), :], c_hbm.at[c], out_sem.at[1]),
        pltpu.make_async_copy(sq, n_hbm.at[c, x], out_sem.at[2]),
    ]
    stores[0].start()
    for h in range(2):
        w_end(h)
        rows = w_half(h)
        w = jnp.concatenate([wfull[b, rows, :] for b in range(4)], axis=1)
        for kb in range(4):
            done = span(0, kb + 1)
            cs[rows, lanes(kb)] = dot3(w[:, done], xinv[span(kb, kb + 1), done], 1, 1)
    ends[1].start()
    stores[1].start()
    sq[...] = jnp.sum(cs[...] * cs[...], axis=0, keepdims=True)
    stores[2].start()
    sums = [
        send(sq, n_hbm.at[c, x], s_n.at[i], r_n.at[i], to)
        for i, to in enumerate(
            [on_x(2), on_x(1), on_x(3)]
            + [(f, ((x + k) % NX) * 2 + o) for k in (2, 1, 3, 0)]
        )
    ]
    for copy in pending[:-len(sums)]:
        copy.wait_send()
    @pl.when(x == 0)
    def _():
        for copy in early():
            copy.wait_send()

    for copy in diagonals() + list(rest_x()) + gram_back_z(0, first) + gram_back_z(1, rest):
        copy.wait_send()
    for h in range(2):
        for copy in list(w_y(h)) + w_z(h) + w_back_z(h) + list(w_back_y(h)):
            copy.wait_send()
    for copy in ends + sums:
        copy.wait_recv()
    ends[1].wait_send()
    for copy in sums:
        copy.wait_send()
    for store in stores:
        store.wait()


def finish(mom_ref, grad_ref, q_ref, c_ref, n_ref, nm_ref, nb_ref, up_ref):
    q, coeffs = q_ref[0], c_ref[0]
    error = lax.dot_general(
        coeffs.astype(BF16), q.astype(BF16), (((1,), (1,)), ((), ())), preferred_element_type=F32
    )
    nm_ref[0] = mom_ref[0] + grad_ref[0].astype(F32) - 0.05 * error
    basis = coeffs * lax.rsqrt(n_ref[0, 0] + n_ref[0, 1] + n_ref[0, 2] + n_ref[0, 3] + 1e-06)
    nb_ref[0] = basis
    up_ref[0] = (math.sqrt(D * FF / RANK) * dot3(basis, q, 1, 1)).astype(BF16)


def on_device(momentum, grad, basis):
    vm = pltpu.VMEM
    chunk = (4, BLK, BLK)
    scratch = [
        vm((2, COLS, ROWS), F32), vm((2, COLS, ROWS), BF16), vm((2, COLS, RANK), F32),
        pltpu.SemaphoreType.DMA((4,)),
        vm((2, COLS, ROWS), F32), vm((COLS, ROWS), F32),
        vm(chunk, F32), vm(chunk, F32), vm(chunk, F32), vm(chunk, F32),
        vm((BLK, BLK), F32), vm((3, BLK, BLK), F32), vm(chunk, F32),
        vm((2, 64, BLK), F32),
        vm((4, 5, 64, BLK), F32), vm((7, 5, 8, BLK), F32), vm((5, 8, BLK), F32),
        vm((3, 5, 8, BLK), F32), vm((5, 8, BLK), F32), vm((4, 5, 64, BLK), F32), vm((2, 64, BLK), F32),
        vm((4, 2 * COLS, BLK), F32),
        vm((3, 2 * COLS, BLK), F32), vm((2 * COLS, BLK), F32),
        vm((2, 7, COLS // NZ, BLK), F32), vm((4, 2 * COLS, BLK), F32),
        vm((RANK, RANK), F32), vm((RANK, RANK), F32), vm((BLK, RANK), F32),
        *[vm((BLK, BLK), F32)] * 2,
        vm((ROWS, RANK), F32), vm((2 * COLS, RANK), F32),
        vm((1, RANK), F32),
        pltpu.SemaphoreType.DMA((3,)),
    ]
    for n in (2, 3, 3, (2, 7), (2, 3), 9, (2, 7), (2, 3), (2, 7), (2, 7), (2, 3), 2, 7):
        shape = n if isinstance(n, tuple) else (n,)
        scratch += [pltpu.SemaphoreType.DMA(shape), pltpu.SemaphoreType.DMA(shape)]
    hbm = pl.BlockSpec(memory_space=pl.ANY)
    momentum, grad = jnp.swapaxes(momentum, 1, 2), jnp.swapaxes(grad, 1, 2)
    q, coeffs, sums = pl.pallas_call(
        kernel,
        out_shape=(
            jax.ShapeDtypeStruct((2, ROWS, RANK), F32),
            jax.ShapeDtypeStruct((2, COLS, RANK), F32),
            jax.ShapeDtypeStruct((2, NX, 1, RANK), F32),
        ),
        in_specs=[hbm] * 3,
        out_specs=(hbm,) * 3,
        scratch_shapes=scratch,
        compiler_params=pltpu.CompilerParams(
            collective_id=0, has_side_effects=True, vmem_limit_bytes=58 * 2**20
        ),
    )(momentum, grad, basis)

    def one(*shape):
        return pl.BlockSpec((1, *shape), lambda i: (i,) + (0,) * len(shape))

    nm, nb, up = pl.pallas_call(
        finish,
        grid=(2,),
        out_shape=(
            jax.ShapeDtypeStruct((2, COLS, ROWS), F32),
            jax.ShapeDtypeStruct((2, COLS, RANK), F32),
            jax.ShapeDtypeStruct((2, COLS, ROWS), BF16),
        ),
        in_specs=[one(COLS, ROWS), one(COLS, ROWS), one(ROWS, RANK), one(COLS, RANK), one(NX, 1, RANK)],
        out_specs=(one(COLS, ROWS), one(COLS, RANK), one(COLS, ROWS)),
        compiler_params=pltpu.CompilerParams(vmem_limit_bytes=58 * 2**20),
    )(momentum, grad, q, coeffs, sums)
    return jnp.swapaxes(nm, 1, 2), nb, jnp.swapaxes(up, 1, 2)


def solution(mesh):
    in_specs = (P(None, "fsdp", "tensor"), P(None, "fsdp", "tensor"), P(None, "tensor", None))
    out_specs = (P(None, "fsdp", "tensor"), P(None, "tensor", None), P(None, "fsdp", "tensor"))
    return jax.shard_map(
        on_device, mesh=mesh, in_specs=in_specs, out_specs=out_specs, check_vma=False
    )
```

```python
import functools
import math

import jax
import jax.numpy as jnp
from jax import lax
from jax.experimental import pallas as pl
from jax.experimental.pallas import tpu as pltpu
from jax.sharding import PartitionSpec as P

D = 4096
FF = 1536
RANK = 512
NX, NY, NZ = 4, 4, 8
ROWS = 128
COLS = 192
BLK = 128
NB = 16
F32 = jnp.float32
BF16 = jnp.bfloat16
HIGHEST = lax.Precision.HIGHEST
MESH = pl.DeviceIdType.MESH

PLACE = {(2 * x + h, x): (x, h) for x in range(NX) for h in range(2)}
PLACE.update({(2 * (x + 1 - x // 3) + h, x % 3): (x, 2 + h) for x in range(NX) for h in range(2)})
PLACE.update({(2 * (2 + (x + 1) % 2) + x // 2, (x + 1) % 2): (x, 4) for x in range(NX)})


def dot6(a, b, ca, cb):
    return lax.dot_general(
        a, b, (((ca,), (cb,)), ((), ())), precision=HIGHEST, preferred_element_type=F32
    )


def split(a):
    hi = a.astype(BF16)
    return hi, (a - hi.astype(F32)).astype(BF16)


def dot3(a, b, ca, cb):
    dims = (((ca,), (cb,)), ((), ()))
    ah, al = split(a)
    bh, bl = split(b)
    one = functools.partial(lax.dot_general, dimension_numbers=dims, preferred_element_type=F32)
    return one(ah, bh) + (one(ah, bl) + one(al, bh))


def gram_long(a):
    hi = a.astype(BF16).astype(F32)
    rest = a - hi
    mid = rest.astype(BF16).astype(F32)
    low = rest - mid
    lhs = jnp.concatenate([hi, hi, hi, mid, mid, low], axis=0).astype(BF16)
    rhs = jnp.concatenate([hi, mid, low, hi, mid, hi], axis=0).astype(BF16)
    return lax.dot_general(lhs, rhs, (((0,), (0,)), ((), ())), preferred_element_type=F32)


def invert_factor(m_ref, out_ref, prev, pan, between):
    lane = lax.broadcasted_iota(jnp.int32, (NB, BLK), 1)
    sub = lax.broadcasted_iota(jnp.int32, (NB, BLK), 0)
    lane_all = lax.broadcasted_iota(jnp.int32, (BLK, BLK), 1)
    eye = lax.broadcasted_iota(jnp.int32, (BLK, BLK), 0) == lane_all
    diagonal = jnp.where(eye, m_ref[...], 0.0)
    scale_row = lax.rsqrt(jnp.sum(diagonal, axis=0, keepdims=True))
    scale_col = lax.rsqrt(jnp.sum(diagonal, axis=1, keepdims=True))
    scaled = m_ref[...] * scale_col * scale_row
    m_ref[...] = scaled
    pan[...] = scaled[:NB]
    prev[...] = jnp.zeros_like(prev)

    def columns(rows, rel):
        return [
            jnp.broadcast_to(
                jnp.sum(jnp.where(rel == j, rows, 0.0), axis=1, keepdims=True), (NB, BLK)
            )
            for j in range(NB)
        ]

    def step(b, carry):
        for at, call in between:
            pl.when(b == at)(call)
        r0 = pl.multiple_of(b * NB, NB)
        after = pl.multiple_of(jnp.minimum(r0 + NB, BLK - NB), NB)
        rel = lane - r0
        inside = jnp.logical_and(rel >= 0, rel < NB)
        rel_all = lane_all - r0
        inside_before = jnp.logical_and(rel_all >= -NB, rel_all < 0)

        m_ref[...] = jnp.where(inside_before, 0.0, m_ref[...]) - gram_long(prev[...])

        rows = pan[...]
        cols = jnp.stack(columns(rows, rel))
        full = jnp.where(inside, jnp.where(rel == sub, 1.0, 0.0), rows)
        lower = full
        scale = jnp.zeros((NB, BLK), F32)
        for p in range(0, NB, 2):
            u1, u2 = cols[0], cols[1]
            a, e, d = u1[p : p + 1], u2[p : p + 1], u2[p + 1 : p + 2]
            det = a * d - e * e
            inv = pl.reciprocal(det, approx=True)
            inv = inv * (2.0 - det * inv)
            v1, v2 = d * u1 - e * u2, a * u2 - e * u1
            ia = 1.0 / a
            under = sub > p + 1
            w1, w2 = v1 * inv, v2 * inv
            l1 = jnp.where(under, w1, jnp.where(sub == p + 1, e * ia, 0.0))
            l2 = jnp.where(under, w2, 0.0)
            lower = lower - (l1 * lower[p : p + 1] + l2 * lower[p + 1 : p + 2])
            scale = jnp.where(sub == p, lax.rsqrt(a), scale)
            scale = jnp.where(sub == p + 1, lax.rsqrt(det * ia), scale)
            w1 = jnp.where(sub == p, 1.0 - d * inv, jnp.where(sub == p + 1, e * inv, w1))
            w2 = jnp.where(sub == p, e * inv, jnp.where(sub == p + 1, 1.0 - a * inv, w2))
            if p + 2 < NB:
                rest = cols[2:]
                cols = rest - (w1[None] * rest[:, p : p + 1] + w2[None] * rest[:, p + 1 : p + 2])
            full = full - (w1 * full[p : p + 1] + w2 * full[p + 1 : p + 2])
        lower = lower * scale
        prev[...] = lower
        out_ref[pl.ds(r0, NB), :] = lower * scale_row

        rows = m_ref[pl.ds(after, NB), :]
        terms = [m * full[j : j + 1] for j, m in enumerate(columns(rows, rel))]
        while len(terms) > 1:
            terms = [terms[i] + terms[i + 1] for i in range(0, len(terms), 2)]
        pan[...] = jnp.where(inside, 0.0, rows) - terms[0]
        return carry

    lax.fori_loop(0, BLK // NB, step, 0)


def kernel(
    mom_hbm, grad_hbm, basis_hbm, q_hbm, c_hbm, n_hbm,
    mom_ref, grad_ref, basis_ref, in_sem, b2, bsend, pown, poth, prcv, psum, pcomb, xrcv, pfull, halves, gp, zrcv, gz, yrcv, gown, gfull, g10,
    wp, wyrcv, wy, wzrcv, wfull, afac, xinv, mixed, mblk, iblk, prev, pan, qs, cs, sq, out_sem,
    s_pair, r_pair, s_xr, r_xr, s_xa, r_xa, s_zr, r_zr, s_y, r_y, s_gx, r_gx, s_gz, r_gz,
    s_wy, r_wy, s_wz, r_wz, s_wza, r_wza, s_wya, r_wya, s_end, r_end, s_n, r_n,
):
    f = lax.axis_index("fsdp")
    t = lax.axis_index("tensor")
    z, y = f // NY, f % NY
    x, c = t // 2, t % 2
    o = 1 - c

    pair = (f, x * 2 + o)

    def on_x(k):
        return (f, ((x + k + NX) % NX) * 2 + c)

    def on_y(k):
        return (z * NY + (y + k + NY) % NY, t)

    def on_z(k):
        return (((z + k) % NZ) * NY + y, t)

    s = 1 - 2 * c

    pending = []

    def make(src, dst, ssem, rsem, to):
        return pltpu.make_async_remote_copy(
            src_ref=src, dst_ref=dst, send_sem=ssem, recv_sem=rsem,
            device_id=to, device_id_type=MESH,
        )

    def send(*args):
        copy = make(*args)
        copy.start()
        pending.append(copy)
        return copy

    loads = [
        pltpu.make_async_copy(src, dst, in_sem.at[i])
        for i, (src, dst) in enumerate(
            (
                (mom_hbm, mom_ref),
                (grad_hbm, grad_ref),
                (basis_hbm.at[o], basis_ref.at[o]),
                (basis_hbm.at[c], basis_ref.at[c]),
            )
        )
    ]
    for load in loads:
        load.start()
    barrier = pltpu.get_barrier_semaphore()
    peers = [pair] + [on_x(k) for k in range(1, NX)]
    peers += [(f, ((x + k) % NX) * 2 + o) for k in range(1, NX)]
    peers += [on_y(k) for k in range(1, NY)] + [on_z(k) for k in range(1, NZ)]
    for peer in peers:
        pl.semaphore_signal(barrier, inc=1, device_id=peer, device_id_type=MESH)

    for load in loads[:3]:
        load.wait()
    bsend[...] = mom_ref[o] + grad_ref[o].astype(F32)
    p = dot3(bsend[...].T, basis_ref[o], 1, 0)
    for b in range(4):
        poth[b] = p[:, b * BLK : (b + 1) * BLK]
    pl.semaphore_wait(barrier, len(peers))
    cp = send(poth, prcv, s_pair.at[0], r_pair.at[0], pair)
    cb = send(bsend, b2.at[c], s_pair.at[1], r_pair.at[1], pair)
    own = mom_ref[c] + grad_ref[c].astype(F32)
    b2[c] = own
    loads[3].wait()
    p = dot3(own.T, basis_ref[c], 1, 0)
    for b in range(4):
        pown[b] = p[:, b * BLK : (b + 1) * BLK]
    cp.wait_recv()
    for b in range(4):
        psum[b] = pown[b] + prcv[b]

    def sum_start(parts, me, own, own_sem, rcv, rcv_sem, to):
        far = send(parts.at[(me + 2) % 4], rcv.at[0], own_sem.at[0], rcv_sem.at[0], to(s))
        near = send(parts.at[(me - s + 4) % 4], rcv.at[1], own_sem.at[1], rcv_sem.at[1], to(-s))
        return far, near

    def sum_relay(started, parts, me, own, own_sem, rcv, rcv_sem, to):
        started[0].wait_recv()
        own[...] = parts[(me + s + 4) % 4] + rcv[0]
        return started[1], send(own, rcv.at[2], own_sem.at[2], rcv_sem.at[2], to(s))

    def sum_end(started, parts, me, own, own_sem, rcv, rcv_sem, to):
        for copy in started:
            copy.wait_recv()
        return parts[me] + rcv[1] + rcv[2]

    def gather_start(slot, me, ssem, rsem, to):
        return [send(slot(me), slot(me), ssem.at[i], rsem.at[i], to(k)) for i, k in enumerate((s, -s))]

    def gather_relay(started, slot, me, ssem, rsem, to):
        here = slot((me - s + 4) % 4)
        return [started[1], send(here, here, ssem.at[2], rsem.at[2], to(s))]

    args = (psum, x, pcomb, s_xr, xrcv, r_xr, on_x)
    pfull[x] = sum_end(sum_relay(sum_start(*args), *args), *args)
    a_args = (lambda i: pfull.at[i], x, s_xa, r_xa, on_x)
    across = gather_start(*a_args)

    def rows8(k):
        return pl.ds(pl.multiple_of(((z + k) % NZ) * 8, 8), 8)

    first, rest = pl.ds(0, 2), pl.ds(2, 3)
    around = (4, 3, 5, 2, 6, 1, 7)

    def gram_z(part, n):
        return [
            send(
                gp.at[x, n, rows8(k), :], zrcv.at[k - 1, n],
                s_zr.at[part, k - 1], r_zr.at[part, k - 1], on_z(k),
            )
            for k in around
        ]

    def gram_y(part, n, before):
        for copy in before:
            copy.wait_recv()
        total = gp[x, n, rows8(0), :]
        for k in range(NZ - 1):
            total = total + zrcv[k, n]
        gz[n] = total
        return [
            send(gz.at[n], yrcv.at[k - 1, n], s_y.at[part, k - 1], r_y.at[part, k - 1], on_y(k))
            for k in (2, 1, 3)
        ]

    def gram_back_z(part, n):
        here = gfull.at[x, n, rows8(0), :]
        return [
            make(gown.at[n], here, s_gz.at[part, k - 1], r_gz.at[part, k - 1], on_z(k)) for k in around
        ]

    def gram_gather_z(part, n, before):
        for copy in before:
            copy.wait_recv()
        total = gz[n]
        for k in range(NY - 1):
            total = total + yrcv[k, n]
        gown[n] = total
        gfull[x, n, rows8(0), :] = total
        copies = gram_back_z(part, n)
        for copy in copies:
            copy.start()
        return copies

    w_rows = COLS // NZ

    def w_half(h):
        return pl.ds(h * COLS, COLS)

    def w_part(h, k):
        return pl.ds(pl.multiple_of(h * COLS + ((z + k) % NZ) * w_rows, 8), w_rows)

    opposite_first = (2, 1, 3)

    def w_y(h):
        rows = w_half(h)
        return [
            make(
                wp.at[(y + k) % NY, rows, :], wyrcv.at[k - 1, rows, :],
                s_wy.at[h, k - 1], r_wy.at[h, k - 1], on_y(k),
            )
            for k in opposite_first
        ]

    def w_z(h):
        return [
            make(wy.at[w_part(h, k), :], wzrcv.at[h, k - 1], s_wz.at[h, k - 1], r_wz.at[h, k - 1], on_z(k))
            for k in around
        ]

    def w_back_z(h):
        here = wfull.at[y, w_part(h, 0), :]
        return [make(here, here, s_wza.at[h, k - 1], r_wza.at[h, k - 1], on_z(k)) for k in around]

    def w_back_y(h):
        here = wfull.at[y, w_half(h), :]
        return [
            make(here, here, s_wya.at[h, k - 1], r_wya.at[h, k - 1], on_y(k)) for k in opposite_first
        ]

    def w_to_z(h):
        rows = w_half(h)
        for copy in w_y(h):
            copy.wait_recv()
        wy[rows, :] = wp[y, rows, :] + wyrcv[0, rows, :] + wyrcv[1, rows, :] + wyrcv[2, rows, :]
        for copy in w_z(h):
            copy.start()

    def w_from_z(h):
        for copy in w_z(h):
            copy.wait_recv()
        total = wy[w_part(h, 0), :]
        for k in range(NZ - 1):
            total = total + wzrcv[h, k]
        wfull[y, w_part(h, 0), :] = total
        for copy in w_back_z(h):
            copy.start()

    def w_to_y(h):
        for copy in w_back_z(h):
            copy.wait_recv()
        for copy in w_back_y(h):
            copy.start()

    def w_end(h):
        for copy in w_back_y(h):
            copy.wait_recv()

    g = dot6(pfull[x].T, pfull[x], 1, 0)
    for h in range(2):
        gp[x, h] = g[h * 64 : (h + 1) * 64]
    g0 = gram_z(0, first)
    across[0].wait_recv()
    far = gather_relay(across, *a_args)[1]
    across[1].wait_recv()
    g = dot6(pfull[x + 1 - x // 3].T, pfull[x % 3], 1, 0)
    for h in range(2):
        gp[x, 2 + h] = g[h * 64 : (h + 1) * 64]
    between_two = (x + 1) % 2
    g = dot6(pfull[between_two + 2].T, pfull[between_two], 1, 0)
    for h in range(2):
        halves[h] = g[h * 64 : (h + 1) * 64]
    gp[x, 4] = halves[x // 2]
    g1 = gram_z(1, rest)
    g0 = gram_y(0, first, g0)
    far.wait_recv()
    cb.wait_recv()
    for n, k in enumerate((*opposite_first, 0)):
        b = (y + k) % NY
        for h in range(2):
            wp[b, w_half(h), :] = dot3(b2[h], pfull[b], 1, 0)
            if n < 3:
                w_y(h)[n].start()
    g0 = gram_gather_z(0, first, g0)
    g1 = gram_y(1, rest, g1)
    for copy in g0:
        copy.wait_recv()

    def diagonals():
        here = gfull.at[x, first]
        return [make(here, here, s_gx.at[k + 2], r_gx.at[k + 2], on_x(k)) for k in (1, 3, 2)]

    def diagonal_from(chip):
        k = (x - chip + NX) % NX
        here = gfull.at[chip, first]
        return make(here, here, s_gx.at[k + 2], r_gx.at[k + 2], on_x(k))

    @pl.when(x == 0)
    def _():
        for copy in diagonals():
            copy.start()

    gram_gather_z(1, rest, g1)

    @pl.when(x != 0)
    def _():
        for copy in diagonals():
            copy.start()
        diagonal_from(0).wait_recv()

    def span(i, j):
        return slice(i * BLK, j * BLK)

    def rest_x():
        here = gfull.at[x, rest]
        other = gfull.at[(x - s + NX) % NX, rest]
        return (
            make(here, here, s_gx.at[0], r_gx.at[0], on_x(s)),
            make(here, here, s_gx.at[1], r_gx.at[1], on_x(-s)),
            make(other, other, s_gx.at[2], r_gx.at[2], on_x(s)),
        )

    def early():
        here = gfull.at[0, pl.ds(2, 2)]
        return [make(here, g10, s_gx.at[k + 5], r_gx.at[k + 5], on_x(k)) for k in (1, 3, 2)]

    def rest_near():
        for copy in gram_back_z(1, rest):
            copy.wait_recv()

        @pl.when(x == 0)
        def _():
            for copy in early():
                copy.start()
            g10[...] = gfull[0, 2:4]

        for copy in rest_x()[:2]:
            copy.start()

    def rest_far():
        rest_x()[0].wait_recv()
        rest_x()[2].start()

    def diagonal_end(chip):
        @pl.when(x != chip)
        def _():
            diagonal_from(chip).wait_recv()

    def early_end():
        @pl.when(x != 0)
        def _():
            here = gfull.at[0, pl.ds(2, 2)]
            make(here, g10, s_gx.at[x + 5], r_gx.at[x + 5], on_x(x)).wait_recv()

    def rest_end():
        diagonal_end(2)
        diagonal_end(3)
        for copy in rest_x()[1:]:
            copy.wait_recv()
        for i in range(2, 4):
            for j in range(i + 1):
                afac[span(i, i + 1), span(j, j + 1)] = load(i, j)
        panel = dot6(afac[span(2, 4), span(0, 1)], xinv[span(0, 1), span(0, 1)], 1, 1)
        afac[span(2, 4), span(0, 1)] = panel
        afac[span(2, 4), span(1, 2)] = afac[span(2, 4), span(1, 2)] - dot6(
            panel, afac[span(1, 2), span(0, 1)], 1, 1
        )

    def let_go():
        for copy in pending:
            copy.wait_send()
        pending.clear()

    def call(f, h):
        return functools.partial(f, h)

    between = [
        [(2, call(w_to_z, 0)), (4, rest_near), (5, call(w_to_z, 1)), (7, rest_far)],
        [(2, call(w_from_z, 0)), (5, call(w_from_z, 1)), (7, rest_end)],
        [(3, call(w_to_y, 0)), (6, call(w_to_y, 1))],
        [],
    ]

    def load(i, j):
        return jnp.concatenate([gfull[PLACE[(2 * i + h, j)]] for h in range(2)], axis=0)

    def lanes(b):
        return slice(b * BLK, (b + 1) * BLK)

    def half(i):
        return pl.ds(pl.multiple_of(i * COLS, 8), COLS)

    tril = lax.broadcasted_iota(jnp.int32, (BLK, BLK), 0) >= lax.broadcasted_iota(
        jnp.int32, (BLK, BLK), 1
    )
    xinv[...] = jnp.zeros_like(xinv)
    projected = jnp.concatenate([pfull[b] for b in range(4)], axis=1)
    mblk[...] = load(0, 0)
    for kb in range(4):
        here, below, done = span(kb, kb + 1), span(kb + 1, 4), span(0, kb + 1)
        invert_factor(mblk, iblk, prev, pan, between[kb])
        inv = jnp.where(tril, iblk[...], 0.0)
        xinv[here, here] = inv
        if kb == 0:
            early_end()
            diagonal_end(1)
            panel = dot6(g10[...].reshape(BLK, BLK), inv, 1, 1)
            afac[span(1, 2), here] = panel
            mblk[...] = load(1, 1) - dot6(panel, panel, 1, 1)
        if kb == 1:
            afac[below, here] = dot6(afac[below, here], inv, 1, 1)
            left = afac[below, done]
            mblk[...] = afac[span(2, 3), span(2, 3)] - dot6(left[:BLK], left[:BLK], 1, 1)
            under = afac[span(3, 4), span(2, 4)] - dot6(left[BLK:], left, 1, 1)
            afac[span(3, 4), span(2, 4)] = under
        if kb == 2:
            panel = dot6(afac[below, here], inv, 1, 1)
            afac[below, here] = panel
            mblk[...] = afac[below, below] - dot6(panel, panel, 1, 1)
        if kb > 0:
            xinv[here, span(0, kb)] = -dot3(inv, mixed[:, span(0, kb)], 1, 0)
        if kb < 3:
            mixed[:, done] = dot3(afac[span(kb + 1, kb + 2), done], xinv[done, done], 1, 0)
        qs[:, lanes(kb)] = dot3(projected[:, done], xinv[here, done], 1, 1)
        if kb == 1:
            let_go()
    ends = [
        send(qs, q_hbm.at[c], s_end.at[0], r_end.at[0], pair),
        make(cs.at[half(o), :], c_hbm.at[c], s_end.at[1], r_end.at[1], pair),
    ]
    stores = [
        pltpu.make_async_copy(qs, q_hbm.at[c], out_sem.at[0]),
        pltpu.make_async_copy(cs.at[half(c), :], c_hbm.at[c], out_sem.at[1]),
        pltpu.make_async_copy(sq, n_hbm.at[c, x], out_sem.at[2]),
    ]
    stores[0].start()
    for h in range(2):
        w_end(h)
        rows = w_half(h)
        w = jnp.concatenate([wfull[b, rows, :] for b in range(4)], axis=1)
        for kb in range(4):
            done = span(0, kb + 1)
            cs[rows, lanes(kb)] = dot3(w[:, done], xinv[span(kb, kb + 1), done], 1, 1)
    ends[1].start()
    stores[1].start()
    sq[...] = jnp.sum(cs[...] * cs[...], axis=0, keepdims=True)
    stores[2].start()
    sums = [
        send(sq, n_hbm.at[c, x], s_n.at[i], r_n.at[i], to)
        for i, to in enumerate(
            [on_x(2), on_x(1), on_x(3)]
            + [(f, ((x + k) % NX) * 2 + o) for k in (2, 1, 3, 0)]
        )
    ]
    for copy in pending[:-len(sums)]:
        copy.wait_send()
    @pl.when(x == 0)
    def _():
        for copy in early():
            copy.wait_send()

    for copy in diagonals() + list(rest_x()) + gram_back_z(0, first) + gram_back_z(1, rest):
        copy.wait_send()
    for h in range(2):
        for copy in list(w_y(h)) + w_z(h) + w_back_z(h) + list(w_back_y(h)):
            copy.wait_send()
    for copy in ends + sums:
        copy.wait_recv()
    ends[1].wait_send()
    for copy in sums:
        copy.wait_send()
    for store in stores:
        store.wait()


def finish(mom_ref, grad_ref, q_ref, c_ref, n_ref, nm_ref, nb_ref, up_ref):
    q, coeffs = q_ref[0], c_ref[0]
    error = lax.dot_general(
        coeffs.astype(BF16), q.astype(BF16), (((1,), (1,)), ((), ())), preferred_element_type=F32
    )
    nm_ref[0] = mom_ref[0] + grad_ref[0].astype(F32) - 0.05 * error
    basis = coeffs * lax.rsqrt(n_ref[0, 0] + n_ref[0, 1] + n_ref[0, 2] + n_ref[0, 3] + 1e-06)
    nb_ref[0] = basis
    up_ref[0] = (math.sqrt(D * FF / RANK) * dot3(basis, q, 1, 1)).astype(BF16)


def on_device(momentum, grad, basis):
    vm = pltpu.VMEM
    chunk = (4, BLK, BLK)
    scratch = [
        vm((2, COLS, ROWS), F32), vm((2, COLS, ROWS), BF16), vm((2, COLS, RANK), F32),
        pltpu.SemaphoreType.DMA((4,)),
        vm((2, COLS, ROWS), F32), vm((COLS, ROWS), F32),
        vm(chunk, F32), vm(chunk, F32), vm(chunk, F32), vm(chunk, F32),
        vm((BLK, BLK), F32), vm((3, BLK, BLK), F32), vm(chunk, F32),
        vm((2, 64, BLK), F32),
        vm((4, 5, 64, BLK), F32), vm((7, 5, 8, BLK), F32), vm((5, 8, BLK), F32),
        vm((3, 5, 8, BLK), F32), vm((5, 8, BLK), F32), vm((4, 5, 64, BLK), F32), vm((2, 64, BLK), F32),
        vm((4, 2 * COLS, BLK), F32),
        vm((3, 2 * COLS, BLK), F32), vm((2 * COLS, BLK), F32),
        vm((2, 7, COLS // NZ, BLK), F32), vm((4, 2 * COLS, BLK), F32),
        vm((RANK, RANK), F32), vm((RANK, RANK), F32), vm((BLK, RANK), F32),
        *[vm((BLK, BLK), F32)] * 2, *[vm((NB, BLK), F32)] * 2,
        vm((ROWS, RANK), F32), vm((2 * COLS, RANK), F32),
        vm((1, RANK), F32),
        pltpu.SemaphoreType.DMA((3,)),
    ]
    for n in (2, 3, 3, (2, 7), (2, 3), 9, (2, 7), (2, 3), (2, 7), (2, 7), (2, 3), 2, 7):
        shape = n if isinstance(n, tuple) else (n,)
        scratch += [pltpu.SemaphoreType.DMA(shape), pltpu.SemaphoreType.DMA(shape)]
    hbm = pl.BlockSpec(memory_space=pl.ANY)
    momentum, grad = jnp.swapaxes(momentum, 1, 2), jnp.swapaxes(grad, 1, 2)
    q, coeffs, sums = pl.pallas_call(
        kernel,
        out_shape=(
            jax.ShapeDtypeStruct((2, ROWS, RANK), F32),
            jax.ShapeDtypeStruct((2, COLS, RANK), F32),
            jax.ShapeDtypeStruct((2, NX, 1, RANK), F32),
        ),
        in_specs=[hbm] * 3,
        out_specs=(hbm,) * 3,
        scratch_shapes=scratch,
        compiler_params=pltpu.CompilerParams(
            collective_id=0, has_side_effects=True, vmem_limit_bytes=58 * 2**20
        ),
    )(momentum, grad, basis)

    def whole(*shape):
        return pl.BlockSpec((1, *shape), lambda i, j: (i,) + (0,) * len(shape))

    def part(width):
        return pl.BlockSpec((1, COLS // 2, width), lambda i, j: (i, j, 0))

    nm, nb, up = pl.pallas_call(
        finish,
        grid=(2, 2),
        out_shape=(
            jax.ShapeDtypeStruct((2, COLS, ROWS), F32),
            jax.ShapeDtypeStruct((2, COLS, RANK), F32),
            jax.ShapeDtypeStruct((2, COLS, ROWS), BF16),
        ),
        in_specs=[part(ROWS), part(ROWS), whole(ROWS, RANK), part(RANK), whole(NX, 1, RANK)],
        out_specs=(part(ROWS), part(RANK), part(ROWS)),
        compiler_params=pltpu.CompilerParams(vmem_limit_bytes=58 * 2**20),
    )(momentum, grad, q, coeffs, sums)
    return jnp.swapaxes(nm, 1, 2), nb, jnp.swapaxes(up, 1, 2)


def solution(mesh):
    in_specs = (P(None, "fsdp", "tensor"), P(None, "fsdp", "tensor"), P(None, "tensor", None))
    out_specs = (P(None, "fsdp", "tensor"), P(None, "tensor", None), P(None, "fsdp", "tensor"))
    return jax.shard_map(
        on_device, mesh=mesh, in_specs=in_specs, out_specs=out_specs, check_vma=False
    )
```

```python
import functools
import math

import jax
import jax.numpy as jnp
from jax import lax
from jax.experimental import pallas as pl
from jax.experimental.pallas import tpu as pltpu
from jax.sharding import PartitionSpec as P

D = 4096
FF = 1536
RANK = 512
NX, NY, NZ = 4, 4, 8
ROWS = 128
COLS = 192
BLK = 128
NB = 16
F32 = jnp.float32
BF16 = jnp.bfloat16
HIGHEST = lax.Precision.HIGHEST
MESH = pl.DeviceIdType.MESH

PLACE = {(2 * x + h, x): (x, h) for x in range(NX) for h in range(2)}
PLACE.update({(2 * (x + 1 - x // 3) + h, x % 3): (x, 2 + h) for x in range(NX) for h in range(2)})
PLACE.update({(2 * (2 + (x + 1) % 2) + x // 2, (x + 1) % 2): (x, 4) for x in range(NX)})


def dot6(a, b, ca, cb):
    return lax.dot_general(
        a, b, (((ca,), (cb,)), ((), ())), precision=HIGHEST, preferred_element_type=F32
    )


def split(a):
    hi = a.astype(BF16)
    return hi, (a - hi.astype(F32)).astype(BF16)


def dot3(a, b, ca, cb):
    dims = (((ca,), (cb,)), ((), ()))
    ah, al = split(a)
    bh, bl = split(b)
    one = functools.partial(lax.dot_general, dimension_numbers=dims, preferred_element_type=F32)
    return one(ah, bh) + (one(ah, bl) + one(al, bh))


def gram_long(a):
    hi = a.astype(BF16).astype(F32)
    rest = a - hi
    mid = rest.astype(BF16).astype(F32)
    low = rest - mid
    lhs = jnp.concatenate([hi, hi, hi, mid, mid, low], axis=0).astype(BF16)
    rhs = jnp.concatenate([hi, mid, low, hi, mid, hi], axis=0).astype(BF16)
    return lax.dot_general(lhs, rhs, (((0,), (0,)), ((), ())), preferred_element_type=F32)


def invert_factor(m_ref, out_ref, prev, pan, between):
    lane = lax.broadcasted_iota(jnp.int32, (NB, BLK), 1)
    sub = lax.broadcasted_iota(jnp.int32, (NB, BLK), 0)
    lane_all = lax.broadcasted_iota(jnp.int32, (BLK, BLK), 1)
    eye = lax.broadcasted_iota(jnp.int32, (BLK, BLK), 0) == lane_all
    diagonal = jnp.where(eye, m_ref[...], 0.0)
    scale_row = lax.rsqrt(jnp.sum(diagonal, axis=0, keepdims=True))
    scale_col = lax.rsqrt(jnp.sum(diagonal, axis=1, keepdims=True))
    scaled = m_ref[...] * scale_col * scale_row
    m_ref[...] = scaled
    pan[...] = scaled[:NB]
    prev[...] = jnp.zeros_like(prev)

    def columns(rows, rel):
        return [
            jnp.broadcast_to(
                jnp.sum(jnp.where(rel == j, rows, 0.0), axis=1, keepdims=True), (NB, BLK)
            )
            for j in range(NB)
        ]

    def step(b, carry):
        for at, call in between:
            pl.when(b == at)(call)
        r0 = pl.multiple_of(b * NB, NB)
        after = pl.multiple_of(jnp.minimum(r0 + NB, BLK - NB), NB)
        rel = lane - r0
        inside = jnp.logical_and(rel >= 0, rel < NB)
        rel_all = lane_all - r0
        inside_before = jnp.logical_and(rel_all >= -NB, rel_all < 0)

        m_ref[...] = jnp.where(inside_before, 0.0, m_ref[...]) - gram_long(prev[...])

        rows = pan[...]
        cols = jnp.stack(columns(rows, rel))
        full = jnp.where(inside, jnp.where(rel == sub, 1.0, 0.0), rows)
        lower = full
        scale = jnp.zeros((NB, BLK), F32)
        for p in range(0, NB, 2):
            u1, u2 = cols[0], cols[1]
            a, e, d = u1[p : p + 1], u2[p : p + 1], u2[p + 1 : p + 2]
            det = a * d - e * e
            inv = pl.reciprocal(det, approx=True)
            inv = inv * (2.0 - det * inv)
            v1, v2 = d * u1 - e * u2, a * u2 - e * u1
            ia = 1.0 / a
            under = sub > p + 1
            w1, w2 = v1 * inv, v2 * inv
            l1 = jnp.where(under, w1, jnp.where(sub == p + 1, e * ia, 0.0))
            l2 = jnp.where(under, w2, 0.0)
            lower = lower - (l1 * lower[p : p + 1] + l2 * lower[p + 1 : p + 2])
            scale = jnp.where(sub == p, lax.rsqrt(a), scale)
            scale = jnp.where(sub == p + 1, lax.rsqrt(det * ia), scale)
            w1 = jnp.where(sub == p, 1.0 - d * inv, jnp.where(sub == p + 1, e * inv, w1))
            w2 = jnp.where(sub == p, e * inv, jnp.where(sub == p + 1, 1.0 - a * inv, w2))
            if p + 2 < NB:
                rest = cols[2:]
                cols = rest - (w1[None] * rest[:, p : p + 1] + w2[None] * rest[:, p + 1 : p + 2])
            full = full - (w1 * full[p : p + 1] + w2 * full[p + 1 : p + 2])
        lower = lower * scale
        prev[...] = lower
        out_ref[pl.ds(r0, NB), :] = lower * scale_row

        rows = m_ref[pl.ds(after, NB), :]
        terms = [m * full[j : j + 1] for j, m in enumerate(columns(rows, rel))]
        while len(terms) > 1:
            terms = [terms[i] + terms[i + 1] for i in range(0, len(terms), 2)]
        pan[...] = jnp.where(inside, 0.0, rows) - terms[0]
        return carry

    lax.fori_loop(0, BLK // NB, step, 0)


def kernel(
    mom_hbm, grad_hbm, basis_hbm, q_hbm, c_hbm, n_hbm,
    mom_ref, grad_ref, basis_ref, in_sem, b2, bsend, pown, poth, prcv, psum, pcomb, xrcv, pfull, halves, gp, zrcv, gz, yrcv, gown, gfull, g10,
    wp, wyrcv, wy, wzrcv, wfull, afac, xinv, mixed, mblk, iblk, prev, pan, qs, cs, sq, out_sem,
    s_pair, r_pair, s_xr, r_xr, s_xa, r_xa, s_zr, r_zr, s_y, r_y, s_gx, r_gx, s_gz, r_gz,
    s_wy, r_wy, s_wz, r_wz, s_wza, r_wza, s_wya, r_wya, s_end, r_end, s_n, r_n,
):
    f = lax.axis_index("fsdp")
    t = lax.axis_index("tensor")
    z, y = f // NY, f % NY
    x, c = t // 2, t % 2
    o = 1 - c

    pair = (f, x * 2 + o)

    def on_x(k):
        return (f, ((x + k + NX) % NX) * 2 + c)

    def on_y(k):
        return (z * NY + (y + k + NY) % NY, t)

    def on_z(k):
        return (((z + k) % NZ) * NY + y, t)

    s = 1 - 2 * c

    pending = []

    def make(src, dst, ssem, rsem, to):
        return pltpu.make_async_remote_copy(
            src_ref=src, dst_ref=dst, send_sem=ssem, recv_sem=rsem,
            device_id=to, device_id_type=MESH,
        )

    def send(*args):
        copy = make(*args)
        copy.start()
        pending.append(copy)
        return copy

    loads = [
        pltpu.make_async_copy(src, dst, in_sem.at[i])
        for i, (src, dst) in enumerate(
            (
                (mom_hbm, mom_ref),
                (grad_hbm, grad_ref),
                (basis_hbm.at[o], basis_ref.at[o]),
                (basis_hbm.at[c], basis_ref.at[c]),
            )
        )
    ]
    for load in loads:
        load.start()
    barrier = pltpu.get_barrier_semaphore()
    peers = [pair] + [on_x(k) for k in range(1, NX)]
    peers += [(f, ((x + k) % NX) * 2 + o) for k in range(1, NX)]
    peers += [on_y(k) for k in range(1, NY)] + [on_z(k) for k in range(1, NZ)]
    for peer in peers:
        pl.semaphore_signal(barrier, inc=1, device_id=peer, device_id_type=MESH)

    for load in loads[:3]:
        load.wait()
    bsend[...] = mom_ref[o] + grad_ref[o].astype(F32)
    p = dot3(bsend[...], basis_ref[o], 0, 0)
    for b in range(4):
        poth[b] = p[:, b * BLK : (b + 1) * BLK]
    pl.semaphore_wait(barrier, len(peers))
    cp = send(poth, prcv, s_pair.at[0], r_pair.at[0], pair)
    cb = send(bsend, b2.at[c], s_pair.at[1], r_pair.at[1], pair)
    own = mom_ref[c] + grad_ref[c].astype(F32)
    b2[c] = own
    loads[3].wait()
    p = dot3(own, basis_ref[c], 0, 0)
    for b in range(4):
        pown[b] = p[:, b * BLK : (b + 1) * BLK]
    cp.wait_recv()
    for b in range(4):
        psum[b] = pown[b] + prcv[b]

    def sum_start(parts, me, own, own_sem, rcv, rcv_sem, to):
        far = send(parts.at[(me + 2) % 4], rcv.at[0], own_sem.at[0], rcv_sem.at[0], to(s))
        near = send(parts.at[(me - s + 4) % 4], rcv.at[1], own_sem.at[1], rcv_sem.at[1], to(-s))
        return far, near

    def sum_relay(started, parts, me, own, own_sem, rcv, rcv_sem, to):
        started[0].wait_recv()
        own[...] = parts[(me + s + 4) % 4] + rcv[0]
        return started[1], send(own, rcv.at[2], own_sem.at[2], rcv_sem.at[2], to(s))

    def sum_end(started, parts, me, own, own_sem, rcv, rcv_sem, to):
        for copy in started:
            copy.wait_recv()
        return parts[me] + rcv[1] + rcv[2]

    def gather_start(slot, me, ssem, rsem, to):
        return [send(slot(me), slot(me), ssem.at[i], rsem.at[i], to(k)) for i, k in enumerate((s, -s))]

    def gather_relay(started, slot, me, ssem, rsem, to):
        here = slot((me - s + 4) % 4)
        return [started[1], send(here, here, ssem.at[2], rsem.at[2], to(s))]

    args = (psum, x, pcomb, s_xr, xrcv, r_xr, on_x)
    pfull[x] = sum_end(sum_relay(sum_start(*args), *args), *args)
    a_args = (lambda i: pfull.at[i], x, s_xa, r_xa, on_x)
    across = gather_start(*a_args)

    def rows8(k):
        return pl.ds(pl.multiple_of(((z + k) % NZ) * 8, 8), 8)

    first, rest = pl.ds(0, 2), pl.ds(2, 3)
    around = (4, 3, 5, 2, 6, 1, 7)

    def gram_z(part, n):
        return [
            send(
                gp.at[x, n, rows8(k), :], zrcv.at[k - 1, n],
                s_zr.at[part, k - 1], r_zr.at[part, k - 1], on_z(k),
            )
            for k in around
        ]

    def gram_y(part, n, before):
        for copy in before:
            copy.wait_recv()
        total = gp[x, n, rows8(0), :]
        for k in range(NZ - 1):
            total = total + zrcv[k, n]
        gz[n] = total
        return [
            send(gz.at[n], yrcv.at[k - 1, n], s_y.at[part, k - 1], r_y.at[part, k - 1], on_y(k))
            for k in (2, 1, 3)
        ]

    def gram_back_z(part, n):
        here = gfull.at[x, n, rows8(0), :]
        return [
            make(gown.at[n], here, s_gz.at[part, k - 1], r_gz.at[part, k - 1], on_z(k)) for k in around
        ]

    def gram_gather_z(part, n, before):
        for copy in before:
            copy.wait_recv()
        total = gz[n]
        for k in range(NY - 1):
            total = total + yrcv[k, n]
        gown[n] = total
        gfull[x, n, rows8(0), :] = total
        copies = gram_back_z(part, n)
        for copy in copies:
            copy.start()
        return copies

    w_rows = COLS // NZ

    def w_half(h):
        return pl.ds(h * COLS, COLS)

    def w_part(h, k):
        return pl.ds(pl.multiple_of(h * COLS + ((z + k) % NZ) * w_rows, 8), w_rows)

    opposite_first = (2, 1, 3)

    def w_y(h):
        rows = w_half(h)
        return [
            make(
                wp.at[(y + k) % NY, rows, :], wyrcv.at[k - 1, rows, :],
                s_wy.at[h, k - 1], r_wy.at[h, k - 1], on_y(k),
            )
            for k in opposite_first
        ]

    def w_z(h):
        return [
            make(wy.at[w_part(h, k), :], wzrcv.at[h, k - 1], s_wz.at[h, k - 1], r_wz.at[h, k - 1], on_z(k))
            for k in around
        ]

    def w_back_z(h):
        here = wfull.at[y, w_part(h, 0), :]
        return [make(here, here, s_wza.at[h, k - 1], r_wza.at[h, k - 1], on_z(k)) for k in around]

    def w_back_y(h):
        here = wfull.at[y, w_half(h), :]
        return [
            make(here, here, s_wya.at[h, k - 1], r_wya.at[h, k - 1], on_y(k)) for k in opposite_first
        ]

    def w_to_z(h):
        rows = w_half(h)
        for copy in w_y(h):
            copy.wait_recv()
        wy[rows, :] = wp[y, rows, :] + wyrcv[0, rows, :] + wyrcv[1, rows, :] + wyrcv[2, rows, :]
        for copy in w_z(h):
            copy.start()

    def w_from_z(h):
        for copy in w_z(h):
            copy.wait_recv()
        total = wy[w_part(h, 0), :]
        for k in range(NZ - 1):
            total = total + wzrcv[h, k]
        wfull[y, w_part(h, 0), :] = total
        for copy in w_back_z(h):
            copy.start()

    def w_to_y(h):
        for copy in w_back_z(h):
            copy.wait_recv()
        for copy in w_back_y(h):
            copy.start()

    def w_end(h):
        for copy in w_back_y(h):
            copy.wait_recv()

    g = dot6(pfull[x], pfull[x], 0, 0)
    for h in range(2):
        gp[x, h] = g[h * 64 : (h + 1) * 64]
    g0 = gram_z(0, first)
    across[0].wait_recv()
    far = gather_relay(across, *a_args)[1]
    across[1].wait_recv()
    g = dot6(pfull[x + 1 - x // 3], pfull[x % 3], 0, 0)
    for h in range(2):
        gp[x, 2 + h] = g[h * 64 : (h + 1) * 64]
    between_two = (x + 1) % 2
    g = dot6(pfull[between_two + 2], pfull[between_two], 0, 0)
    for h in range(2):
        halves[h] = g[h * 64 : (h + 1) * 64]
    gp[x, 4] = halves[x // 2]
    g1 = gram_z(1, rest)
    g0 = gram_y(0, first, g0)
    far.wait_recv()
    cb.wait_recv()
    for n, k in enumerate((*opposite_first, 0)):
        b = (y + k) % NY
        for h in range(2):
            wp[b, w_half(h), :] = dot3(b2[h], pfull[b], 1, 0)
            if n < 3:
                w_y(h)[n].start()
    g0 = gram_gather_z(0, first, g0)
    g1 = gram_y(1, rest, g1)
    for copy in g0:
        copy.wait_recv()

    def diagonals():
        here = gfull.at[x, first]
        return [make(here, here, s_gx.at[k + 2], r_gx.at[k + 2], on_x(k)) for k in (1, 3, 2)]

    def diagonal_from(chip):
        k = (x - chip + NX) % NX
        here = gfull.at[chip, first]
        return make(here, here, s_gx.at[k + 2], r_gx.at[k + 2], on_x(k))

    @pl.when(x == 0)
    def _():
        for copy in diagonals():
            copy.start()

    gram_gather_z(1, rest, g1)

    @pl.when(x != 0)
    def _():
        for copy in diagonals():
            copy.start()
        diagonal_from(0).wait_recv()

    def span(i, j):
        return slice(i * BLK, j * BLK)

    def rest_x():
        here = gfull.at[x, rest]
        other = gfull.at[(x - s + NX) % NX, rest]
        return (
            make(here, here, s_gx.at[0], r_gx.at[0], on_x(s)),
            make(here, here, s_gx.at[1], r_gx.at[1], on_x(-s)),
            make(other, other, s_gx.at[2], r_gx.at[2], on_x(s)),
        )

    def early():
        here = gfull.at[0, pl.ds(2, 2)]
        return [make(here, g10, s_gx.at[k + 5], r_gx.at[k + 5], on_x(k)) for k in (1, 3, 2)]

    def rest_near():
        for copy in gram_back_z(1, rest):
            copy.wait_recv()

        @pl.when(x == 0)
        def _():
            for copy in early():
                copy.start()
            g10[...] = gfull[0, 2:4]

        for copy in rest_x()[:2]:
            copy.start()

    def rest_far():
        rest_x()[0].wait_recv()
        rest_x()[2].start()

    def diagonal_end(chip):
        @pl.when(x != chip)
        def _():
            diagonal_from(chip).wait_recv()

    def early_end():
        @pl.when(x != 0)
        def _():
            here = gfull.at[0, pl.ds(2, 2)]
            make(here, g10, s_gx.at[x + 5], r_gx.at[x + 5], on_x(x)).wait_recv()

    def rest_end():
        diagonal_end(2)
        diagonal_end(3)
        for copy in rest_x()[1:]:
            copy.wait_recv()
        for i in range(2, 4):
            for j in range(i + 1):
                afac[span(i, i + 1), span(j, j + 1)] = load(i, j)
        panel = dot6(afac[span(2, 4), span(0, 1)], xinv[span(0, 1), span(0, 1)], 1, 1)
        afac[span(2, 4), span(0, 1)] = panel
        afac[span(2, 4), span(1, 2)] = afac[span(2, 4), span(1, 2)] - dot6(
            panel, afac[span(1, 2), span(0, 1)], 1, 1
        )

    def let_go():
        for copy in pending:
            copy.wait_send()
        pending.clear()

    def call(f, h):
        return functools.partial(f, h)

    between = [
        [(2, call(w_to_z, 0)), (4, rest_near), (5, call(w_to_z, 1)), (7, rest_far)],
        [(2, call(w_from_z, 0)), (5, call(w_from_z, 1)), (7, rest_end)],
        [(3, call(w_to_y, 0)), (6, call(w_to_y, 1))],
        [],
    ]

    def load(i, j):
        return jnp.concatenate([gfull[PLACE[(2 * i + h, j)]] for h in range(2)], axis=0)

    def lanes(b):
        return slice(b * BLK, (b + 1) * BLK)

    def half(i):
        return pl.ds(pl.multiple_of(i * COLS, 8), COLS)

    tril = lax.broadcasted_iota(jnp.int32, (BLK, BLK), 0) >= lax.broadcasted_iota(
        jnp.int32, (BLK, BLK), 1
    )
    xinv[...] = jnp.zeros_like(xinv)
    projected = jnp.concatenate([pfull[b] for b in range(4)], axis=1)
    mblk[...] = load(0, 0)
    for kb in range(4):
        here, below, done = span(kb, kb + 1), span(kb + 1, 4), span(0, kb + 1)
        invert_factor(mblk, iblk, prev, pan, between[kb])
        inv = jnp.where(tril, iblk[...], 0.0)
        xinv[here, here] = inv
        if kb == 0:
            early_end()
            diagonal_end(1)
            panel = dot6(g10[...].reshape(BLK, BLK), inv, 1, 1)
            afac[span(1, 2), here] = panel
            mblk[...] = load(1, 1) - dot6(panel, panel, 1, 1)
        if kb == 1:
            afac[below, here] = dot6(afac[below, here], inv, 1, 1)
            left = afac[below, done]
            mblk[...] = afac[span(2, 3), span(2, 3)] - dot6(left[:BLK], left[:BLK], 1, 1)
            under = afac[span(3, 4), span(2, 4)] - dot6(left[BLK:], left, 1, 1)
            afac[span(3, 4), span(2, 4)] = under
        if kb == 2:
            panel = dot6(afac[below, here], inv, 1, 1)
            afac[below, here] = panel
            mblk[...] = afac[below, below] - dot6(panel, panel, 1, 1)
        if kb > 0:
            xinv[here, span(0, kb)] = -dot3(inv, mixed[:, span(0, kb)], 1, 0)
        if kb < 3:
            mixed[:, done] = dot3(afac[span(kb + 1, kb + 2), done], xinv[done, done], 1, 0)
        qs[:, lanes(kb)] = dot3(projected[:, done], xinv[here, done], 1, 1)
        if kb == 1:
            let_go()
    ends = [
        send(qs, q_hbm.at[c], s_end.at[0], r_end.at[0], pair),
        make(cs.at[half(o), :], c_hbm.at[c], s_end.at[1], r_end.at[1], pair),
    ]
    stores = [
        pltpu.make_async_copy(qs, q_hbm.at[c], out_sem.at[0]),
        pltpu.make_async_copy(cs.at[half(c), :], c_hbm.at[c], out_sem.at[1]),
        pltpu.make_async_copy(sq, n_hbm.at[c, x], out_sem.at[2]),
    ]
    stores[0].start()
    for h in range(2):
        w_end(h)
        rows = w_half(h)
        w = jnp.concatenate([wfull[b, rows, :] for b in range(4)], axis=1)
        for kb in range(4):
            done = span(0, kb + 1)
            cs[rows, lanes(kb)] = dot3(w[:, done], xinv[span(kb, kb + 1), done], 1, 1)
    ends[1].start()
    stores[1].start()
    sq[...] = jnp.sum(cs[...] * cs[...], axis=0, keepdims=True)
    stores[2].start()
    sums = [
        send(sq, n_hbm.at[c, x], s_n.at[i], r_n.at[i], to)
        for i, to in enumerate(
            [on_x(2), on_x(1), on_x(3)]
            + [(f, ((x + k) % NX) * 2 + o) for k in (2, 1, 3, 0)]
        )
    ]
    for copy in pending[:-len(sums)]:
        copy.wait_send()
    @pl.when(x == 0)
    def _():
        for copy in early():
            copy.wait_send()

    for copy in diagonals() + list(rest_x()) + gram_back_z(0, first) + gram_back_z(1, rest):
        copy.wait_send()
    for h in range(2):
        for copy in list(w_y(h)) + w_z(h) + w_back_z(h) + list(w_back_y(h)):
            copy.wait_send()
    for copy in ends + sums:
        copy.wait_recv()
    ends[1].wait_send()
    for copy in sums:
        copy.wait_send()
    for store in stores:
        store.wait()


def finish(
    mom_hbm, grad_hbm, q_hbm, c_hbm, n_hbm, nm_hbm, nb_hbm, up_hbm,
    mom_ref, grad_ref, q_ref, c_ref, n_ref, nm_ref, nb_ref, up_ref, in_sem, out_sem,
):
    pairs = ((c_hbm, c_ref), (n_hbm, n_ref), (q_hbm, q_ref), (mom_hbm, mom_ref), (grad_hbm, grad_ref))
    loads = [
        [pltpu.make_async_copy(src.at[m], dst.at[m], in_sem.at[m, i]) for i, (src, dst) in enumerate(pairs)]
        for m in range(2)
    ]
    for copies in loads:
        for copy in copies:
            copy.start()
    stores = []

    def store(src, dst, m, i):
        copy = pltpu.make_async_copy(src.at[m], dst.at[m], out_sem.at[m, i])
        copy.start()
        stores.append(copy)

    for m in range(2):
        for copy in loads[m][:2]:
            copy.wait()
        coeffs = c_ref[m]
        basis = coeffs * lax.rsqrt(n_ref[m, 0] + n_ref[m, 1] + n_ref[m, 2] + n_ref[m, 3] + 1e-06)
        nb_ref[m] = basis
        store(nb_ref, nb_hbm, m, 0)
        for copy in loads[m][2:]:
            copy.wait()
        q = q_ref[m]
        error = lax.dot_general(
            coeffs.astype(BF16), q.astype(BF16), (((1,), (1,)), ((), ())), preferred_element_type=F32
        )
        nm_ref[m] = mom_ref[m] + grad_ref[m].astype(F32) - 0.05 * error
        store(nm_ref, nm_hbm, m, 1)
        up_ref[m] = (math.sqrt(D * FF / RANK) * dot3(basis, q, 1, 1)).astype(BF16)
        store(up_ref, up_hbm, m, 2)
    for copy in stores:
        copy.wait()


def on_device(momentum, grad, basis):
    vm = pltpu.VMEM
    chunk = (4, BLK, BLK)
    scratch = [
        vm((2, COLS, ROWS), F32), vm((2, COLS, ROWS), BF16), vm((2, COLS, RANK), F32),
        pltpu.SemaphoreType.DMA((4,)),
        vm((2, COLS, ROWS), F32), vm((COLS, ROWS), F32),
        vm(chunk, F32), vm(chunk, F32), vm(chunk, F32), vm(chunk, F32),
        vm((BLK, BLK), F32), vm((3, BLK, BLK), F32), vm(chunk, F32),
        vm((2, 64, BLK), F32),
        vm((4, 5, 64, BLK), F32), vm((7, 5, 8, BLK), F32), vm((5, 8, BLK), F32),
        vm((3, 5, 8, BLK), F32), vm((5, 8, BLK), F32), vm((4, 5, 64, BLK), F32), vm((2, 64, BLK), F32),
        vm((4, 2 * COLS, BLK), F32),
        vm((3, 2 * COLS, BLK), F32), vm((2 * COLS, BLK), F32),
        vm((2, 7, COLS // NZ, BLK), F32), vm((4, 2 * COLS, BLK), F32),
        vm((RANK, RANK), F32), vm((RANK, RANK), F32), vm((BLK, RANK), F32),
        *[vm((BLK, BLK), F32)] * 2, *[vm((NB, BLK), F32)] * 2,
        vm((ROWS, RANK), F32), vm((2 * COLS, RANK), F32),
        vm((1, RANK), F32),
        pltpu.SemaphoreType.DMA((3,)),
    ]
    for n in (2, 3, 3, (2, 7), (2, 3), 9, (2, 7), (2, 3), (2, 7), (2, 7), (2, 3), 2, 7):
        shape = n if isinstance(n, tuple) else (n,)
        scratch += [pltpu.SemaphoreType.DMA(shape), pltpu.SemaphoreType.DMA(shape)]
    hbm = pl.BlockSpec(memory_space=pl.ANY)
    momentum, grad = jnp.swapaxes(momentum, 1, 2), jnp.swapaxes(grad, 1, 2)
    q, coeffs, sums = pl.pallas_call(
        kernel,
        out_shape=(
            jax.ShapeDtypeStruct((2, ROWS, RANK), F32),
            jax.ShapeDtypeStruct((2, COLS, RANK), F32),
            jax.ShapeDtypeStruct((2, NX, 1, RANK), F32),
        ),
        in_specs=[hbm] * 3,
        out_specs=(hbm,) * 3,
        scratch_shapes=scratch,
        compiler_params=pltpu.CompilerParams(
            collective_id=0, has_side_effects=True, vmem_limit_bytes=58 * 2**20
        ),
    )(momentum, grad, basis)

    shapes = (
        jax.ShapeDtypeStruct((2, COLS, ROWS), F32),
        jax.ShapeDtypeStruct((2, COLS, RANK), F32),
        jax.ShapeDtypeStruct((2, COLS, ROWS), BF16),
    )
    nm, nb, up = pl.pallas_call(
        finish,
        out_shape=shapes,
        in_specs=[hbm] * 5,
        out_specs=(hbm,) * 3,
        scratch_shapes=[vm(v.shape, v.dtype) for v in (momentum, grad, q, coeffs, sums, *shapes)]
        + [pltpu.SemaphoreType.DMA((2, 5)), pltpu.SemaphoreType.DMA((2, 3))],
        compiler_params=pltpu.CompilerParams(vmem_limit_bytes=58 * 2**20),
    )(momentum, grad, q, coeffs, sums)
    return jnp.swapaxes(nm, 1, 2), nb, jnp.swapaxes(up, 1, 2)


def solution(mesh):
    in_specs = (P(None, "fsdp", "tensor"), P(None, "fsdp", "tensor"), P(None, "tensor", None))
    out_specs = (P(None, "fsdp", "tensor"), P(None, "tensor", None), P(None, "fsdp", "tensor"))
    return jax.shard_map(
        on_device, mesh=mesh, in_specs=in_specs, out_specs=out_specs, check_vma=False
    )
```

```python
import functools
import math

import jax
import jax.numpy as jnp
from jax import lax
from jax.experimental import pallas as pl
from jax.experimental.pallas import tpu as pltpu
from jax.sharding import PartitionSpec as P

D = 4096
FF = 1536
RANK = 512
NX, NY, NZ = 4, 4, 8
ROWS = 128
COLS = 192
BLK = 128
NB = 16
F32 = jnp.float32
BF16 = jnp.bfloat16
HIGHEST = lax.Precision.HIGHEST
MESH = pl.DeviceIdType.MESH

PLACE = {(2 * x + h, x): (x, h) for x in range(NX) for h in range(2)}
PLACE.update({(2 * (x + 1 - x // 3) + h, x % 3): (x, 2 + h) for x in range(NX) for h in range(2)})
PLACE.update({(2 * (2 + (x + 1) % 2) + x // 2, (x + 1) % 2): (x, 4) for x in range(NX)})


def dot6(a, b, ca, cb):
    return lax.dot_general(
        a, b, (((ca,), (cb,)), ((), ())), precision=HIGHEST, preferred_element_type=F32
    )


def split(a):
    hi = a.astype(BF16)
    return hi, (a - hi.astype(F32)).astype(BF16)


def dot3(a, b, ca, cb):
    dims = (((ca,), (cb,)), ((), ()))
    ah, al = split(a)
    bh, bl = split(b)
    one = functools.partial(lax.dot_general, dimension_numbers=dims, preferred_element_type=F32)
    return one(ah, bh) + (one(ah, bl) + one(al, bh))


def gram_long(a):
    hi = a.astype(BF16).astype(F32)
    rest = a - hi
    mid = rest.astype(BF16).astype(F32)
    low = rest - mid
    lhs = jnp.concatenate([hi, hi, hi, mid, mid, low], axis=0).astype(BF16)
    rhs = jnp.concatenate([hi, mid, low, hi, mid, hi], axis=0).astype(BF16)
    return lax.dot_general(lhs, rhs, (((0,), (0,)), ((), ())), preferred_element_type=F32)


def invert_factor(m_ref, out_ref, prev, pan, between):
    lane = lax.broadcasted_iota(jnp.int32, (NB, BLK), 1)
    sub = lax.broadcasted_iota(jnp.int32, (NB, BLK), 0)
    lane_all = lax.broadcasted_iota(jnp.int32, (BLK, BLK), 1)
    eye = lax.broadcasted_iota(jnp.int32, (BLK, BLK), 0) == lane_all
    diagonal = jnp.where(eye, m_ref[...], 0.0)
    scale_row = lax.rsqrt(jnp.sum(diagonal, axis=0, keepdims=True))
    scale_col = lax.rsqrt(jnp.sum(diagonal, axis=1, keepdims=True))
    scaled = m_ref[...] * scale_col * scale_row
    m_ref[...] = scaled
    pan[...] = scaled[:NB]
    prev[...] = jnp.zeros_like(prev)

    def columns(rows, rel):
        return [
            jnp.broadcast_to(
                jnp.sum(jnp.where(rel == j, rows, 0.0), axis=1, keepdims=True), (NB, BLK)
            )
            for j in range(NB)
        ]

    def step(b, carry):
        for at, call in between:
            pl.when(b == at)(call)
        r0 = pl.multiple_of(b * NB, NB)
        after = pl.multiple_of(jnp.minimum(r0 + NB, BLK - NB), NB)
        rel = lane - r0
        inside = jnp.logical_and(rel >= 0, rel < NB)
        rel_all = lane_all - r0
        inside_before = jnp.logical_and(rel_all >= -NB, rel_all < 0)

        m_ref[...] = jnp.where(inside_before, 0.0, m_ref[...]) - gram_long(prev[...])

        rows = pan[...]
        cols = jnp.stack(columns(rows, rel))
        full = jnp.where(inside, jnp.where(rel == sub, 1.0, 0.0), rows)
        lower = full
        scale = jnp.zeros((NB, BLK), F32)
        for p in range(0, NB, 2):
            u1, u2 = cols[0], cols[1]
            a, e, d = u1[p : p + 1], u2[p : p + 1], u2[p + 1 : p + 2]
            det = a * d - e * e
            inv = pl.reciprocal(det, approx=True)
            inv = inv * (2.0 - det * inv)
            v1, v2 = d * u1 - e * u2, a * u2 - e * u1
            ia = 1.0 / a
            under = sub > p + 1
            w1, w2 = v1 * inv, v2 * inv
            l1 = jnp.where(under, w1, jnp.where(sub == p + 1, e * ia, 0.0))
            l2 = jnp.where(under, w2, 0.0)
            lower = lower - (l1 * lower[p : p + 1] + l2 * lower[p + 1 : p + 2])
            scale = jnp.where(sub == p, lax.rsqrt(a), scale)
            scale = jnp.where(sub == p + 1, lax.rsqrt(det * ia), scale)
            w1 = jnp.where(sub == p, 1.0 - d * inv, jnp.where(sub == p + 1, e * inv, w1))
            w2 = jnp.where(sub == p, e * inv, jnp.where(sub == p + 1, 1.0 - a * inv, w2))
            if p + 2 < NB:
                rest = cols[2:]
                cols = rest - (w1[None] * rest[:, p : p + 1] + w2[None] * rest[:, p + 1 : p + 2])
            full = full - (w1 * full[p : p + 1] + w2 * full[p + 1 : p + 2])
        lower = lower * scale
        prev[...] = lower
        out_ref[pl.ds(r0, NB), :] = lower * scale_row

        rows = m_ref[pl.ds(after, NB), :]
        terms = [m * full[j : j + 1] for j, m in enumerate(columns(rows, rel))]
        while len(terms) > 1:
            terms = [terms[i] + terms[i + 1] for i in range(0, len(terms), 2)]
        pan[...] = jnp.where(inside, 0.0, rows) - terms[0]
        return carry

    lax.fori_loop(0, BLK // NB, step, 0)


def kernel(
    mom_hbm, grad_hbm, basis_hbm, q_hbm, c_hbm, n_hbm,
    mom_ref, grad_ref, basis_ref, in_sem, b2, bsend, pown, poth, prcv, psum, pcomb, xrcv, pfull, halves, gp, zrcv, gz, yrcv, gown, gfull, g10,
    wp, wyrcv, wy, wzrcv, wfull, afac, xinv, mixed, mblk, iblk, prev, pan, qs, cs, sq, out_sem,
    s_pair, r_pair, s_xr, r_xr, s_xa, r_xa, s_zr, r_zr, s_y, r_y, s_gx, r_gx, s_gz, r_gz,
    s_wy, r_wy, s_wz, r_wz, s_wza, r_wza, s_wya, r_wya, s_end, r_end, s_n, r_n,
):
    f = lax.axis_index("fsdp")
    t = lax.axis_index("tensor")
    z, y = f // NY, f % NY
    x, c = t // 2, t % 2
    o = 1 - c

    pair = (f, x * 2 + o)

    def on_x(k):
        return (f, ((x + k + NX) % NX) * 2 + c)

    def on_y(k):
        return (z * NY + (y + k + NY) % NY, t)

    def on_z(k):
        return (((z + k) % NZ) * NY + y, t)

    s = 1 - 2 * c

    pending = []

    def make(src, dst, ssem, rsem, to):
        return pltpu.make_async_remote_copy(
            src_ref=src, dst_ref=dst, send_sem=ssem, recv_sem=rsem,
            device_id=to, device_id_type=MESH,
        )

    def send(*args):
        copy = make(*args)
        copy.start()
        pending.append(copy)
        return copy

    loads = [
        pltpu.make_async_copy(src, dst, in_sem.at[i])
        for i, (src, dst) in enumerate(
            (
                (mom_hbm, mom_ref),
                (grad_hbm, grad_ref),
                (basis_hbm.at[o], basis_ref.at[o]),
                (basis_hbm.at[c], basis_ref.at[c]),
            )
        )
    ]
    for load in loads:
        load.start()
    barrier = pltpu.get_barrier_semaphore()
    peers = [pair] + [on_x(k) for k in range(1, NX)]
    peers += [(f, ((x + k) % NX) * 2 + o) for k in range(1, NX)]
    peers += [on_y(k) for k in range(1, NY)] + [on_z(k) for k in range(1, NZ)]
    for peer in peers:
        pl.semaphore_signal(barrier, inc=1, device_id=peer, device_id_type=MESH)

    for load in loads[:3]:
        load.wait()
    bsend[...] = mom_ref[o] + grad_ref[o].astype(F32)
    p = dot3(bsend[...], basis_ref[o], 0, 0)
    for b in range(4):
        poth[b] = p[:, b * BLK : (b + 1) * BLK]
    pl.semaphore_wait(barrier, len(peers))
    cp = send(poth, prcv, s_pair.at[0], r_pair.at[0], pair)
    cb = send(bsend, b2.at[c], s_pair.at[1], r_pair.at[1], pair)
    own = mom_ref[c] + grad_ref[c].astype(F32)
    b2[c] = own
    loads[3].wait()
    p = dot3(own, basis_ref[c], 0, 0)
    for b in range(4):
        pown[b] = p[:, b * BLK : (b + 1) * BLK]
    cp.wait_recv()
    for b in range(4):
        psum[b] = pown[b] + prcv[b]

    def sum_start(parts, me, own, own_sem, rcv, rcv_sem, to):
        far = send(parts.at[(me + 2) % 4], rcv.at[0], own_sem.at[0], rcv_sem.at[0], to(s))
        near = send(parts.at[(me - s + 4) % 4], rcv.at[1], own_sem.at[1], rcv_sem.at[1], to(-s))
        return far, near

    def sum_relay(started, parts, me, own, own_sem, rcv, rcv_sem, to):
        started[0].wait_recv()
        own[...] = parts[(me + s + 4) % 4] + rcv[0]
        return started[1], send(own, rcv.at[2], own_sem.at[2], rcv_sem.at[2], to(s))

    def sum_end(started, parts, me, own, own_sem, rcv, rcv_sem, to):
        for copy in started:
            copy.wait_recv()
        return parts[me] + rcv[1] + rcv[2]

    def gather_start(slot, me, ssem, rsem, to):
        return [send(slot(me), slot(me), ssem.at[i], rsem.at[i], to(k)) for i, k in enumerate((s, -s))]

    def gather_relay(started, slot, me, ssem, rsem, to):
        here = slot((me - s + 4) % 4)
        return [started[1], send(here, here, ssem.at[2], rsem.at[2], to(s))]

    args = (psum, x, pcomb, s_xr, xrcv, r_xr, on_x)
    pfull[x] = sum_end(sum_relay(sum_start(*args), *args), *args)
    a_args = (lambda i: pfull.at[i], x, s_xa, r_xa, on_x)
    across = gather_start(*a_args)

    def rows8(k):
        return pl.ds(pl.multiple_of(((z + k) % NZ) * 8, 8), 8)

    first, rest = pl.ds(0, 2), pl.ds(2, 3)
    around = (4, 3, 5, 2, 6, 1, 7)

    def gram_z(part, n):
        return [
            send(
                gp.at[x, n, rows8(k), :], zrcv.at[k - 1, n],
                s_zr.at[part, k - 1], r_zr.at[part, k - 1], on_z(k),
            )
            for k in around
        ]

    def gram_y(part, n, before):
        for copy in before:
            copy.wait_recv()
        total = gp[x, n, rows8(0), :]
        for k in range(NZ - 1):
            total = total + zrcv[k, n]
        gz[n] = total
        return [
            send(gz.at[n], yrcv.at[k - 1, n], s_y.at[part, k - 1], r_y.at[part, k - 1], on_y(k))
            for k in (2, 1, 3)
        ]

    def gram_back_z(part, n):
        here = gfull.at[x, n, rows8(0), :]
        return [
            make(gown.at[n], here, s_gz.at[part, k - 1], r_gz.at[part, k - 1], on_z(k)) for k in around
        ]

    def gram_gather_z(part, n, before):
        for copy in before:
            copy.wait_recv()
        total = gz[n]
        for k in range(NY - 1):
            total = total + yrcv[k, n]
        gown[n] = total
        gfull[x, n, rows8(0), :] = total
        copies = gram_back_z(part, n)
        for copy in copies:
            copy.start()
        return copies

    w_rows = COLS // NZ

    def w_half(h):
        return pl.ds(h * COLS, COLS)

    def w_part(h, k):
        return pl.ds(pl.multiple_of(h * COLS + ((z + k) % NZ) * w_rows, 8), w_rows)

    opposite_first = (2, 1, 3)

    def w_y(h):
        rows = w_half(h)
        return [
            make(
                wp.at[(y + k) % NY, rows, :], wyrcv.at[k - 1, rows, :],
                s_wy.at[h, k - 1], r_wy.at[h, k - 1], on_y(k),
            )
            for k in opposite_first
        ]

    def w_z(h):
        return [
            make(wy.at[w_part(h, k), :], wzrcv.at[h, k - 1], s_wz.at[h, k - 1], r_wz.at[h, k - 1], on_z(k))
            for k in around
        ]

    def w_back_z(h):
        here = wfull.at[y, w_part(h, 0), :]
        return [make(here, here, s_wza.at[h, k - 1], r_wza.at[h, k - 1], on_z(k)) for k in around]

    def w_back_y(h):
        here = wfull.at[y, w_half(h), :]
        return [
            make(here, here, s_wya.at[h, k - 1], r_wya.at[h, k - 1], on_y(k)) for k in opposite_first
        ]

    def w_to_z(h):
        rows = w_half(h)
        for copy in w_y(h):
            copy.wait_recv()
        wy[rows, :] = wp[y, rows, :] + wyrcv[0, rows, :] + wyrcv[1, rows, :] + wyrcv[2, rows, :]
        for copy in w_z(h):
            copy.start()

    def w_from_z(h):
        for copy in w_z(h):
            copy.wait_recv()
        total = wy[w_part(h, 0), :]
        for k in range(NZ - 1):
            total = total + wzrcv[h, k]
        wfull[y, w_part(h, 0), :] = total
        for copy in w_back_z(h):
            copy.start()

    def w_to_y(h):
        for copy in w_back_z(h):
            copy.wait_recv()
        for copy in w_back_y(h):
            copy.start()

    def w_end(h):
        for copy in w_back_y(h):
            copy.wait_recv()

    g = dot6(pfull[x], pfull[x], 0, 0)
    for h in range(2):
        gp[x, h] = g[h * 64 : (h + 1) * 64]
    g0 = gram_z(0, first)
    across[0].wait_recv()
    far = gather_relay(across, *a_args)[1]
    across[1].wait_recv()
    g = dot6(pfull[x + 1 - x // 3], pfull[x % 3], 0, 0)
    for h in range(2):
        gp[x, 2 + h] = g[h * 64 : (h + 1) * 64]
    between_two = (x + 1) % 2
    g = dot6(pfull[between_two + 2], pfull[between_two], 0, 0)
    for h in range(2):
        halves[h] = g[h * 64 : (h + 1) * 64]
    gp[x, 4] = halves[x // 2]
    g1 = gram_z(1, rest)
    g0 = gram_y(0, first, g0)
    far.wait_recv()
    cb.wait_recv()
    for n, k in enumerate((*opposite_first, 0)):
        b = (y + k) % NY
        for h in range(2):
            wp[b, w_half(h), :] = dot3(b2[h], pfull[b], 1, 0)
            if n < 3:
                w_y(h)[n].start()
    g0 = gram_gather_z(0, first, g0)
    g1 = gram_y(1, rest, g1)
    for copy in g0:
        copy.wait_recv()

    def diagonals():
        here = gfull.at[x, first]
        return [make(here, here, s_gx.at[k + 2], r_gx.at[k + 2], on_x(k)) for k in (1, 3, 2)]

    def diagonal_from(chip):
        k = (x - chip + NX) % NX
        here = gfull.at[chip, first]
        return make(here, here, s_gx.at[k + 2], r_gx.at[k + 2], on_x(k))

    @pl.when(x == 0)
    def _():
        for copy in diagonals():
            copy.start()

    gram_gather_z(1, rest, g1)

    @pl.when(x != 0)
    def _():
        for copy in diagonals():
            copy.start()
        diagonal_from(0).wait_recv()

    def span(i, j):
        return slice(i * BLK, j * BLK)

    def rest_x():
        here = gfull.at[x, rest]
        other = gfull.at[(x - s + NX) % NX, rest]
        return (
            make(here, here, s_gx.at[0], r_gx.at[0], on_x(s)),
            make(here, here, s_gx.at[1], r_gx.at[1], on_x(-s)),
            make(other, other, s_gx.at[2], r_gx.at[2], on_x(s)),
        )

    def early():
        here = gfull.at[0, pl.ds(2, 2)]
        return [make(here, g10, s_gx.at[k + 5], r_gx.at[k + 5], on_x(k)) for k in (1, 3, 2)]

    def rest_near():
        for copy in gram_back_z(1, rest):
            copy.wait_recv()

        @pl.when(x == 0)
        def _():
            for copy in early():
                copy.start()
            g10[...] = gfull[0, 2:4]

        for copy in rest_x()[:2]:
            copy.start()

    def rest_far():
        rest_x()[0].wait_recv()
        rest_x()[2].start()

    def diagonal_end(chip):
        @pl.when(x != chip)
        def _():
            diagonal_from(chip).wait_recv()

    def early_end():
        @pl.when(x != 0)
        def _():
            here = gfull.at[0, pl.ds(2, 2)]
            make(here, g10, s_gx.at[x + 5], r_gx.at[x + 5], on_x(x)).wait_recv()

    def rest_end():
        diagonal_end(2)
        diagonal_end(3)
        for copy in rest_x()[1:]:
            copy.wait_recv()
        for i in range(2, 4):
            for j in range(i + 1):
                afac[span(i, i + 1), span(j, j + 1)] = load(i, j)
        panel = dot6(afac[span(2, 4), span(0, 1)], xinv[span(0, 1), span(0, 1)], 1, 1)
        afac[span(2, 4), span(0, 1)] = panel
        afac[span(2, 4), span(1, 2)] = afac[span(2, 4), span(1, 2)] - dot6(
            panel, afac[span(1, 2), span(0, 1)], 1, 1
        )

    def let_go():
        for copy in pending:
            copy.wait_send()
        pending.clear()

    def call(f, h):
        return functools.partial(f, h)

    between = [
        [(3, call(w_to_z, 0)), (4, rest_near), (6, call(w_to_z, 1)), (7, rest_far)],
        [(4, call(w_from_z, 0)), (6, call(w_from_z, 1)), (7, rest_end)],
        [(4, call(w_to_y, 0)), (6, call(w_to_y, 1))],
        [],
    ]

    def load(i, j):
        return jnp.concatenate([gfull[PLACE[(2 * i + h, j)]] for h in range(2)], axis=0)

    def lanes(b):
        return slice(b * BLK, (b + 1) * BLK)

    def half(i):
        return pl.ds(pl.multiple_of(i * COLS, 8), COLS)

    tril = lax.broadcasted_iota(jnp.int32, (BLK, BLK), 0) >= lax.broadcasted_iota(
        jnp.int32, (BLK, BLK), 1
    )
    xinv[...] = jnp.zeros_like(xinv)
    projected = jnp.concatenate([pfull[b] for b in range(4)], axis=1)
    mblk[...] = load(0, 0)
    for kb in range(4):
        here, below, done = span(kb, kb + 1), span(kb + 1, 4), span(0, kb + 1)
        invert_factor(mblk, iblk, prev, pan, between[kb])
        inv = jnp.where(tril, iblk[...], 0.0)
        xinv[here, here] = inv
        if kb == 0:
            early_end()
            diagonal_end(1)
            panel = dot6(g10[...].reshape(BLK, BLK), inv, 1, 1)
            afac[span(1, 2), here] = panel
            mblk[...] = load(1, 1) - dot6(panel, panel, 1, 1)
        if kb == 1:
            afac[below, here] = dot6(afac[below, here], inv, 1, 1)
            left = afac[below, done]
            mblk[...] = afac[span(2, 3), span(2, 3)] - dot6(left[:BLK], left[:BLK], 1, 1)
            under = afac[span(3, 4), span(2, 4)] - dot6(left[BLK:], left, 1, 1)
            afac[span(3, 4), span(2, 4)] = under
        if kb == 2:
            panel = dot6(afac[below, here], inv, 1, 1)
            afac[below, here] = panel
            mblk[...] = afac[below, below] - dot6(panel, panel, 1, 1)
        if kb > 0:
            xinv[here, span(0, kb)] = -dot3(inv, mixed[:, span(0, kb)], 1, 0)
        if kb < 3:
            mixed[:, done] = dot3(afac[span(kb + 1, kb + 2), done], xinv[done, done], 1, 0)
        qs[:, lanes(kb)] = dot3(projected[:, done], xinv[here, done], 1, 1)
        if kb == 1:
            let_go()
    ends = [
        send(qs, q_hbm.at[c], s_end.at[0], r_end.at[0], pair),
        make(cs.at[half(o), :], c_hbm.at[c], s_end.at[1], r_end.at[1], pair),
    ]
    stores = [
        pltpu.make_async_copy(qs, q_hbm.at[c], out_sem.at[0]),
        pltpu.make_async_copy(cs.at[half(c), :], c_hbm.at[c], out_sem.at[1]),
        pltpu.make_async_copy(sq, n_hbm.at[c, x], out_sem.at[2]),
    ]
    stores[0].start()
    for h in range(2):
        w_end(h)
        rows = w_half(h)
        w = jnp.concatenate([wfull[b, rows, :] for b in range(4)], axis=1)
        for kb in range(4):
            done = span(0, kb + 1)
            cs[rows, lanes(kb)] = dot3(w[:, done], xinv[span(kb, kb + 1), done], 1, 1)
    ends[1].start()
    stores[1].start()
    sq[...] = jnp.sum(cs[...] * cs[...], axis=0, keepdims=True)
    stores[2].start()
    sums = [
        send(sq, n_hbm.at[c, x], s_n.at[i], r_n.at[i], to)
        for i, to in enumerate(
            [on_x(2), on_x(1), on_x(3)]
            + [(f, ((x + k) % NX) * 2 + o) for k in (2, 1, 3, 0)]
        )
    ]
    for copy in pending[:-len(sums)]:
        copy.wait_send()
    @pl.when(x == 0)
    def _():
        for copy in early():
            copy.wait_send()

    for copy in diagonals() + list(rest_x()) + gram_back_z(0, first) + gram_back_z(1, rest):
        copy.wait_send()
    for h in range(2):
        for copy in list(w_y(h)) + w_z(h) + w_back_z(h) + list(w_back_y(h)):
            copy.wait_send()
    for copy in ends + sums:
        copy.wait_recv()
    ends[1].wait_send()
    for copy in sums:
        copy.wait_send()
    for store in stores:
        store.wait()


def finish(mom_ref, grad_ref, q_ref, c_ref, n_ref, nm_ref, nb_ref, up_ref):
    for m in range(2):
        q, coeffs = q_ref[m], c_ref[m]
        error = lax.dot_general(
            coeffs.astype(BF16), q.astype(BF16), (((1,), (1,)), ((), ())), preferred_element_type=F32
        )
        nm_ref[m] = mom_ref[m] + grad_ref[m].astype(F32) - 0.05 * error
        basis = coeffs * lax.rsqrt(n_ref[m, 0] + n_ref[m, 1] + n_ref[m, 2] + n_ref[m, 3] + 1e-06)
        nb_ref[m] = basis
        up_ref[m] = (math.sqrt(D * FF / RANK) * dot3(basis, q, 1, 1)).astype(BF16)


def on_device(momentum, grad, basis):
    vm = pltpu.VMEM
    chunk = (4, BLK, BLK)
    scratch = [
        vm((2, COLS, ROWS), F32), vm((2, COLS, ROWS), BF16), vm((2, COLS, RANK), F32),
        pltpu.SemaphoreType.DMA((4,)),
        vm((2, COLS, ROWS), F32), vm((COLS, ROWS), F32),
        vm(chunk, F32), vm(chunk, F32), vm(chunk, F32), vm(chunk, F32),
        vm((BLK, BLK), F32), vm((3, BLK, BLK), F32), vm(chunk, F32),
        vm((2, 64, BLK), F32),
        vm((4, 5, 64, BLK), F32), vm((7, 5, 8, BLK), F32), vm((5, 8, BLK), F32),
        vm((3, 5, 8, BLK), F32), vm((5, 8, BLK), F32), vm((4, 5, 64, BLK), F32), vm((2, 64, BLK), F32),
        vm((4, 2 * COLS, BLK), F32),
        vm((3, 2 * COLS, BLK), F32), vm((2 * COLS, BLK), F32),
        vm((2, 7, COLS // NZ, BLK), F32), vm((4, 2 * COLS, BLK), F32),
        vm((RANK, RANK), F32), vm((RANK, RANK), F32), vm((BLK, RANK), F32),
        *[vm((BLK, BLK), F32)] * 2, *[vm((NB, BLK), F32)] * 2,
        vm((ROWS, RANK), F32), vm((2 * COLS, RANK), F32),
        vm((1, RANK), F32),
        pltpu.SemaphoreType.DMA((3,)),
    ]
    for n in (2, 3, 3, (2, 7), (2, 3), 9, (2, 7), (2, 3), (2, 7), (2, 7), (2, 3), 2, 7):
        shape = n if isinstance(n, tuple) else (n,)
        scratch += [pltpu.SemaphoreType.DMA(shape), pltpu.SemaphoreType.DMA(shape)]
    hbm = pl.BlockSpec(memory_space=pl.ANY)
    momentum, grad = jnp.swapaxes(momentum, 1, 2), jnp.swapaxes(grad, 1, 2)
    q, coeffs, sums = pl.pallas_call(
        kernel,
        out_shape=(
            jax.ShapeDtypeStruct((2, ROWS, RANK), F32),
            jax.ShapeDtypeStruct((2, COLS, RANK), F32),
            jax.ShapeDtypeStruct((2, NX, 1, RANK), F32),
        ),
        in_specs=[hbm] * 3,
        out_specs=(hbm,) * 3,
        scratch_shapes=scratch,
        compiler_params=pltpu.CompilerParams(
            collective_id=0, has_side_effects=True, vmem_limit_bytes=58 * 2**20
        ),
    )(momentum, grad, basis)

    def both(*shape):
        return pl.BlockSpec((2, *shape), lambda i: (0,) * (len(shape) + 1))

    nm, nb, up = pl.pallas_call(
        finish,
        grid=(1,),
        out_shape=(
            jax.ShapeDtypeStruct((2, COLS, ROWS), F32),
            jax.ShapeDtypeStruct((2, COLS, RANK), F32),
            jax.ShapeDtypeStruct((2, COLS, ROWS), BF16),
        ),
        in_specs=[both(COLS, ROWS), both(COLS, ROWS), both(ROWS, RANK), both(COLS, RANK), both(NX, 1, RANK)],
        out_specs=(both(COLS, ROWS), both(COLS, RANK), both(COLS, ROWS)),
        compiler_params=pltpu.CompilerParams(vmem_limit_bytes=58 * 2**20),
    )(momentum, grad, q, coeffs, sums)
    return jnp.swapaxes(nm, 1, 2), nb, jnp.swapaxes(up, 1, 2)


def solution(mesh):
    in_specs = (P(None, "fsdp", "tensor"), P(None, "fsdp", "tensor"), P(None, "tensor", None))
    out_specs = (P(None, "fsdp", "tensor"), P(None, "tensor", None), P(None, "fsdp", "tensor"))
    return jax.shard_map(
        on_device, mesh=mesh, in_specs=in_specs, out_specs=out_specs, check_vma=False
    )
```

```python
import functools
import math

import jax
import jax.numpy as jnp
from jax import lax
from jax.experimental import pallas as pl
from jax.experimental.pallas import tpu as pltpu
from jax.sharding import PartitionSpec as P

D = 4096
FF = 1536
RANK = 512
NX, NY, NZ = 4, 4, 8
ROWS = 128
COLS = 192
BLK = 128
NB = 16
F32 = jnp.float32
BF16 = jnp.bfloat16
HIGHEST = lax.Precision.HIGHEST
MESH = pl.DeviceIdType.MESH

PLACE = {(2 * x + h, x): (x, h) for x in range(NX) for h in range(2)}
PLACE.update({(2 * (x + 1 - x // 3) + h, x % 3): (x, 2 + h) for x in range(NX) for h in range(2)})
PLACE.update({(2 * (2 + (x + 1) % 2) + x // 2, (x + 1) % 2): (x, 4) for x in range(NX)})


def dot6(a, b, ca, cb):
    return lax.dot_general(
        a, b, (((ca,), (cb,)), ((), ())), precision=HIGHEST, preferred_element_type=F32
    )


def split(a):
    hi = a.astype(BF16)
    return hi, (a - hi.astype(F32)).astype(BF16)


def dot3(a, b, ca, cb):
    dims = (((ca,), (cb,)), ((), ()))
    ah, al = split(a)
    bh, bl = split(b)
    one = functools.partial(lax.dot_general, dimension_numbers=dims, preferred_element_type=F32)
    return one(ah, bh) + (one(ah, bl) + one(al, bh))


def gram_long(a):
    hi = a.astype(BF16).astype(F32)
    rest = a - hi
    mid = rest.astype(BF16).astype(F32)
    low = rest - mid
    lhs = jnp.concatenate([hi, hi, hi, mid, mid, low], axis=0).astype(BF16)
    rhs = jnp.concatenate([hi, mid, low, hi, mid, hi], axis=0).astype(BF16)
    return lax.dot_general(lhs, rhs, (((0,), (0,)), ((), ())), preferred_element_type=F32)


def invert_factor(m_ref, out_ref, prev, pan, between):
    lane = lax.broadcasted_iota(jnp.int32, (NB, BLK), 1)
    sub = lax.broadcasted_iota(jnp.int32, (NB, BLK), 0)
    lane_all = lax.broadcasted_iota(jnp.int32, (BLK, BLK), 1)
    eye = lax.broadcasted_iota(jnp.int32, (BLK, BLK), 0) == lane_all
    diagonal = jnp.where(eye, m_ref[...], 0.0)
    scale_row = lax.rsqrt(jnp.sum(diagonal, axis=0, keepdims=True))
    scale_col = lax.rsqrt(jnp.sum(diagonal, axis=1, keepdims=True))
    scaled = m_ref[...] * scale_col * scale_row
    m_ref[...] = scaled
    pan[...] = scaled[:NB]
    prev[...] = jnp.zeros_like(prev)

    def columns(rows, rel):
        return [
            jnp.broadcast_to(
                jnp.sum(jnp.where(rel == j, rows, 0.0), axis=1, keepdims=True), (NB, BLK)
            )
            for j in range(NB)
        ]

    def step(b, carry):
        for at, call in between:
            pl.when(b == at)(call)
        r0 = pl.multiple_of(b * NB, NB)
        after = pl.multiple_of(jnp.minimum(r0 + NB, BLK - NB), NB)
        rel = lane - r0
        inside = jnp.logical_and(rel >= 0, rel < NB)
        rel_all = lane_all - r0
        inside_before = jnp.logical_and(rel_all >= -NB, rel_all < 0)

        m_ref[...] = jnp.where(inside_before, 0.0, m_ref[...]) - gram_long(prev[...])

        rows = pan[...]
        cols = jnp.stack(columns(rows, rel))
        full = jnp.where(inside, jnp.where(rel == sub, 1.0, 0.0), rows)
        lower = full
        scale = jnp.zeros((NB, BLK), F32)
        for p in range(0, NB, 2):
            u1, u2 = cols[0], cols[1]
            a, e, d = u1[p : p + 1], u2[p : p + 1], u2[p + 1 : p + 2]
            det = a * d - e * e
            inv = pl.reciprocal(det, approx=True)
            inv = inv * (2.0 - det * inv)
            v1, v2 = d * u1 - e * u2, a * u2 - e * u1
            ia = 1.0 / a
            under = sub > p + 1
            w1, w2 = v1 * inv, v2 * inv
            l1 = jnp.where(under, w1, jnp.where(sub == p + 1, e * ia, 0.0))
            l2 = jnp.where(under, w2, 0.0)
            lower = lower - (l1 * lower[p : p + 1] + l2 * lower[p + 1 : p + 2])
            scale = jnp.where(sub == p, lax.rsqrt(a), scale)
            scale = jnp.where(sub == p + 1, lax.rsqrt(det * ia), scale)
            w1 = jnp.where(sub == p, 1.0 - d * inv, jnp.where(sub == p + 1, e * inv, w1))
            w2 = jnp.where(sub == p, e * inv, jnp.where(sub == p + 1, 1.0 - a * inv, w2))
            if p + 2 < NB:
                rest = cols[2:]
                cols = rest - (w1[None] * rest[:, p : p + 1] + w2[None] * rest[:, p + 1 : p + 2])
            full = full - (w1 * full[p : p + 1] + w2 * full[p + 1 : p + 2])
        lower = lower * scale
        prev[...] = lower
        out_ref[pl.ds(r0, NB), :] = lower * scale_row

        rows = m_ref[pl.ds(after, NB), :]
        terms = [m * full[j : j + 1] for j, m in enumerate(columns(rows, rel))]
        while len(terms) > 1:
            terms = [terms[i] + terms[i + 1] for i in range(0, len(terms), 2)]
        pan[...] = jnp.where(inside, 0.0, rows) - terms[0]
        return carry

    lax.fori_loop(0, BLK // NB, step, 0)


def kernel(
    mom_hbm, grad_hbm, basis_hbm, q_hbm, c_hbm, n_hbm,
    mom_ref, grad_ref, basis_ref, in_sem, b2, bsend, pown, poth, prcv, psum, pcomb, xrcv, pfull, halves, gp, zrcv, gz, yrcv, gown, gfull, g10,
    wp, wyrcv, wy, wzrcv, wfull, afac, xinv, mixed, mblk, iblk, prev, pan, qs, cs, sq, out_sem,
    s_pair, r_pair, s_xr, r_xr, s_xa, r_xa, s_zr, r_zr, s_y, r_y, s_gx, r_gx, s_gz, r_gz,
    s_wy, r_wy, s_wz, r_wz, s_wza, r_wza, s_wya, r_wya, s_end, r_end, s_n, r_n,
):
    f = lax.axis_index("fsdp")
    t = lax.axis_index("tensor")
    z, y = f // NY, f % NY
    x, c = t // 2, t % 2
    o = 1 - c

    pair = (f, x * 2 + o)

    def on_x(k):
        return (f, ((x + k + NX) % NX) * 2 + c)

    def on_y(k):
        return (z * NY + (y + k + NY) % NY, t)

    def on_z(k):
        return (((z + k) % NZ) * NY + y, t)

    s = 1 - 2 * c

    pending = []

    def make(src, dst, ssem, rsem, to):
        return pltpu.make_async_remote_copy(
            src_ref=src, dst_ref=dst, send_sem=ssem, recv_sem=rsem,
            device_id=to, device_id_type=MESH,
        )

    def send(*args):
        copy = make(*args)
        copy.start()
        pending.append(copy)
        return copy

    loads = [
        pltpu.make_async_copy(src, dst, in_sem.at[i])
        for i, (src, dst) in enumerate(
            (
                (mom_hbm, mom_ref),
                (grad_hbm, grad_ref),
                (basis_hbm.at[o], basis_ref.at[o]),
                (basis_hbm.at[c], basis_ref.at[c]),
            )
        )
    ]
    for load in loads:
        load.start()
    barrier = pltpu.get_barrier_semaphore()
    peers = [pair] + [on_x(k) for k in range(1, NX)]
    peers += [(f, ((x + k) % NX) * 2 + o) for k in range(1, NX)]
    peers += [on_y(k) for k in range(1, NY)] + [on_z(k) for k in range(1, NZ)]
    for peer in peers:
        pl.semaphore_signal(barrier, inc=1, device_id=peer, device_id_type=MESH)

    for load in loads[:3]:
        load.wait()
    bsend[...] = mom_ref[o] + grad_ref[o].astype(F32)
    pl.semaphore_wait(barrier, len(peers))
    chunks = []
    for k in (2, 1, 3, 0):
        b = (x + k) % NX
        at = pl.ds(pl.multiple_of(b * BLK, BLK), BLK)
        poth[b] = dot3(bsend[...], basis_ref[o, :, at], 0, 0)
        chunks.append(send(poth.at[b], prcv.at[b], s_pair.at[1 + k], r_pair.at[1 + k], pair))
    cb = send(bsend, b2.at[c], s_pair.at[0], r_pair.at[0], pair)
    own = mom_ref[c] + grad_ref[c].astype(F32)
    b2[c] = own
    loads[3].wait()
    p = dot3(own, basis_ref[c], 0, 0)
    for b in range(4):
        pown[b] = p[:, b * BLK : (b + 1) * BLK]
    for k, copy in zip((2, 1, 3, 0), chunks, strict=True):
        copy.wait_recv()
        b = (x + k) % NX
        psum[b] = pown[b] + prcv[b]

    def sum_start(parts, me, own, own_sem, rcv, rcv_sem, to):
        far = send(parts.at[(me + 2) % 4], rcv.at[0], own_sem.at[0], rcv_sem.at[0], to(s))
        near = send(parts.at[(me - s + 4) % 4], rcv.at[1], own_sem.at[1], rcv_sem.at[1], to(-s))
        return far, near

    def sum_relay(started, parts, me, own, own_sem, rcv, rcv_sem, to):
        started[0].wait_recv()
        own[...] = parts[(me + s + 4) % 4] + rcv[0]
        return started[1], send(own, rcv.at[2], own_sem.at[2], rcv_sem.at[2], to(s))

    def sum_end(started, parts, me, own, own_sem, rcv, rcv_sem, to):
        for copy in started:
            copy.wait_recv()
        return parts[me] + rcv[1] + rcv[2]

    def gather_start(slot, me, ssem, rsem, to):
        return [send(slot(me), slot(me), ssem.at[i], rsem.at[i], to(k)) for i, k in enumerate((s, -s))]

    def gather_relay(started, slot, me, ssem, rsem, to):
        here = slot((me - s + 4) % 4)
        return [started[1], send(here, here, ssem.at[2], rsem.at[2], to(s))]

    args = (psum, x, pcomb, s_xr, xrcv, r_xr, on_x)
    pfull[x] = sum_end(sum_relay(sum_start(*args), *args), *args)
    a_args = (lambda i: pfull.at[i], x, s_xa, r_xa, on_x)
    across = gather_start(*a_args)

    def rows8(k):
        return pl.ds(pl.multiple_of(((z + k) % NZ) * 8, 8), 8)

    first, rest = pl.ds(0, 2), pl.ds(2, 3)
    around = (4, 3, 5, 2, 6, 1, 7)

    def gram_z(part, n):
        return [
            send(
                gp.at[x, n, rows8(k), :], zrcv.at[k - 1, n],
                s_zr.at[part, k - 1], r_zr.at[part, k - 1], on_z(k),
            )
            for k in around
        ]

    def gram_y(part, n, before):
        for copy in before:
            copy.wait_recv()
        total = gp[x, n, rows8(0), :]
        for k in range(NZ - 1):
            total = total + zrcv[k, n]
        gz[n] = total
        return [
            send(gz.at[n], yrcv.at[k - 1, n], s_y.at[part, k - 1], r_y.at[part, k - 1], on_y(k))
            for k in (2, 1, 3)
        ]

    def gram_back_z(part, n):
        here = gfull.at[x, n, rows8(0), :]
        return [
            make(gown.at[n], here, s_gz.at[part, k - 1], r_gz.at[part, k - 1], on_z(k)) for k in around
        ]

    def gram_gather_z(part, n, before):
        for copy in before:
            copy.wait_recv()
        total = gz[n]
        for k in range(NY - 1):
            total = total + yrcv[k, n]
        gown[n] = total
        gfull[x, n, rows8(0), :] = total
        copies = gram_back_z(part, n)
        for copy in copies:
            copy.start()
        return copies

    w_rows = COLS // NZ

    def w_half(h):
        return pl.ds(h * COLS, COLS)

    def w_part(h, k):
        return pl.ds(pl.multiple_of(h * COLS + ((z + k) % NZ) * w_rows, 8), w_rows)

    opposite_first = (2, 1, 3)

    def w_y(h):
        rows = w_half(h)
        return [
            make(
                wp.at[(y + k) % NY, rows, :], wyrcv.at[k - 1, rows, :],
                s_wy.at[h, k - 1], r_wy.at[h, k - 1], on_y(k),
            )
            for k in opposite_first
        ]

    def w_z(h):
        return [
            make(wy.at[w_part(h, k), :], wzrcv.at[h, k - 1], s_wz.at[h, k - 1], r_wz.at[h, k - 1], on_z(k))
            for k in around
        ]

    def w_back_z(h):
        here = wfull.at[y, w_part(h, 0), :]
        return [make(here, here, s_wza.at[h, k - 1], r_wza.at[h, k - 1], on_z(k)) for k in around]

    def w_back_y(h):
        here = wfull.at[y, w_half(h), :]
        return [
            make(here, here, s_wya.at[h, k - 1], r_wya.at[h, k - 1], on_y(k)) for k in opposite_first
        ]

    def w_to_z(h):
        rows = w_half(h)
        for copy in w_y(h):
            copy.wait_recv()
        wy[rows, :] = wp[y, rows, :] + wyrcv[0, rows, :] + wyrcv[1, rows, :] + wyrcv[2, rows, :]
        for copy in w_z(h):
            copy.start()

    def w_from_z(h):
        for copy in w_z(h):
            copy.wait_recv()
        total = wy[w_part(h, 0), :]
        for k in range(NZ - 1):
            total = total + wzrcv[h, k]
        wfull[y, w_part(h, 0), :] = total
        for copy in w_back_z(h):
            copy.start()

    def w_to_y(h):
        for copy in w_back_z(h):
            copy.wait_recv()
        for copy in w_back_y(h):
            copy.start()

    def w_end(h):
        for copy in w_back_y(h):
            copy.wait_recv()

    g = dot6(pfull[x], pfull[x], 0, 0)
    for h in range(2):
        gp[x, h] = g[h * 64 : (h + 1) * 64]
    g0 = gram_z(0, first)
    across[0].wait_recv()
    far = gather_relay(across, *a_args)[1]
    across[1].wait_recv()
    g = dot6(pfull[x + 1 - x // 3], pfull[x % 3], 0, 0)
    for h in range(2):
        gp[x, 2 + h] = g[h * 64 : (h + 1) * 64]
    between_two = (x + 1) % 2
    g = dot6(pfull[between_two + 2], pfull[between_two], 0, 0)
    for h in range(2):
        halves[h] = g[h * 64 : (h + 1) * 64]
    gp[x, 4] = halves[x // 2]
    g1 = gram_z(1, rest)
    g0 = gram_y(0, first, g0)
    far.wait_recv()
    cb.wait_recv()
    for n, k in enumerate((*opposite_first, 0)):
        b = (y + k) % NY
        for h in range(2):
            wp[b, w_half(h), :] = dot3(b2[h], pfull[b], 1, 0)
            if n < 3:
                w_y(h)[n].start()
    g0 = gram_gather_z(0, first, g0)
    g1 = gram_y(1, rest, g1)
    for copy in g0:
        copy.wait_recv()

    def diagonals():
        here = gfull.at[x, first]
        return [make(here, here, s_gx.at[k + 2], r_gx.at[k + 2], on_x(k)) for k in (1, 3, 2)]

    def diagonal_from(chip):
        k = (x - chip + NX) % NX
        here = gfull.at[chip, first]
        return make(here, here, s_gx.at[k + 2], r_gx.at[k + 2], on_x(k))

    @pl.when(x == 0)
    def _():
        for copy in diagonals():
            copy.start()

    gram_gather_z(1, rest, g1)

    @pl.when(x != 0)
    def _():
        for copy in diagonals():
            copy.start()
        diagonal_from(0).wait_recv()

    def span(i, j):
        return slice(i * BLK, j * BLK)

    def rest_x():
        here = gfull.at[x, rest]
        other = gfull.at[(x - s + NX) % NX, rest]
        return (
            make(here, here, s_gx.at[0], r_gx.at[0], on_x(s)),
            make(here, here, s_gx.at[1], r_gx.at[1], on_x(-s)),
            make(other, other, s_gx.at[2], r_gx.at[2], on_x(s)),
        )

    def early():
        here = gfull.at[0, pl.ds(2, 2)]
        return [make(here, g10, s_gx.at[k + 5], r_gx.at[k + 5], on_x(k)) for k in (1, 3, 2)]

    def rest_near():
        for copy in gram_back_z(1, rest):
            copy.wait_recv()

        @pl.when(x == 0)
        def _():
            for copy in early():
                copy.start()
            g10[...] = gfull[0, 2:4]

        for copy in rest_x()[:2]:
            copy.start()

    def rest_far():
        rest_x()[0].wait_recv()
        rest_x()[2].start()

    def diagonal_end(chip):
        @pl.when(x != chip)
        def _():
            diagonal_from(chip).wait_recv()

    def early_end():
        @pl.when(x != 0)
        def _():
            here = gfull.at[0, pl.ds(2, 2)]
            make(here, g10, s_gx.at[x + 5], r_gx.at[x + 5], on_x(x)).wait_recv()

    def rest_end():
        diagonal_end(2)
        diagonal_end(3)
        for copy in rest_x()[1:]:
            copy.wait_recv()
        for i in range(2, 4):
            for j in range(i + 1):
                afac[span(i, i + 1), span(j, j + 1)] = load(i, j)
        panel = dot6(afac[span(2, 4), span(0, 1)], xinv[span(0, 1), span(0, 1)], 1, 1)
        afac[span(2, 4), span(0, 1)] = panel
        afac[span(2, 4), span(1, 2)] = afac[span(2, 4), span(1, 2)] - dot6(
            panel, afac[span(1, 2), span(0, 1)], 1, 1
        )

    def let_go():
        for copy in pending:
            copy.wait_send()
        pending.clear()

    def call(f, h):
        return functools.partial(f, h)

    between = [
        [(2, call(w_to_z, 0)), (4, rest_near), (5, call(w_to_z, 1)), (7, rest_far)],
        [(2, call(w_from_z, 0)), (5, call(w_from_z, 1)), (7, rest_end)],
        [(3, call(w_to_y, 0)), (6, call(w_to_y, 1))],
        [],
    ]

    def load(i, j):
        return jnp.concatenate([gfull[PLACE[(2 * i + h, j)]] for h in range(2)], axis=0)

    def lanes(b):
        return slice(b * BLK, (b + 1) * BLK)

    def half(i):
        return pl.ds(pl.multiple_of(i * COLS, 8), COLS)

    tril = lax.broadcasted_iota(jnp.int32, (BLK, BLK), 0) >= lax.broadcasted_iota(
        jnp.int32, (BLK, BLK), 1
    )
    xinv[...] = jnp.zeros_like(xinv)
    projected = jnp.concatenate([pfull[b] for b in range(4)], axis=1)
    mblk[...] = load(0, 0)
    for kb in range(4):
        here, below, done = span(kb, kb + 1), span(kb + 1, 4), span(0, kb + 1)
        invert_factor(mblk, iblk, prev, pan, between[kb])
        inv = jnp.where(tril, iblk[...], 0.0)
        xinv[here, here] = inv
        if kb == 0:
            early_end()
            diagonal_end(1)
            panel = dot6(g10[...].reshape(BLK, BLK), inv, 1, 1)
            afac[span(1, 2), here] = panel
            mblk[...] = load(1, 1) - dot6(panel, panel, 1, 1)
        if kb == 1:
            afac[below, here] = dot6(afac[below, here], inv, 1, 1)
            left = afac[below, done]
            mblk[...] = afac[span(2, 3), span(2, 3)] - dot6(left[:BLK], left[:BLK], 1, 1)
            under = afac[span(3, 4), span(2, 4)] - dot6(left[BLK:], left, 1, 1)
            afac[span(3, 4), span(2, 4)] = under
        if kb == 2:
            panel = dot6(afac[below, here], inv, 1, 1)
            afac[below, here] = panel
            mblk[...] = afac[below, below] - dot6(panel, panel, 1, 1)
        if kb > 0:
            xinv[here, span(0, kb)] = -dot3(inv, mixed[:, span(0, kb)], 1, 0)
        if kb < 3:
            mixed[:, done] = dot3(afac[span(kb + 1, kb + 2), done], xinv[done, done], 1, 0)
        qs[:, lanes(kb)] = dot3(projected[:, done], xinv[here, done], 1, 1)
        if kb == 1:
            let_go()
    ends = [
        send(qs, q_hbm.at[c], s_end.at[0], r_end.at[0], pair),
        make(cs.at[half(o), :], c_hbm.at[c], s_end.at[1], r_end.at[1], pair),
    ]
    stores = [
        pltpu.make_async_copy(qs, q_hbm.at[c], out_sem.at[0]),
        pltpu.make_async_copy(cs.at[half(c), :], c_hbm.at[c], out_sem.at[1]),
        pltpu.make_async_copy(sq, n_hbm.at[c, x], out_sem.at[2]),
    ]
    stores[0].start()
    for h in range(2):
        w_end(h)
        rows = w_half(h)
        w = jnp.concatenate([wfull[b, rows, :] for b in range(4)], axis=1)
        for kb in range(4):
            done = span(0, kb + 1)
            cs[rows, lanes(kb)] = dot3(w[:, done], xinv[span(kb, kb + 1), done], 1, 1)
    ends[1].start()
    stores[1].start()
    sq[...] = jnp.sum(cs[...] * cs[...], axis=0, keepdims=True)
    stores[2].start()
    sums = [
        send(sq, n_hbm.at[c, x], s_n.at[i], r_n.at[i], to)
        for i, to in enumerate(
            [on_x(2), on_x(1), on_x(3)]
            + [(f, ((x + k) % NX) * 2 + o) for k in (2, 1, 3, 0)]
        )
    ]
    for copy in pending[:-len(sums)]:
        copy.wait_send()
    @pl.when(x == 0)
    def _():
        for copy in early():
            copy.wait_send()

    for copy in diagonals() + list(rest_x()) + gram_back_z(0, first) + gram_back_z(1, rest):
        copy.wait_send()
    for h in range(2):
        for copy in list(w_y(h)) + w_z(h) + w_back_z(h) + list(w_back_y(h)):
            copy.wait_send()
    for copy in ends + sums:
        copy.wait_recv()
    ends[1].wait_send()
    for copy in sums:
        copy.wait_send()
    for store in stores:
        store.wait()


def finish(mom_ref, grad_ref, q_ref, c_ref, n_ref, nm_ref, nb_ref, up_ref):
    q, coeffs = q_ref[0], c_ref[0]
    error = lax.dot_general(
        coeffs.astype(BF16), q.astype(BF16), (((1,), (1,)), ((), ())), preferred_element_type=F32
    )
    nm_ref[0] = mom_ref[0] + grad_ref[0].astype(F32) - 0.05 * error
    basis = coeffs * lax.rsqrt(n_ref[0, 0] + n_ref[0, 1] + n_ref[0, 2] + n_ref[0, 3] + 1e-06)
    nb_ref[0] = basis
    up_ref[0] = (math.sqrt(D * FF / RANK) * dot3(basis, q, 1, 1)).astype(BF16)


def on_device(momentum, grad, basis):
    vm = pltpu.VMEM
    chunk = (4, BLK, BLK)
    scratch = [
        vm((2, COLS, ROWS), F32), vm((2, COLS, ROWS), BF16), vm((2, COLS, RANK), F32),
        pltpu.SemaphoreType.DMA((4,)),
        vm((2, COLS, ROWS), F32), vm((COLS, ROWS), F32),
        vm(chunk, F32), vm(chunk, F32), vm(chunk, F32), vm(chunk, F32),
        vm((BLK, BLK), F32), vm((3, BLK, BLK), F32), vm(chunk, F32),
        vm((2, 64, BLK), F32),
        vm((4, 5, 64, BLK), F32), vm((7, 5, 8, BLK), F32), vm((5, 8, BLK), F32),
        vm((3, 5, 8, BLK), F32), vm((5, 8, BLK), F32), vm((4, 5, 64, BLK), F32), vm((2, 64, BLK), F32),
        vm((4, 2 * COLS, BLK), F32),
        vm((3, 2 * COLS, BLK), F32), vm((2 * COLS, BLK), F32),
        vm((2, 7, COLS // NZ, BLK), F32), vm((4, 2 * COLS, BLK), F32),
        vm((RANK, RANK), F32), vm((RANK, RANK), F32), vm((BLK, RANK), F32),
        *[vm((BLK, BLK), F32)] * 2, *[vm((NB, BLK), F32)] * 2,
        vm((ROWS, RANK), F32), vm((2 * COLS, RANK), F32),
        vm((1, RANK), F32),
        pltpu.SemaphoreType.DMA((3,)),
    ]
    for n in (5, 3, 3, (2, 7), (2, 3), 9, (2, 7), (2, 3), (2, 7), (2, 7), (2, 3), 2, 7):
        shape = n if isinstance(n, tuple) else (n,)
        scratch += [pltpu.SemaphoreType.DMA(shape), pltpu.SemaphoreType.DMA(shape)]
    hbm = pl.BlockSpec(memory_space=pl.ANY)
    momentum, grad = jnp.swapaxes(momentum, 1, 2), jnp.swapaxes(grad, 1, 2)
    q, coeffs, sums = pl.pallas_call(
        kernel,
        out_shape=(
            jax.ShapeDtypeStruct((2, ROWS, RANK), F32),
            jax.ShapeDtypeStruct((2, COLS, RANK), F32),
            jax.ShapeDtypeStruct((2, NX, 1, RANK), F32),
        ),
        in_specs=[hbm] * 3,
        out_specs=(hbm,) * 3,
        scratch_shapes=scratch,
        compiler_params=pltpu.CompilerParams(
            collective_id=0, has_side_effects=True, vmem_limit_bytes=58 * 2**20
        ),
    )(momentum, grad, basis)

    def one(*shape):
        return pl.BlockSpec((1, *shape), lambda i: (i,) + (0,) * len(shape))

    nm, nb, up = pl.pallas_call(
        finish,
        grid=(2,),
        out_shape=(
            jax.ShapeDtypeStruct((2, COLS, ROWS), F32),
            jax.ShapeDtypeStruct((2, COLS, RANK), F32),
            jax.ShapeDtypeStruct((2, COLS, ROWS), BF16),
        ),
        in_specs=[one(COLS, ROWS), one(COLS, ROWS), one(ROWS, RANK), one(COLS, RANK), one(NX, 1, RANK)],
        out_specs=(one(COLS, ROWS), one(COLS, RANK), one(COLS, ROWS)),
        compiler_params=pltpu.CompilerParams(vmem_limit_bytes=58 * 2**20),
    )(momentum, grad, q, coeffs, sums)
    return jnp.swapaxes(nm, 1, 2), nb, jnp.swapaxes(up, 1, 2)


def solution(mesh):
    in_specs = (P(None, "fsdp", "tensor"), P(None, "fsdp", "tensor"), P(None, "tensor", None))
    out_specs = (P(None, "fsdp", "tensor"), P(None, "tensor", None), P(None, "fsdp", "tensor"))
    return jax.shard_map(
        on_device, mesh=mesh, in_specs=in_specs, out_specs=out_specs, check_vma=False
    )
```
